32 devices in a mesh: sp: 4 (over z), fsdp: 2 (over x), rep: 4 (over y, core).
Axes of the slice: x: 2, y: 2, z: 4, core: 2. Of those that a mesh axis runs over, the one named last changes fastest.
Arguments:
- hidden: bfloat16 [16, 256, 4096], P(('fsdp', 'rep'), 'sp'), may hold values from -6 to 6
- query_base: bfloat16 [16, 256, 4096], P(('fsdp', 'rep'), 'sp'), may hold values from -6 to 6
- key_span: bfloat16 [16, 256, 1024], P(('fsdp', 'rep'), 'sp'), may hold values from -6 to 6
- value_base: bfloat16 [16, 256, 1024], P(('fsdp', 'rep'), 'sp'), may hold values from -6 to 6
- past_keys: bfloat16 [16, 16, 1024], P(('fsdp', 'rep'), 'sp'), may hold values from -6 to 6
- past_values: bfloat16 [16, 16, 1024], P(('fsdp', 'rep'), 'sp'), may hold values from -6 to 6
- grad_out: bfloat16 [16, 256, 4096], P(('fsdp', 'rep'), 'sp'), may hold values from -6 to 6
- adapter_down: bfloat16 [4096, 128], P(('sp', 'fsdp')), may hold values from -0.09375 to 0.09375
- adapter_up: bfloat16 [64, 5120], P(None, ('sp', 'fsdp')), may hold values from -0.75 to 0.75
Outputs:
- attended: bfloat16 [16, 256, 4096], P(('fsdp', 'rep'), 'sp')
- grad_query: bfloat16 [16, 256, 4096], P(('fsdp', 'rep'), 'sp')
- grad_value: bfloat16 [16, 256, 1024], P(('fsdp', 'rep'), 'sp')
- grad_hidden: bfloat16 [16, 256, 4096], P(('fsdp', 'rep'), 'sp')
- grad_down: float32 [4096, 128], P(('sp', 'fsdp'))
- grad_up: float32 [64, 5120], P(None, ('sp', 'fsdp'))
The draws below stay inside these ranges and needn't reach their ends.
All inputs are finite; a program needn't handle non-finite values.
Results may differ from the reference program's by a relative error of at most 0.02.
Values may be sent and summed in bfloat16 or wider, within the bound.
No kernel may reach another device: no remote copies, remote signals or barrier semaphores. Data moves between devices by JAX's collectives and lax.ppermute only.
A program may use at most 128 MiB of HBM per device.

```python
import math
import jax
import jax.numpy as jnp
from jax import lax

D = 4096
HEADS = 32
KV_HEADS = 8
HEAD_DIM = 128
RANK = 64
KV = 1024
SPAN = 256
PAST = 16
SEQS = 16


def draw_query_base(key, part):
    key = jax.random.fold_in(key, 11)
    base_draw = jax.random.truncated_normal(key, -6.0, 6.0, (SEQS, SPAN, D), jnp.float32)
    return base_draw.astype(jnp.bfloat16)


def draw_past_keys(key, part):
    key = jax.random.fold_in(key, 12)
    base_draw = jax.random.truncated_normal(key, -6.0, 6.0, (SEQS, PAST, KV), jnp.float32)
    return base_draw.astype(jnp.bfloat16)


def spiked(array, stream_key, source, target, shards_of, factor):
    def block_of(axis_at):
        return (jnp.arange(array.shape[axis_at]) // (array.shape[axis_at] // shards_of)).reshape((-1,) + (1,) * (array.ndim - 1 - axis_at))

    first = jax.random.permutation(stream_key, shards_of)[block_of(target)]
    second = (block_of(target) + shards_of // 2) % shards_of
    return jnp.where((block_of(source) == first) | (block_of(source) == second), factor * array, array)


def shard_levels(stream_key, shape, cuts, least, high):
    factor_of = 1.0
    for axis_at, shards_of in cuts:
        heights = jax.random.uniform(jax.random.fold_in(jax.random.fold_in(stream_key, 6), axis_at), (shards_of,), jnp.float32, least / len(cuts), high / len(cuts))
        factor_of = factor_of * jnp.repeat(jnp.exp(heights), shape[axis_at] // shards_of).reshape((-1,) + (1,) * (len(shape) - 1 - axis_at))
    return factor_of


def centred(own_key, extent, deviation, reach, split=(), held_as=jnp.bfloat16):
    array = jax.random.normal(own_key, extent, jnp.float32) * deviation
    if len(split) > 0:
        array = shard_levels(own_key, extent, split, -0.22, 0.18) * array
    return jnp.clip(array, min=-reach, max=reach).astype(held_as)


def heavy_noise(own_key, extent, spread, limit, split, heavy, held_as=jnp.bfloat16):
    result = spread * jax.random.normal(own_key, extent, jnp.float32)
    if split:
        result = result * shard_levels(own_key, extent, split, -0.22, 0.18)
    return jnp.clip(spiked(result, jax.random.fold_in(own_key, 3), *heavy), -limit, limit).astype(held_as)


def setup_inputs(seed: int = 0) -> dict:
    arg_keys = jax.random.split(jax.random.key(seed), 10)
    hidden = heavy_noise(arg_keys[0], (SEQS, SPAN, D), 1.0, 6.0, ((0, 8), (1, 4)), (1, 2, 4, 2.0))
    query_base = draw_query_base(jax.random.fold_in(arg_keys[9], 71), 0)
    key_span = centred(arg_keys[2], (SEQS, SPAN, KV), 1.0, 6.0, ((0, 8), (1, 4)))
    value_base = centred(arg_keys[3], (SEQS, SPAN, KV), 1.0, 6.0, ((0, 8), (1, 4)))
    past_keys = draw_past_keys(jax.random.fold_in(arg_keys[9], 71), 0)
    past_values = centred(arg_keys[5], (SEQS, PAST, KV), 1.0, 6.0, ((0, 8), (1, 4)))
    grad_out = centred(arg_keys[6], (SEQS, SPAN, D), 1.0, 6.0, ((0, 8), (1, 4)))
    adapter_down = centred(arg_keys[7], (D, 2 * RANK), D ** -0.5, 0.09375, ((0, 8),))
    adapter_up = centred(arg_keys[8], (RANK, D + KV), RANK ** -0.5, 0.75, ((1, 8),))
    return {"hidden": hidden, "query_base": query_base, "key_span": key_span, "value_base": value_base, "past_keys": past_keys, "past_values": past_values, "grad_out": grad_out, "adapter_down": adapter_down, "adapter_up": adapter_up}


rope_base = 500000.0

def rotary_tables(row_count, offset, head_dim):
    half_dim = head_dim // 2
    position = (jnp.arange(row_count, dtype=jnp.int32) + offset).astype(jnp.float32)
    inverse = jnp.exp(jnp.arange(half_dim, dtype=jnp.float32) * (-2.0 * math.log(rope_base) / head_dim))
    angle_table = position[:, None] * inverse[None, :]
    return (jnp.cos(angle_table), jnp.sin(angle_table))

def rotate(source, cosine, sine_table, head_dim, backward):
    full_shape = source.shape
    half_dim = head_dim // 2
    split_pairs = source.reshape(full_shape[:-1] + (full_shape[-1] // head_dim, 2, half_dim))
    first_half = split_pairs[..., 0, :]
    second_half = split_pairs[..., 1, :]
    cos_wide = cosine[:, None, :]
    sin_wide = sine_table[:, None, :]
    if backward:
        new_first = first_half * cos_wide + second_half * sin_wide
        new_second = second_half * cos_wide - first_half * sin_wide
    else:
        new_first = first_half * cos_wide - second_half * sin_wide
        new_second = second_half * cos_wide + first_half * sin_wide
    return jnp.stack([new_first, new_second], axis=-2).reshape(full_shape)

def reference(hidden, query_base, key_span, value_base, past_keys, past_values, grad_out, adapter_down, adapter_up):
    group_size = HEADS // KV_HEADS
    key_len = PAST + SPAN
    score_scale = 1.0 / math.sqrt(HEAD_DIM)
    flat_rows = hidden.reshape(SEQS * SPAN, D)
    low_rank = jnp.dot(flat_rows, adapter_down, preferred_element_type=jnp.float32).astype(jnp.bfloat16)
    query_delta = jnp.dot(low_rank[:, :RANK], adapter_up[:, :D], preferred_element_type=jnp.float32)
    value_delta = jnp.dot(low_rank[:, RANK:], adapter_up[:, D:], preferred_element_type=jnp.float32)
    cosine, sine_table = rotary_tables(SPAN, PAST, HEAD_DIM)
    turned = rotate(query_delta.reshape(SEQS, SPAN, D), cosine, sine_table, HEAD_DIM, False)
    query_rows = (query_base.astype(jnp.float32) + turned).astype(jnp.bfloat16)
    value_rows = (value_base.astype(jnp.float32) + value_delta.reshape(SEQS, SPAN, KV)).astype(jnp.bfloat16)

    def by_heads(source, row_count, head_count):
        return source.reshape(SEQS, row_count, head_count, HEAD_DIM).transpose(0, 2, 1, 3)

    def widen_heads(source):
        return jnp.repeat(by_heads(source, key_len, KV_HEADS), group_size, axis=1).reshape(SEQS * HEADS, key_len, HEAD_DIM)
    key_rows = widen_heads(jnp.concatenate([past_keys, key_span], axis=1))
    all_values = widen_heads(jnp.concatenate([past_values, value_rows], axis=1))
    queries = by_heads(query_rows, SPAN, HEADS).reshape(SEQS * HEADS, SPAN, HEAD_DIM)
    grad_rows = by_heads(grad_out, SPAN, HEADS).reshape(SEQS * HEADS, SPAN, HEAD_DIM)
    visible = jnp.arange(key_len, dtype=jnp.int32)[None, :] <= PAST + jnp.arange(SPAN, dtype=jnp.int32)[:, None]

    def one_head(head_items):
        head_query, head_keys, head_values, head_grad = head_items
        scores = jnp.dot(head_query, head_keys.T, preferred_element_type=jnp.float32) * score_scale
        masked = jnp.where(visible, scores, -jnp.inf)
        row_max = lax.optimization_barrier(jnp.max(masked, axis=-1, keepdims=True))
        exp_scores = jnp.exp(masked - row_max)
        probability = exp_scores / lax.optimization_barrier(jnp.sum(exp_scores, axis=-1, keepdims=True))
        weights = probability.astype(jnp.bfloat16)
        out_block = jnp.dot(weights, head_values, preferred_element_type=jnp.float32).astype(jnp.bfloat16)
        prob_grad = jnp.dot(head_grad, head_values.T, preferred_element_type=jnp.float32)
        row_delta = lax.optimization_barrier(jnp.sum(head_grad.astype(jnp.float32) * out_block.astype(jnp.float32), axis=-1, keepdims=True))
        score_grad = (probability * (prob_grad - row_delta)).astype(jnp.bfloat16)
        query_grad = (jnp.dot(score_grad, head_keys, preferred_element_type=jnp.float32) * score_scale).astype(jnp.bfloat16)
        value_term = jnp.dot(weights[:, PAST:].T, head_grad, preferred_element_type=jnp.float32).astype(jnp.bfloat16)
        return (out_block, query_grad, value_term)
    head_outs, query_grads, value_terms = lax.map(one_head, (queries, key_rows, all_values, grad_rows))

    def to_tokens(source, head_count):
        return source.reshape(SEQS, head_count, SPAN, HEAD_DIM).transpose(0, 2, 1, 3).reshape(SEQS, SPAN, head_count * HEAD_DIM)

    def group_sum(source):
        summed = source.reshape(SEQS, KV_HEADS, group_size, SPAN, HEAD_DIM).astype(jnp.float32).sum(axis=2)
        return to_tokens(summed.astype(jnp.bfloat16), KV_HEADS)
    attended = to_tokens(head_outs, HEADS)
    grad_query = to_tokens(query_grads, HEADS)
    grad_value = group_sum(value_terms)
    query_back = rotate(grad_query.astype(jnp.float32), cosine, sine_table, HEAD_DIM, True).astype(jnp.bfloat16).reshape(SEQS * SPAN, D)
    value_back = grad_value.reshape(SEQS * SPAN, KV)
    low_grad = jnp.concatenate([jnp.dot(query_back, adapter_up[:, :D].T, preferred_element_type=jnp.float32), jnp.dot(value_back, adapter_up[:, D:].T, preferred_element_type=jnp.float32)], axis=1).astype(jnp.bfloat16)
    grad_hidden = jnp.dot(low_grad, adapter_down.T, preferred_element_type=jnp.float32).astype(jnp.bfloat16).reshape(SEQS, SPAN, D)
    grad_down = jnp.dot(flat_rows.T, low_grad, preferred_element_type=jnp.float32)
    grad_up = jnp.concatenate([jnp.dot(low_rank[:, :RANK].T, query_back, preferred_element_type=jnp.float32), jnp.dot(low_rank[:, RANK:].T, value_back, preferred_element_type=jnp.float32)], axis=1)
    return (attended, grad_query, grad_value, grad_hidden, grad_down, grad_up)
```

```python
import functools
import math

import jax
import jax.numpy as jnp
from jax import lax
from jax.experimental import pallas as pl
from jax.experimental.pallas import tpu as pltpu
from jax.sharding import PartitionSpec as P

D = 4096
HEADS = 32
KV_HEADS = 8
HEAD_DIM = 128
RANK = 64
KV = 1024
GROUP = HEADS // KV_HEADS
WIDE = GROUP * HEAD_DIM
ROPE_BASE = 500000.0
HIDDEN_MASK = -1e30
CHUNKS = 2

f32 = jnp.float32
bf16 = jnp.bfloat16


def rotary_tables(row_count, offset):
    half = HEAD_DIM // 2
    position = (jnp.arange(row_count, dtype=jnp.int32) + offset).astype(f32)
    inverse = jnp.exp(jnp.arange(half, dtype=f32) * (-2.0 * math.log(ROPE_BASE) / HEAD_DIM))
    angle = position[:, None] * inverse[None, :]
    cosine, sine = jnp.cos(angle), jnp.sin(angle)
    return (
        jnp.concatenate([cosine, cosine], axis=1),
        jnp.concatenate([-sine, sine], axis=1),
    )


def cyclic(x, axis, shift):
    n = lax.axis_size(axis)
    return lax.ppermute(x, axis, [(i, (i + shift) % n) for i in range(n)])


def along(x, axis, shift):
    n = lax.axis_size(axis)
    return lax.ppermute(x, axis, [(i, i + shift) for i in range(n) if 0 <= i + shift < n])


def partner(x, axis, mask):
    n = lax.axis_size(axis)
    return lax.ppermute(x, axis, [(i, i ^ mask) for i in range(n)])


def mm(a, b, ca, cb):
    return lax.dot_general(a, b, (((ca,), (cb,)), ((), ())), preferred_element_type=f32)


def attention_kernel(shards, place_ref, *refs, aliased):
    it = iter(refs)
    q_ref, g_ref, upq_ref, upv_ref, pk_ref, pv_ref, cos_ref, sin_ref = (next(it) for _ in range(8))
    low_refs = [next(it) for _ in range(shards)]
    k_refs = [next(it) for _ in range(shards)]
    v_refs = [next(it) for _ in range(shards)]
    if aliased:
        next(it), next(it)
    att_ref, gq_ref, gup_ref, lgq_ref, lgv_ref = (next(it) for _ in range(5))
    gv_refs = [next(it) for _ in range(shards)]

    seqs, tokens = q_ref.shape[0], q_ref.shape[1]
    span = shards * tokens
    past = pk_ref.shape[1]
    scale = 1.0 / math.sqrt(HEAD_DIM)
    place = place_ref[0]
    cos, sin = cos_ref[...], sin_ref[...]
    upq, upv = upq_ref[...], upv_ref[...]

    @pl.when(pl.program_id(0) == 0)
    def _():
        lgq_ref[...] = jnp.zeros_like(lgq_ref)
        lgv_ref[...] = jnp.zeros_like(lgv_ref)

    col = lax.broadcasted_iota(jnp.int32, (tokens, span + past), 1)
    row = lax.broadcasted_iota(jnp.int32, (tokens, span + past), 0)
    seen = (
        (col <= row)
        | ((col >= tokens) & (col < (place + 1) * tokens))
        | (col >= span)
    )
    bias = jnp.where(seen, 0.0, HIDDEN_MASK)
    bias = jnp.concatenate([bias] * GROUP, axis=0)

    def heads(x):
        return jnp.concatenate(
            [x[:, h * HEAD_DIM : (h + 1) * HEAD_DIM] for h in range(GROUP)], axis=0
        )

    def lanes(x):
        return jnp.concatenate([x[h * tokens : (h + 1) * tokens] for h in range(GROUP)], axis=1)

    cos4 = jnp.concatenate([cos] * GROUP, axis=0)
    sin4 = jnp.concatenate([sin] * GROUP, axis=0)
    grad_up_q = None
    for s in range(seqs):
        low = low_refs[0][s]
        low_q = low[:, :RANK]
        delta = heads(mm(low_q, upq, 1, 0))
        delta = delta * cos4 + pltpu.roll(delta, HEAD_DIM // 2, 1) * sin4
        q = (heads(q_ref[s]).astype(f32) + delta).astype(bf16)
        g = heads(g_ref[s])
        low_v = jnp.concatenate([r[s][:, RANK:] for r in low_refs], axis=0)
        keys = jnp.concatenate([r[s] for r in k_refs] + [pk_ref[s]], axis=0)
        base = jnp.concatenate([r[s] for r in v_refs], axis=0).astype(f32)
        vals = jnp.concatenate([(base + mm(low_v, upv, 1, 0)).astype(bf16), pv_ref[s]], axis=0)

        scores = mm(q, keys, 1, 1) * scale + bias
        top = jnp.max(scores, axis=-1, keepdims=True)
        e = jnp.exp(scores - top)
        probs = e / jnp.sum(e, axis=-1, keepdims=True)
        weights = probs.astype(bf16)
        out = mm(weights, vals, 1, 0).astype(bf16)
        att_ref[s] = lanes(out)
        prob_grad = mm(g, vals, 1, 1)
        row_delta = jnp.sum(g.astype(f32) * out.astype(f32), axis=-1, keepdims=True)
        score_grad = (probs * (prob_grad - row_delta)).astype(bf16)
        gq = (mm(score_grad, keys, 1, 0) * scale).astype(bf16)
        gq_ref[s] = lanes(gq)
        gq32 = gq.astype(f32)
        back = (gq32 * cos4 - pltpu.roll(gq32, HEAD_DIM // 2, 1) * sin4).astype(bf16)
        back = lanes(back)
        lgq_ref[s] += mm(back, upq, 1, 1)
        gv = mm(weights[:, :span], g, 0, 0).astype(bf16)
        for k in range(shards):
            gv_refs[k][s] = gv[k * tokens : (k + 1) * tokens]
        lgv_ref[s] += mm(gv, upv, 1, 1)
        up_q = mm(low_q, back, 0, 0)
        up_v = mm(low_v, gv, 0, 0)
        grad_up_q = up_q if s == 0 else grad_up_q + up_q
        grad_up_v = up_v if s == 0 else grad_up_v + up_v
    gup_ref[:, :WIDE] = grad_up_q.astype(bf16)
    gup_ref[:, WIDE:] = grad_up_v.astype(bf16)


def attention_chunk(
    chunk, groups, place, query_base, grad_out, up_full, past, cos, sin, lows, kvs, earlier
):
    shards = len(kvs)
    seqs, tokens = query_base.shape[:2]
    past_len = past.shape[1]
    first = chunk * groups
    q_heads = D // HEAD_DIM
    aliased = earlier is not None

    def at(block, fn):
        return pl.BlockSpec(block, fn)

    def whole(x):
        return pl.BlockSpec(x.shape, lambda g: (0,) * x.ndim)

    token_block = (seqs, tokens, WIDE)
    in_specs = [pl.BlockSpec(memory_space=pltpu.SMEM)]
    in_specs += [at(token_block, lambda g: (0, 0, first + g))] * 2
    in_specs += [at((RANK, WIDE), lambda g: (0, first + g))]
    in_specs += [at((RANK, HEAD_DIM), lambda g: (0, q_heads + first + g))]
    in_specs += [at((seqs, past_len, HEAD_DIM), lambda g: (0, 0, first + g))]
    in_specs += [at((seqs, past_len, HEAD_DIM), lambda g: (0, 0, KV_HEADS + first + g))]
    in_specs += [whole(cos), whole(sin)]
    in_specs += [whole(x) for x in lows]
    in_specs += [at((seqs, tokens, HEAD_DIM), lambda g: (0, 0, g))] * shards
    in_specs += [at((seqs, tokens, HEAD_DIM), lambda g: (0, 0, groups + g))] * shards
    operands = [place, query_base, grad_out, up_full, up_full, past, past, cos, sin]
    operands += list(lows) + list(kvs) + list(kvs)
    aliases = {}
    if aliased:
        aliases = {len(operands): 0, len(operands) + 1: 1}
        in_specs += [pl.BlockSpec(memory_space=pl.ANY)] * 2
        operands += list(earlier)
    shape = jax.ShapeDtypeStruct
    out_shape = [
        shape(query_base.shape, bf16),
        shape(query_base.shape, bf16),
        shape((RANK, groups * (WIDE + HEAD_DIM)), bf16),
        shape((seqs, tokens, RANK), f32),
        shape((seqs, shards * tokens, RANK), f32),
    ] + [shape((seqs, tokens, groups * HEAD_DIM), bf16)] * shards
    out_specs = [
        at(token_block, lambda g: (0, 0, first + g)),
        at(token_block, lambda g: (0, 0, first + g)),
        at((RANK, WIDE + HEAD_DIM), lambda g: (0, g)),
        at((seqs, tokens, RANK), lambda g: (0, 0, 0)),
        at((seqs, shards * tokens, RANK), lambda g: (0, 0, 0)),
    ] + [at((seqs, tokens, HEAD_DIM), lambda g: (0, 0, g))] * shards
    pairs = seqs * groups * GROUP * tokens * (shards * tokens + past_len)
    out = pl.pallas_call(
        functools.partial(attention_kernel, shards, aliased=aliased),
        grid=(groups,),
        in_specs=in_specs,
        out_specs=out_specs,
        out_shape=out_shape,
        input_output_aliases=aliases,
        compiler_params=pltpu.CompilerParams(vmem_limit_bytes=48 * 1024 * 1024),
        cost_estimate=pl.CostEstimate(
            flops=pairs * HEAD_DIM * 14, bytes_accessed=8 * 1024 * 1024, transcendentals=pairs
        ),
        name="attention",
    )(*operands)
    return out[:5], out[5:]


def gather_adapters(adapter_down, adapter_up):
    sp, fs, rp = (lax.axis_size(a) for a in ("sp", "fsdp", "rep"))
    z, x, r = (lax.axis_index(a) for a in ("sp", "fsdp", "rep"))
    split = 2 if rp % 2 == 0 else 1
    half = lax.rem(r, split)

    def gather(shard):
        rows = shard.shape[0] // split
        own = lax.dynamic_slice_in_dim(shard, half * rows, rows, 0)
        parts = [own] + [cyclic(own, "fsdp", k) for k in range(1, fs)]
        ordered = []
        for a in range(fs):
            pick = parts[0]
            for k in range(1, fs):
                pick = jnp.where(lax.rem(x - k + fs, fs) == a, parts[k], pick)
            ordered.append(pick)
        pair = jnp.stack(ordered)
        buf = jnp.zeros((sp,) + pair.shape, pair.dtype)
        for k in range(sp):
            piece = pair if k == 0 else cyclic(pair, "sp", k)
            buf = lax.dynamic_update_index_in_dim(buf, piece, lax.rem(z - k + sp, sp), 0)
        if split == 1:
            return buf.reshape((sp * fs, 1) + own.shape)
        other = partner(buf, "rep", 1)
        both = jnp.stack(
            [jnp.where(half == 0, buf, other), jnp.where(half == 0, other, buf)], axis=2
        )
        return both.reshape((sp * fs, split) + own.shape)

    down = gather(adapter_down).reshape(D, 2 * RANK)
    up = gather(adapter_up)
    up = up.reshape(sp * fs, RANK, -1).transpose(1, 0, 2).reshape(RANK, D + KV)
    return down, up


def halve_over_rep(x):
    rp = lax.axis_size("rep")
    r = lax.axis_index("rep")
    lead = x.shape[:-3]
    at = len(lead)
    bits = rp.bit_length() - 1
    for b in range(bits):
        x = x.reshape(lead + (rp >> (b + 1), 2) + x.shape[-2:])
        mine = lax.rem(lax.div(r, 1 << b), 2)
        send = lax.dynamic_index_in_dim(x, 1 - mine, at + 1, keepdims=False)
        keep = lax.dynamic_index_in_dim(x, mine, at + 1, keepdims=False)
        got = partner(send, "rep", 1 << b)
        x = (keep.astype(f32) + got.astype(f32)).astype(bf16)
    return x.reshape(lead + x.shape[-2:])


def scatter_over(x, axis):
    n = lax.axis_size(axis)
    i = lax.axis_index(axis)
    total = lax.dynamic_index_in_dim(x, i, 0, keepdims=False).astype(f32)
    for k in range(1, n):
        send = lax.dynamic_index_in_dim(x, lax.rem(i + k, n), 0, keepdims=False)
        total = total + cyclic(send, axis, k).astype(f32)
    return total


def gather_rep(own):
    rp = lax.axis_size("rep")
    r = lax.axis_index("rep")
    parts = [own] + [partner(own, "rep", m) for m in range(1, rp)]
    ordered = []
    for q in range(rp):
        pick = parts[0]
        for m in range(1, rp):
            pick = jnp.where((r ^ m) == q, parts[m], pick)
        ordered.append(pick)
    return jnp.concatenate(ordered, axis=0).astype(f32)


def body(
    hidden,
    query_base,
    key_span,
    value_base,
    past_keys,
    past_values,
    grad_out,
    adapter_down,
    adapter_up,
):
    sp, fs, rp = (lax.axis_size(a) for a in ("sp", "fsdp", "rep"))
    z = lax.axis_index("sp")
    seqs, tokens = hidden.shape[:2]
    past_len = past_keys.shape[1] * sp
    groups = KV_HEADS // CHUNKS
    width = groups * HEAD_DIM
    own_rows = hidden.reshape(seqs * tokens, D)

    down_full, up_full = gather_adapters(adapter_down, adapter_up)

    own_past = jnp.concatenate([past_keys, past_values], axis=2)
    past = jnp.concatenate([own_past] + [cyclic(own_past, "sp", k) for k in range(1, sp)], axis=1)

    chunk_kvs = []
    for c in range(CHUNKS):
        cols = slice(c * width, (c + 1) * width)
        own = jnp.concatenate([key_span[:, :, cols], value_base[:, :, cols]], axis=2)
        kvs = [own]
        for k in range(1, sp):
            kvs.append(along(own, "sp", k) if k <= 2 else along(kvs[k - 1], "sp", 1))
        chunk_kvs.append(kvs)

    low_rank = jnp.dot(own_rows, down_full, preferred_element_type=f32).astype(bf16)
    low_own = low_rank.reshape(seqs, tokens, 2 * RANK)
    lows = [low_own] + [along(low_own, "sp", k) for k in range(1, sp)]

    cos, sin = rotary_tables(tokens, past_len + z * tokens)
    place = z.astype(jnp.int32).reshape(1)

    earlier = None
    value_chunks, up_parts, low_grad_q, low_grad_v = [], [], 0.0, 0.0
    for c in range(CHUNKS):
        (att, gq, gup, lgq, lgv), gvs = attention_chunk(
            c, groups, place, query_base, grad_out, up_full, past, cos, sin,
            lows, chunk_kvs[c], earlier,
        )
        earlier = (att, gq)
        low_grad_q = low_grad_q + lgq
        low_grad_v = low_grad_v + lgv
        total = gvs[0].astype(f32)
        for k in range(1, sp):
            total = total + along(gvs[k], "sp", -k).astype(f32)
        value_chunks.append(total.astype(bf16))
        up_parts.append(halve_over_rep(gup.reshape(rp, RANK // rp, gup.shape[1])))
    attended, grad_query = earlier
    grad_value = jnp.concatenate(value_chunks, axis=2)

    low_v_total = low_grad_v[:, :tokens]
    for k in range(1, sp):
        part = low_grad_v[:, k * tokens : (k + 1) * tokens].astype(bf16)
        low_v_total = low_v_total + along(part, "sp", -k).astype(f32)
    low_grad = (
        jnp.concatenate([low_grad_q, low_v_total], axis=2)
        .astype(bf16)
        .reshape(seqs * tokens, 2 * RANK)
    )
    grad_hidden = jnp.dot(low_grad, down_full.T, preferred_element_type=f32).astype(bf16)

    down_part = jnp.dot(own_rows.T, low_grad, preferred_element_type=f32).astype(bf16)
    down_part = down_part.reshape(sp * fs, rp, D // (sp * fs * rp), 2 * RANK)
    down_part = halve_over_rep(down_part)
    up_rows = RANK // rp
    up_part = jnp.concatenate(up_parts, axis=1).reshape(up_rows, KV_HEADS, WIDE + HEAD_DIM)
    up_part = jnp.concatenate(
        [
            up_part[:, :, :WIDE].reshape(up_rows, D),
            up_part[:, :, WIDE:].reshape(up_rows, KV),
        ],
        axis=1,
    )
    up_part = up_part.reshape(up_rows, sp * fs, -1).transpose(1, 0, 2)

    def spread(x):
        x = x.reshape((sp, fs) + x.shape[1:]).swapaxes(0, 1)
        x = scatter_over(x, "fsdp").astype(bf16)
        return gather_rep(scatter_over(x, "sp").astype(bf16))

    grad_down = spread(down_part)
    grad_up = spread(up_part)
    return (
        attended,
        grad_query,
        grad_value,
        grad_hidden.reshape(seqs, tokens, D),
        grad_down,
        grad_up,
    )


def solution(mesh):
    rows = P(("fsdp", "rep"), "sp", None)
    down, up = P(("sp", "fsdp"), None), P(None, ("sp", "fsdp"))
    return jax.shard_map(
        body,
        mesh=mesh,
        in_specs=(rows,) * 7 + (down, up),
        out_specs=(rows,) * 4 + (down, up),
        check_vma=False,
    )
```

```python
import functools
import math

import jax
import jax.numpy as jnp
from jax import lax
from jax.experimental import pallas as pl
from jax.experimental.pallas import tpu as pltpu
from jax.sharding import PartitionSpec as P

D = 4096
HEADS = 32
KV_HEADS = 8
HEAD_DIM = 128
RANK = 64
KV = 1024
GROUP = HEADS // KV_HEADS
WIDE = GROUP * HEAD_DIM
ROPE_BASE = 500000.0
HIDDEN_MASK = -1e30
CHUNKS = 2

f32 = jnp.float32
bf16 = jnp.bfloat16


def rotary_tables(row_count, offset):
    half = HEAD_DIM // 2
    position = (jnp.arange(row_count, dtype=jnp.int32) + offset).astype(f32)
    inverse = jnp.exp(jnp.arange(half, dtype=f32) * (-2.0 * math.log(ROPE_BASE) / HEAD_DIM))
    angle = position[:, None] * inverse[None, :]
    cosine, sine = jnp.cos(angle), jnp.sin(angle)
    return (
        jnp.concatenate([cosine, cosine], axis=1),
        jnp.concatenate([-sine, sine], axis=1),
    )


def cyclic(x, axis, shift):
    n = lax.axis_size(axis)
    return lax.ppermute(x, axis, [(i, (i + shift) % n) for i in range(n)])


def along(x, axis, shift):
    n = lax.axis_size(axis)
    return lax.ppermute(x, axis, [(i, i + shift) for i in range(n) if 0 <= i + shift < n])


def partner(x, axis, mask):
    n = lax.axis_size(axis)
    return lax.ppermute(x, axis, [(i, i ^ mask) for i in range(n)])


def mm(a, b, ca, cb):
    return lax.dot_general(a, b, (((ca,), (cb,)), ((), ())), preferred_element_type=f32)


def attention_kernel(shards, earlier_count, place_ref, *refs):
    it = iter(refs)

    def take(n):
        return [next(it) for _ in range(n)]

    q_ref, g_ref, upq_ref, upv_ref, pk_ref, pv_ref, cos_ref, sin_ref = take(8)
    low_refs, k_refs, v_refs = take(shards), take(shards), take(shards)
    before = take(2) if earlier_count else None
    take(earlier_count)
    att_ref, gq_ref, guq_ref, guv_ref = take(4)
    gv_refs = take(shards)
    lgq_ref, lgv_ref = take(2)

    seqs, tokens = q_ref.shape[0], q_ref.shape[1]
    parts, part_rows = guq_ref.shape[1:3]
    span = shards * tokens
    past = pk_ref.shape[1]
    scale = 1.0 / math.sqrt(HEAD_DIM)
    place = place_ref[0]
    cos, sin = cos_ref[...], sin_ref[...]
    upq = jnp.concatenate([upq_ref[h] for h in range(GROUP)], axis=1)
    upv = upv_ref[0]

    @pl.when(pl.program_id(0) == 0)
    def _():
        if before is None:
            lgq_ref[...] = jnp.zeros_like(lgq_ref)
            lgv_ref[...] = jnp.zeros_like(lgv_ref)
        else:
            lgq_ref[...] = before[0][...]
            lgv_ref[...] = before[1][...]

    col = lax.broadcasted_iota(jnp.int32, (tokens, span + past), 1)
    row = lax.broadcasted_iota(jnp.int32, (tokens, span + past), 0)
    seen = (col <= row) | ((col >= tokens) & (col < (place + 1) * tokens)) | (col >= span)
    bias = jnp.where(seen, 0.0, HIDDEN_MASK)
    bias = jnp.concatenate([bias] * GROUP, axis=0)

    def heads(x):
        return jnp.concatenate(
            [x[:, h * HEAD_DIM : (h + 1) * HEAD_DIM] for h in range(GROUP)], axis=0
        )

    def lanes(x):
        return jnp.concatenate([x[h * tokens : (h + 1) * tokens] for h in range(GROUP)], axis=1)

    cos4 = jnp.concatenate([cos] * GROUP, axis=0)
    sin4 = jnp.concatenate([sin] * GROUP, axis=0)
    for s in range(seqs):
        low = low_refs[0][s]
        low_q = low[:, :RANK]
        delta = heads(mm(low_q, upq, 1, 0))
        delta = delta * cos4 + pltpu.roll(delta, HEAD_DIM // 2, 1) * sin4
        q = (heads(q_ref[s]).astype(f32) + delta).astype(bf16)
        g = heads(g_ref[s])
        low_v = jnp.concatenate([r[s][:, RANK:] for r in low_refs], axis=0)
        keys = jnp.concatenate([r[s] for r in k_refs] + [pk_ref[s]], axis=0)
        base = jnp.concatenate([r[s] for r in v_refs], axis=0).astype(f32)
        vals = jnp.concatenate([(base + mm(low_v, upv, 1, 0)).astype(bf16), pv_ref[s]], axis=0)

        scores = mm(q, keys, 1, 1) * scale + bias
        top = jnp.max(scores, axis=-1, keepdims=True)
        e = jnp.exp(scores - top)
        probs = e / jnp.sum(e, axis=-1, keepdims=True)
        weights = probs.astype(bf16)
        out = mm(weights, vals, 1, 0).astype(bf16)
        att_ref[s] = lanes(out)
        prob_grad = mm(g, vals, 1, 1)
        row_delta = jnp.sum(g.astype(f32) * out.astype(f32), axis=-1, keepdims=True)
        score_grad = (probs * (prob_grad - row_delta)).astype(bf16)
        gq = (mm(score_grad, keys, 1, 0) * scale).astype(bf16)
        gq_ref[s] = lanes(gq)
        gq32 = gq.astype(f32)
        back = (gq32 * cos4 - pltpu.roll(gq32, HEAD_DIM // 2, 1) * sin4).astype(bf16)
        back = lanes(back)
        lgq_ref[s] += mm(back, upq, 1, 1)
        gv = mm(weights[:, :span], g, 0, 0).astype(bf16)
        for k in range(shards):
            gv_refs[k][s] = gv[k * tokens : (k + 1) * tokens]
        lgv_ref[s] += mm(gv, upv, 1, 1)
        up_q = mm(low_q, back, 0, 0)
        up_v = mm(low_v, gv, 0, 0)
        grad_up_q = up_q if s == 0 else grad_up_q + up_q
        grad_up_v = up_v if s == 0 else grad_up_v + up_v
    grad_up_q, grad_up_v = grad_up_q.astype(bf16), grad_up_v.astype(bf16)
    for p in range(parts):
        rows = slice(p * part_rows, (p + 1) * part_rows)
        for h in range(GROUP):
            guq_ref[h, p] = grad_up_q[rows, h * HEAD_DIM : (h + 1) * HEAD_DIM]
        guv_ref[0, p] = grad_up_v[rows]


def attention_chunk(
    chunk, groups, place, query_base, grad_out, up_blocks, past, cos, sin, lows, kvs, earlier
):
    shards = len(kvs)
    parts = lax.axis_size("rep")
    seqs, tokens = query_base.shape[:2]
    past_len = past.shape[1]
    first = chunk * groups

    def whole(x):
        return pl.BlockSpec(x.shape, lambda g: (0,) * len(x.shape))

    spec = pl.BlockSpec
    q_spec = spec((seqs, tokens, WIDE), lambda g: (0, 0, first + g))
    gv_spec = spec((seqs, tokens, HEAD_DIM), lambda g: (0, 0, first + g))
    past_block = (seqs, past_len, HEAD_DIM)
    in_specs = [
        spec(memory_space=pltpu.SMEM),
        q_spec,
        q_spec,
        spec((GROUP, RANK, HEAD_DIM), lambda g: (first + g, 0, 0)),
        spec((1, RANK, HEAD_DIM), lambda g: (HEADS + first + g, 0, 0)),
        spec(past_block, lambda g: (0, 0, first + g)),
        spec(past_block, lambda g: (0, 0, KV_HEADS + first + g)),
        whole(cos),
        whole(sin),
    ]
    in_specs += [whole(x) for x in lows]
    in_specs += [spec((seqs, tokens, HEAD_DIM), lambda g: (0, 0, g))] * shards
    in_specs += [spec((seqs, tokens, HEAD_DIM), lambda g: (0, 0, groups + g))] * shards
    operands = [place, query_base, grad_out, up_blocks, up_blocks, past, past, cos, sin]
    operands += list(lows) + list(kvs) + list(kvs)
    shape = jax.ShapeDtypeStruct
    low_q_shape = shape((seqs, tokens, RANK), f32)
    low_v_shape = shape((seqs, shards * tokens, RANK), f32)
    placed_shapes = [
        shape(query_base.shape, bf16),
        shape(query_base.shape, bf16),
        shape((HEADS, parts, RANK // parts, HEAD_DIM), bf16),
        shape((KV_HEADS, parts, RANK // parts, HEAD_DIM), bf16),
    ] + [shape((seqs, tokens, KV), bf16)] * shards
    placed_specs = [
        q_spec,
        q_spec,
        spec((GROUP, parts, RANK // parts, HEAD_DIM), lambda g: (first + g, 0, 0, 0)),
        spec((1, parts, RANK // parts, HEAD_DIM), lambda g: (first + g, 0, 0, 0)),
    ] + [gv_spec] * shards
    aliases = {}
    placed = len(placed_shapes)
    if earlier is not None:
        in_specs += [whole(low_q_shape), whole(low_v_shape)]
        operands += list(earlier[placed:])
        aliases = {len(operands) + i: i for i in range(placed)}
        in_specs += [spec(memory_space=pl.ANY)] * placed
        operands += list(earlier[:placed])
    pairs = seqs * groups * GROUP * tokens * (shards * tokens + past_len)
    return pl.pallas_call(
        functools.partial(attention_kernel, shards, placed if earlier is not None else 0),
        grid=(groups,),
        in_specs=in_specs,
        out_specs=placed_specs + [whole(low_q_shape), whole(low_v_shape)],
        out_shape=placed_shapes + [low_q_shape, low_v_shape],
        input_output_aliases=aliases,
        compiler_params=pltpu.CompilerParams(vmem_limit_bytes=48 * 1024 * 1024),
        cost_estimate=pl.CostEstimate(
            flops=pairs * HEAD_DIM * 28, bytes_accessed=16 * 1024 * 1024, transcendentals=pairs
        ),
        name="attention",
    )(*operands)


def low_rank_kernel(fs, index_ref, own_ref, other_ref, hidden_ref, down_ref, up_ref, low_ref):
    z, x, c = index_ref[0], index_ref[1], index_ref[2]
    pieces = own_ref.shape[0]
    sp = pieces // fs
    down_rows = D // (2 * pieces)
    blocks = up_ref.shape[0] // pieces
    up_rows = RANK // 2
    for r in range(pieces):
        shard = (z ^ (r % sp)) * fs + (x ^ (r // sp))
        for ref, half in ((own_ref, c), (other_ref, 1 - c)):
            at = pl.multiple_of((shard * 2 + half) * down_rows, down_rows)
            down_ref[pl.ds(at, down_rows), :] = ref[r, :down_rows]
            at = pl.multiple_of(half * up_rows, up_rows)
            for j in range(blocks):
                lo = down_rows + j * up_rows
                up_ref[shard * blocks + j, pl.ds(at, up_rows), :] = ref[r, lo : lo + up_rows]
    rows = jnp.concatenate([hidden_ref[s] for s in range(hidden_ref.shape[0])], axis=0)
    low = mm(rows, down_ref[...], 1, 0).astype(bf16)
    for s in range(low_ref.shape[0]):
        low_ref[s] = low[s * low_ref.shape[1] : (s + 1) * low_ref.shape[1]]


def adapters_packed(hidden, adapter_down, adapter_up, own_past):
    sp, fs = lax.axis_size("sp"), lax.axis_size("fsdp")
    z, x, r = (lax.axis_index(a) for a in ("sp", "fsdp", "rep"))
    c = lax.rem(r, 2)
    down_rows, up_rows = adapter_down.shape[0] // 2, RANK // 2
    blocks = adapter_up.shape[1] // HEAD_DIM
    down = lax.dynamic_slice_in_dim(adapter_down, c * down_rows, down_rows, 0)
    up = lax.dynamic_slice_in_dim(adapter_up, c * up_rows, up_rows, 0)
    up = [up[:, j * HEAD_DIM : (j + 1) * HEAD_DIM] for j in range(blocks)]
    rows = down_rows + blocks * up_rows
    buf = jnp.concatenate([down] + up + [own_past.reshape(-1, 2 * RANK)], axis=0)[None]
    step = 1
    while step < sp:
        buf = jnp.concatenate([buf, partner(buf, "sp", step)], axis=0)
        step *= 2
    seqs, each = own_past.shape[:2]
    past = buf[:, rows:].reshape(sp, seqs, each, -1).swapaxes(0, 1).reshape(seqs, sp * each, -1)
    buf = buf[:, :rows]
    step = 1
    while step < fs:
        buf = jnp.concatenate([buf, partner(buf, "fsdp", step)], axis=0)
        step *= 2
    other = partner(buf, "rep", 1)
    index = jnp.stack([z, x, c]).astype(jnp.int32)
    vmem = pl.BlockSpec(memory_space=pltpu.VMEM)
    seqs, tokens = hidden.shape[:2]
    down_full, up_blocks, low = pl.pallas_call(
        functools.partial(low_rank_kernel, fs),
        in_specs=[pl.BlockSpec(memory_space=pltpu.SMEM)] + [vmem] * 3,
        out_specs=[vmem] * 3,
        out_shape=[
            jax.ShapeDtypeStruct((D, 2 * RANK), bf16),
            jax.ShapeDtypeStruct((HEADS + KV_HEADS, RANK, HEAD_DIM), bf16),
            jax.ShapeDtypeStruct((seqs, tokens, 2 * RANK), bf16),
        ],
        compiler_params=pltpu.CompilerParams(vmem_limit_bytes=32 * 1024 * 1024),
        cost_estimate=pl.CostEstimate(
            flops=2 * seqs * tokens * D * 2 * RANK, bytes_accessed=5 * 2**20, transcendentals=0
        ),
        name="low_rank",
    )(index, buf, other, hidden)
    return down_full, up_blocks, low, past


def adapters_plain(hidden, adapter_down, adapter_up, own_past):
    sp = lax.axis_size("sp")
    seqs, tokens = hidden.shape[:2]
    past = jnp.concatenate([own_past] + [cyclic(own_past, "sp", k) for k in range(1, sp)], axis=1)
    down_full = lax.all_gather(adapter_down, ("sp", "fsdp"), axis=0, tiled=True)
    up_full = lax.all_gather(adapter_up, ("sp", "fsdp"), axis=1, tiled=True)
    rows = hidden.reshape(seqs * tokens, D)
    low = jnp.dot(rows, down_full, preferred_element_type=f32).astype(bf16)
    up_blocks = up_full.reshape(RANK, HEADS + KV_HEADS, HEAD_DIM).swapaxes(0, 1)
    return down_full, up_blocks, low.reshape(seqs, tokens, 2 * RANK), past


def grad_hidden_kernel(low_ref, down_ref, out_ref):
    out = mm(low_ref[...], down_ref[...], 1, 1).astype(bf16)
    tokens = out_ref.shape[1]
    for s in range(out_ref.shape[0]):
        out_ref[s] = out[s * tokens : (s + 1) * tokens]


def grad_hidden_of(low_grad, down_full, seqs, tokens):
    columns = 1024
    return pl.pallas_call(
        grad_hidden_kernel,
        grid=(D // columns,),
        in_specs=[
            pl.BlockSpec(low_grad.shape, lambda i: (0, 0)),
            pl.BlockSpec((columns, 2 * RANK), lambda i: (i, 0)),
        ],
        out_specs=pl.BlockSpec((seqs, tokens, columns), lambda i: (0, 0, i)),
        out_shape=jax.ShapeDtypeStruct((seqs, tokens, D), bf16),
        compiler_params=pltpu.CompilerParams(vmem_limit_bytes=32 * 1024 * 1024),
        cost_estimate=pl.CostEstimate(
            flops=2 * seqs * tokens * D * 2 * RANK, bytes_accessed=2**21, transcendentals=0
        ),
        name="grad_hidden",
    )(low_grad, down_full)


def adapter_grads_kernel(core_ref, hidden_ref, low_ref, guq_ref, guv_ref, send_ref, keep_ref, gd_ref):
    c = core_ref[0]
    shards, pairs = send_ref.shape[:2]
    down_rows = gd_ref.shape[1]
    columns = 2 * pairs * down_rows
    blocks = (HEADS + KV_HEADS) // shards
    up_rows = guq_ref.shape[2]
    low = low_ref[...]
    for b in range(shards):
        cols = [hidden_ref[s, :, b * columns : (b + 1) * columns] for s in range(hidden_ref.shape[0])]
        part = mm(jnp.concatenate(cols, axis=0), low, 0, 0).astype(bf16)
        for q in range(2 * pairs):
            gd_ref[q] = part[q * down_rows : (q + 1) * down_rows]
        for hi in range(pairs):
            for ref, q in ((send_ref, 2 * hi + 1 - c), (keep_ref, 2 * hi + c)):
                ref[b, hi, :down_rows] = gd_ref[q]
                for j in range(blocks):
                    block = b * blocks + j
                    src = guq_ref[block, q] if block < HEADS else guv_ref[block - HEADS, q]
                    lo = down_rows + j * up_rows
                    ref[b, hi, lo : lo + up_rows] = src


def packed_grads(hidden, low_grad, guq, guv, shards):
    rp, r = lax.axis_size("rep"), lax.axis_index("rep")
    c = lax.rem(r, 2)
    down_rows, up_rows = D // (shards * rp), RANK // rp
    up_width = (D + KV) // shards
    rows = down_rows + up_rows * up_width // (2 * RANK)
    if up_width % HEAD_DIM == 0:
        vmem = pl.BlockSpec(memory_space=pltpu.VMEM)
        packed = jax.ShapeDtypeStruct((shards, rp // 2, rows, 2 * RANK), bf16)
        return pl.pallas_call(
            adapter_grads_kernel,
            in_specs=[pl.BlockSpec(memory_space=pltpu.SMEM)] + [vmem] * 4,
            out_specs=[vmem] * 2,
            out_shape=[packed] * 2,
            scratch_shapes=[pltpu.VMEM((rp, down_rows, 2 * RANK), bf16)],
            compiler_params=pltpu.CompilerParams(vmem_limit_bytes=32 * 1024 * 1024),
            cost_estimate=pl.CostEstimate(
                flops=2 * hidden.size * 2 * RANK, bytes_accessed=5 * 2**20, transcendentals=0
            ),
            name="adapter_grads",
        )(c.astype(jnp.int32).reshape(1), hidden, low_grad, guq, guv)
    own_rows = hidden.reshape(-1, D)
    down = jnp.dot(own_rows.T, low_grad, preferred_element_type=f32).astype(bf16)
    down = down.reshape(shards, rp, down_rows, 2 * RANK)
    up = jnp.concatenate([guq, guv], axis=0).transpose(1, 2, 0, 3)
    up = up.reshape(rp, up_rows, shards, up_width).transpose(2, 0, 1, 3)
    up = up.reshape(shards, rp, -1, 2 * RANK)
    both = jnp.concatenate([down, up], axis=2).reshape(shards, rp // 2, 2, rows, 2 * RANK)
    send = lax.dynamic_index_in_dim(both, 1 - c, 2, keepdims=False)
    keep = lax.dynamic_index_in_dim(both, c, 2, keepdims=False)
    return send, keep


def finish_grads(send, keep):
    sp, fs, rp = (lax.axis_size(a) for a in ("sp", "fsdp", "rep"))
    z, x, r = (lax.axis_index(a) for a in ("sp", "fsdp", "rep"))
    shards, _, rows, lanes = send.shape
    got = partner(send, "rep", 1)
    for b in range(1, rp.bit_length() - 1):
        shape = (shards, rp >> (b + 1), 2, rows, lanes)
        mine = lax.rem(lax.div(r, 1 << b), 2)

        def half(i):
            return sum(
                lax.dynamic_index_in_dim(a.reshape(shape), i, 2, keepdims=False).astype(f32)
                for a in (keep, got)
            ).astype(bf16)

        send, keep = half(1 - mine), half(mine)
        got = partner(send, "rep", 1 << b)
    shape = (sp, fs, rows, lanes)

    def over_fsdp(i):
        return sum(
            lax.dynamic_index_in_dim(a.reshape(shape), i, 1, keepdims=False).astype(f32)
            for a in (keep, got)
        ).astype(bf16)

    total = over_fsdp(x).astype(f32)
    for k in range(1, fs):
        total = total + cyclic(over_fsdp(lax.rem(x + k, fs)), "fsdp", k).astype(f32)
    over_sp = total.astype(bf16)
    total = lax.dynamic_index_in_dim(over_sp, z, 0, keepdims=False).astype(f32)
    for k in range(1, sp):
        send = lax.dynamic_index_in_dim(over_sp, lax.rem(z + k, sp), 0, keepdims=False)
        total = total + cyclic(send, "sp", k).astype(f32)
    own = total.astype(bf16)
    parts = [own] + [partner(own, "rep", m) for m in range(1, rp)]
    ordered = []
    for q in range(rp):
        pick = parts[0]
        for m in range(1, rp):
            pick = jnp.where((r ^ m) == q, parts[m], pick)
        ordered.append(pick.astype(f32))
    down_rows, up_rows = D // (shards * rp), RANK // rp
    up_width = (D + KV) // shards
    grad_down = jnp.concatenate([p[:down_rows] for p in ordered], axis=0)
    ups = []
    for p in ordered:
        up = p[down_rows:]
        if up_width % HEAD_DIM == 0:
            up = [up[lo : lo + up_rows] for lo in range(0, up.shape[0], up_rows)]
            up = jnp.concatenate(up, axis=1)
        ups.append(up.reshape(up_rows, up_width))
    return grad_down, jnp.concatenate(ups, axis=0)


def body(
    hidden,
    query_base,
    key_span,
    value_base,
    past_keys,
    past_values,
    grad_out,
    adapter_down,
    adapter_up,
):
    sp, fs = lax.axis_size("sp"), lax.axis_size("fsdp")
    z = lax.axis_index("sp")
    seqs, tokens = hidden.shape[:2]
    past_len = past_keys.shape[1] * sp
    groups = KV_HEADS // CHUNKS
    width = groups * HEAD_DIM

    own_past = jnp.concatenate([past_keys, past_values], axis=2)
    even = adapter_up.shape[1] % HEAD_DIM == 0
    adapters = adapters_packed if even else adapters_plain
    down_full, up_blocks, low_own, past = adapters(hidden, adapter_down, adapter_up, own_past)

    chunk_kvs = []
    for c in range(CHUNKS):
        cols = slice(c * width, (c + 1) * width)
        kvs = [jnp.concatenate([key_span[:, :, cols], value_base[:, :, cols]], axis=2)]
        for k in range(1, sp):
            kvs.append(along(kvs[k - 1], "sp", 1))
        chunk_kvs.append(kvs)

    lows = [low_own] + [along(low_own, "sp", k) for k in range(1, sp)]
    cos, sin = rotary_tables(tokens, past_len + z * tokens)
    place = z.astype(jnp.int32).reshape(1)

    made = None
    for c in range(CHUNKS):
        made = attention_chunk(
            c, groups, place, query_base, grad_out, up_blocks, past, cos, sin,
            lows, chunk_kvs[c], made,
        )
    attended, grad_query, guq, guv = made[:4]
    gvs = made[4 : 4 + sp]
    low_grad_q, low_grad_v = made[4 + sp :]

    low_v_total = low_grad_v[:, :tokens]
    for k in range(1, sp):
        part = low_grad_v[:, k * tokens : (k + 1) * tokens].astype(bf16)
        low_v_total = low_v_total + along(part, "sp", -k).astype(f32)
    low_grad = (
        jnp.concatenate([low_grad_q, low_v_total], axis=2)
        .astype(bf16)
        .reshape(seqs * tokens, 2 * RANK)
    )
    send, keep = packed_grads(hidden, low_grad, guq, guv, sp * fs)
    grad_down, grad_up = finish_grads(send, keep)
    grad_hidden = grad_hidden_of(low_grad, down_full, seqs, tokens)

    grad_value = gvs[0].astype(f32)
    for k in range(1, sp):
        grad_value = grad_value + along(gvs[k], "sp", -k).astype(f32)
    return (
        attended,
        grad_query,
        grad_value.astype(bf16),
        grad_hidden,
        grad_down,
        grad_up,
    )


def solution(mesh):
    rows = P(("fsdp", "rep"), "sp", None)
    down, up = P(("sp", "fsdp"), None), P(None, ("sp", "fsdp"))
    return jax.shard_map(
        body,
        mesh=mesh,
        in_specs=(rows,) * 7 + (down, up),
        out_specs=(rows,) * 4 + (down, up),
        check_vma=False,
    )
```

```python
import functools
import math

import jax
import jax.numpy as jnp
from jax import lax
from jax.experimental import pallas as pl
from jax.experimental.pallas import tpu as pltpu
from jax.sharding import PartitionSpec as P

D = 4096
HEADS = 32
KV_HEADS = 8
HEAD_DIM = 128
RANK = 64
KV = 1024
GROUP = HEADS // KV_HEADS
WIDE = GROUP * HEAD_DIM
ROPE_BASE = 500000.0
HIDDEN_MASK = -1e30
CHUNKS = ((0, 5), (5, 8))
LOG2_E = 1.4426950408889634

f32 = jnp.float32
bf16 = jnp.bfloat16


def rotary_tables(row_count, offset):
    half = HEAD_DIM // 2
    position = (jnp.arange(row_count, dtype=jnp.int32) + offset).astype(f32)
    inverse = jnp.exp(jnp.arange(half, dtype=f32) * (-2.0 * math.log(ROPE_BASE) / HEAD_DIM))
    angle = position[:, None] * inverse[None, :]
    cosine, sine = jnp.cos(angle), jnp.sin(angle)
    return (
        jnp.concatenate([cosine, cosine], axis=1),
        jnp.concatenate([-sine, sine], axis=1),
    )


def cyclic(x, axis, shift):
    n = lax.axis_size(axis)
    return lax.ppermute(x, axis, [(i, (i + shift) % n) for i in range(n)])


def along(x, axis, shift):
    n = lax.axis_size(axis)
    return lax.ppermute(x, axis, [(i, i + shift) for i in range(n) if 0 <= i + shift < n])


def partner(x, axis, mask):
    n = lax.axis_size(axis)
    return lax.ppermute(x, axis, [(i, i ^ mask) for i in range(n)])


def tie(x, *others):
    return lax.optimization_barrier((x,) + others)[0]


def mm(a, b, ca, cb):
    return lax.dot_general(a, b, (((ca,), (cb,)), ((), ())), preferred_element_type=f32)


def attention_kernel(shards, earlier_count, place_ref, *refs):
    it = iter(refs)

    def take(n):
        return [next(it) for _ in range(n)]

    q_ref, g_ref, upq_ref, upv_ref, pk_ref, pv_ref, cos_ref, sin_ref = take(8)
    low_refs, k_refs, v_refs = take(shards), take(shards), take(shards)
    before = take(2) if earlier_count else None
    take(earlier_count)
    att_ref, gq_ref, guq_ref, guv_ref = take(4)
    gv_refs = take(shards)
    lgq_ref, lgv_ref = take(2)

    seqs, tokens = q_ref.shape[0], q_ref.shape[1]
    parts, part_rows = guq_ref.shape[1:3]
    span = shards * tokens
    past = pk_ref.shape[1]
    scale = 1.0 / math.sqrt(HEAD_DIM)
    place = place_ref[0]
    cos, sin = cos_ref[...], sin_ref[...]
    upq = jnp.concatenate([upq_ref[h] for h in range(GROUP)], axis=1)
    upv = upv_ref[0]

    @pl.when(pl.program_id(0) == 0)
    def _():
        if before is None:
            lgq_ref[...] = jnp.zeros_like(lgq_ref)
            lgv_ref[...] = jnp.zeros_like(lgv_ref)
        else:
            lgq_ref[...] = before[0][...]
            lgv_ref[...] = before[1][...]

    col = lax.broadcasted_iota(jnp.int32, (tokens, span + past), 1)
    row = lax.broadcasted_iota(jnp.int32, (tokens, span + past), 0)
    seen = (col <= row) | ((col >= tokens) & (col < (place + 1) * tokens)) | (col >= span)
    bias = jnp.where(seen, 0.0, HIDDEN_MASK)
    bias = jnp.concatenate([bias] * GROUP, axis=0)

    def heads(x):
        return jnp.concatenate(
            [x[:, h * HEAD_DIM : (h + 1) * HEAD_DIM] for h in range(GROUP)], axis=0
        )

    def lanes(x):
        return jnp.concatenate([x[h * tokens : (h + 1) * tokens] for h in range(GROUP)], axis=1)

    cos4 = jnp.concatenate([cos] * GROUP, axis=0)
    sin4 = jnp.concatenate([sin] * GROUP, axis=0)
    for s in range(seqs):
        low = low_refs[0][s]
        low_q = low[:, :RANK]
        delta = heads(mm(low_q, upq, 1, 0))
        delta = delta * cos4 + pltpu.roll(delta, HEAD_DIM // 2, 1) * sin4
        q = (heads(q_ref[s]).astype(f32) + delta).astype(bf16)
        g = heads(g_ref[s])
        low_v = jnp.concatenate([r[s][:, RANK:] for r in low_refs], axis=0)
        keys = jnp.concatenate([r[s] for r in k_refs] + [pk_ref[s]], axis=0)
        base = jnp.concatenate([r[s] for r in v_refs], axis=0).astype(f32)
        vals = jnp.concatenate([(base + mm(low_v, upv, 1, 0)).astype(bf16), pv_ref[s]], axis=0)

        scores = mm(q, keys, 1, 1) * (scale * LOG2_E) + bias
        top = jnp.max(scores, axis=-1, keepdims=True)
        e = jnp.exp2(scores - top)
        inverse = 1.0 / jnp.sum(e, axis=-1, keepdims=True)
        weights = e.astype(bf16)
        out = (mm(weights, vals, 1, 0) * inverse).astype(bf16)
        att_ref[s] = lanes(out)
        g = (g.astype(f32) * inverse).astype(bf16)
        prob_grad = mm(g, vals, 1, 1)
        row_delta = jnp.sum(g.astype(f32) * out.astype(f32), axis=-1, keepdims=True)
        score_grad = (e * (prob_grad - row_delta)).astype(bf16)
        gq = (mm(score_grad, keys, 1, 0) * scale).astype(bf16)
        gq_ref[s] = lanes(gq)
        gq32 = gq.astype(f32)
        back = (gq32 * cos4 - pltpu.roll(gq32, HEAD_DIM // 2, 1) * sin4).astype(bf16)
        back = lanes(back)
        lgq_ref[s] += mm(back, upq, 1, 1)
        gv = mm(weights[:, :span], g, 0, 0).astype(bf16)
        for k in range(shards):
            gv_refs[k][s] = gv[k * tokens : (k + 1) * tokens]
        lgv_ref[s] += mm(gv, upv, 1, 1)
        up_q = mm(low_q, back, 0, 0)
        up_v = mm(low_v, gv, 0, 0)
        grad_up_q = up_q if s == 0 else grad_up_q + up_q
        grad_up_v = up_v if s == 0 else grad_up_v + up_v
    grad_up_q, grad_up_v = grad_up_q.astype(bf16), grad_up_v.astype(bf16)
    for p in range(parts):
        rows = slice(p * part_rows, (p + 1) * part_rows)
        for h in range(GROUP):
            guq_ref[h, p] = grad_up_q[rows, h * HEAD_DIM : (h + 1) * HEAD_DIM]
        guv_ref[0, p] = grad_up_v[rows]


def attention_chunk(
    first, last, place, query_base, grad_out, up_blocks, past, cos, sin, lows, kvs, earlier
):
    shards = len(kvs)
    parts = lax.axis_size("rep")
    seqs, tokens = query_base.shape[:2]
    past_len = past.shape[1]
    groups = last - first

    def whole(x):
        return pl.BlockSpec(x.shape, lambda g: (0,) * len(x.shape))

    spec = pl.BlockSpec
    q_spec = spec((seqs, tokens, WIDE), lambda g: (0, 0, first + g))
    gv_spec = spec((seqs, tokens, HEAD_DIM), lambda g: (0, 0, first + g))
    past_block = (seqs, past_len, HEAD_DIM)
    in_specs = [
        spec(memory_space=pltpu.SMEM),
        q_spec,
        q_spec,
        spec((GROUP, RANK, HEAD_DIM), lambda g: (first + g, 0, 0)),
        spec((1, RANK, HEAD_DIM), lambda g: (HEADS + first + g, 0, 0)),
        spec(past_block, lambda g: (0, 0, first + g)),
        spec(past_block, lambda g: (0, 0, KV_HEADS + first + g)),
        whole(cos),
        whole(sin),
    ]
    in_specs += [whole(x) for x in lows]
    in_specs += [spec((seqs, tokens, HEAD_DIM), lambda g: (0, 0, g))] * shards
    in_specs += [spec((seqs, tokens, HEAD_DIM), lambda g: (0, 0, groups + g))] * shards
    operands = [place, query_base, grad_out, up_blocks, up_blocks, past, past, cos, sin]
    operands += list(lows) + list(kvs) + list(kvs)
    shape = jax.ShapeDtypeStruct
    low_q_shape = shape((seqs, tokens, RANK), f32)
    low_v_shape = shape((seqs, shards * tokens, RANK), f32)
    placed_shapes = [
        shape(query_base.shape, bf16),
        shape(query_base.shape, bf16),
        shape((HEADS, parts, RANK // parts, HEAD_DIM), bf16),
        shape((KV_HEADS, parts, RANK // parts, HEAD_DIM), bf16),
    ] + [shape((seqs, tokens, KV), bf16)] * shards
    placed_specs = [
        q_spec,
        q_spec,
        spec((GROUP, parts, RANK // parts, HEAD_DIM), lambda g: (first + g, 0, 0, 0)),
        spec((1, parts, RANK // parts, HEAD_DIM), lambda g: (first + g, 0, 0, 0)),
    ] + [gv_spec] * shards
    aliases = {}
    placed = len(placed_shapes)
    if earlier is not None:
        in_specs += [whole(low_q_shape), whole(low_v_shape)]
        operands += list(earlier[placed:])
        aliases = {len(operands) + i: i for i in range(placed)}
        in_specs += [spec(memory_space=pl.ANY)] * placed
        operands += list(earlier[:placed])
    pairs = seqs * groups * GROUP * tokens * (shards * tokens + past_len)
    return pl.pallas_call(
        functools.partial(attention_kernel, shards, placed if earlier is not None else 0),
        grid=(groups,),
        in_specs=in_specs,
        out_specs=placed_specs + [whole(low_q_shape), whole(low_v_shape)],
        out_shape=placed_shapes + [low_q_shape, low_v_shape],
        input_output_aliases=aliases,
        compiler_params=pltpu.CompilerParams(vmem_limit_bytes=48 * 1024 * 1024),
        cost_estimate=pl.CostEstimate(
            flops=pairs * HEAD_DIM * 28, bytes_accessed=16 * 1024 * 1024, transcendentals=pairs
        ),
        name="attention",
    )(*operands)


def low_rank_kernel(fs, index_ref, own_ref, other_ref, hidden_ref, down_ref, up_ref, low_ref):
    z, x, c = index_ref[0], index_ref[1], index_ref[2]
    pieces = own_ref.shape[0]
    sp = pieces // fs
    down_rows = D // (2 * pieces)
    blocks = up_ref.shape[0] // pieces
    up_rows = RANK // 2
    for r in range(pieces):
        shard = (z ^ (r % sp)) * fs + (x ^ (r // sp))
        for ref, half in ((own_ref, c), (other_ref, 1 - c)):
            at = pl.multiple_of((shard * 2 + half) * down_rows, down_rows)
            down_ref[pl.ds(at, down_rows), :] = ref[r, :down_rows]
            at = pl.multiple_of(half * up_rows, up_rows)
            for j in range(blocks):
                lo = down_rows + j * up_rows
                up_ref[shard * blocks + j, pl.ds(at, up_rows), :] = ref[r, lo : lo + up_rows]
    rows = jnp.concatenate([hidden_ref[s] for s in range(hidden_ref.shape[0])], axis=0)
    low = mm(rows, down_ref[...], 1, 0).astype(bf16)
    for s in range(low_ref.shape[0]):
        low_ref[s] = low[s * low_ref.shape[1] : (s + 1) * low_ref.shape[1]]


def adapters_packed(hidden, adapter_down, adapter_up, own_past, after):
    sp, fs = lax.axis_size("sp"), lax.axis_size("fsdp")
    z, x, r = (lax.axis_index(a) for a in ("sp", "fsdp", "rep"))
    c = lax.rem(r, 2)
    down_rows, up_rows = adapter_down.shape[0] // 2, RANK // 2
    blocks = adapter_up.shape[1] // HEAD_DIM
    down = lax.dynamic_slice_in_dim(adapter_down, c * down_rows, down_rows, 0)
    up = lax.dynamic_slice_in_dim(adapter_up, c * up_rows, up_rows, 0)
    up = [up[:, j * HEAD_DIM : (j + 1) * HEAD_DIM] for j in range(blocks)]
    rows = down_rows + blocks * up_rows
    buf = jnp.concatenate([down] + up + [own_past.reshape(-1, 2 * RANK)], axis=0)[None]
    step = 1
    while step < sp:
        buf = jnp.concatenate([buf, partner(buf, "sp", step)], axis=0)
        if step == 1:
            buf = tie(buf, after[0])
        step *= 2
    seqs, each = own_past.shape[:2]
    past = buf[:, rows:].reshape(sp, seqs, each, -1).swapaxes(0, 1).reshape(seqs, sp * each, -1)
    buf = buf[:, :rows]
    step = 1
    while step < fs:
        buf = jnp.concatenate([buf, partner(buf, "fsdp", step)], axis=0)
        step *= 2
    other = partner(tie(buf, after[1]), "rep", 1)
    index = jnp.stack([z, x, c]).astype(jnp.int32)
    vmem = pl.BlockSpec(memory_space=pltpu.VMEM)
    seqs, tokens = hidden.shape[:2]
    down_full, up_blocks, low = pl.pallas_call(
        functools.partial(low_rank_kernel, fs),
        in_specs=[pl.BlockSpec(memory_space=pltpu.SMEM)] + [vmem] * 3,
        out_specs=[vmem] * 3,
        out_shape=[
            jax.ShapeDtypeStruct((D, 2 * RANK), bf16),
            jax.ShapeDtypeStruct((HEADS + KV_HEADS, RANK, HEAD_DIM), bf16),
            jax.ShapeDtypeStruct((seqs, tokens, 2 * RANK), bf16),
        ],
        compiler_params=pltpu.CompilerParams(vmem_limit_bytes=32 * 1024 * 1024),
        cost_estimate=pl.CostEstimate(
            flops=2 * seqs * tokens * D * 2 * RANK, bytes_accessed=5 * 2**20, transcendentals=0
        ),
        name="low_rank",
    )(index, buf, other, hidden)
    return down_full, up_blocks, low, past


def adapters_plain(hidden, adapter_down, adapter_up, own_past, after):
    sp = lax.axis_size("sp")
    seqs, tokens = hidden.shape[:2]
    past = jnp.concatenate([own_past] + [cyclic(own_past, "sp", k) for k in range(1, sp)], axis=1)
    down_full = lax.all_gather(adapter_down, ("sp", "fsdp"), axis=0, tiled=True)
    up_full = lax.all_gather(adapter_up, ("sp", "fsdp"), axis=1, tiled=True)
    rows = hidden.reshape(seqs * tokens, D)
    low = jnp.dot(rows, down_full, preferred_element_type=f32).astype(bf16)
    up_blocks = up_full.reshape(RANK, HEADS + KV_HEADS, HEAD_DIM).swapaxes(0, 1)
    return down_full, up_blocks, low.reshape(seqs, tokens, 2 * RANK), past


def grad_hidden_kernel(low_ref, down_ref, out_ref):
    out = mm(low_ref[...], down_ref[...], 1, 1).astype(bf16)
    tokens = out_ref.shape[1]
    for s in range(out_ref.shape[0]):
        out_ref[s] = out[s * tokens : (s + 1) * tokens]


def grad_hidden_of(low_grad, down_full, seqs, tokens):
    columns = 1024
    return pl.pallas_call(
        grad_hidden_kernel,
        grid=(D // columns,),
        in_specs=[
            pl.BlockSpec(low_grad.shape, lambda i: (0, 0)),
            pl.BlockSpec((columns, 2 * RANK), lambda i: (i, 0)),
        ],
        out_specs=pl.BlockSpec((seqs, tokens, columns), lambda i: (0, 0, i)),
        out_shape=jax.ShapeDtypeStruct((seqs, tokens, D), bf16),
        compiler_params=pltpu.CompilerParams(vmem_limit_bytes=32 * 1024 * 1024),
        cost_estimate=pl.CostEstimate(
            flops=2 * seqs * tokens * D * 2 * RANK, bytes_accessed=2**21, transcendentals=0
        ),
        name="grad_hidden",
    )(low_grad, down_full)


def adapter_grads_kernel(core_ref, hidden_ref, low_ref, guq_ref, guv_ref, send_ref, keep_ref, gd_ref):
    c = core_ref[0]
    shards, pairs = send_ref.shape[:2]
    down_rows = gd_ref.shape[1]
    columns = 2 * pairs * down_rows
    blocks = (HEADS + KV_HEADS) // shards
    up_rows = guq_ref.shape[2]
    low = low_ref[...]
    for b in range(shards):
        cols = [hidden_ref[s, :, b * columns : (b + 1) * columns] for s in range(hidden_ref.shape[0])]
        part = mm(jnp.concatenate(cols, axis=0), low, 0, 0).astype(bf16)
        for q in range(2 * pairs):
            gd_ref[q] = part[q * down_rows : (q + 1) * down_rows]
        for hi in range(pairs):
            for ref, q in ((send_ref, 2 * hi + 1 - c), (keep_ref, 2 * hi + c)):
                ref[b, hi, :down_rows] = gd_ref[q]
                for j in range(blocks):
                    block = b * blocks + j
                    src = guq_ref[block, q] if block < HEADS else guv_ref[block - HEADS, q]
                    lo = down_rows + j * up_rows
                    ref[b, hi, lo : lo + up_rows] = src


def packed_grads(hidden, low_grad, guq, guv, shards):
    rp, r = lax.axis_size("rep"), lax.axis_index("rep")
    c = lax.rem(r, 2)
    down_rows, up_rows = D // (shards * rp), RANK // rp
    up_width = (D + KV) // shards
    rows = down_rows + up_rows * up_width // (2 * RANK)
    if up_width % HEAD_DIM == 0:
        vmem = pl.BlockSpec(memory_space=pltpu.VMEM)
        packed = jax.ShapeDtypeStruct((shards, rp // 2, rows, 2 * RANK), bf16)
        return pl.pallas_call(
            adapter_grads_kernel,
            in_specs=[pl.BlockSpec(memory_space=pltpu.SMEM)] + [vmem] * 4,
            out_specs=[vmem] * 2,
            out_shape=[packed] * 2,
            scratch_shapes=[pltpu.VMEM((rp, down_rows, 2 * RANK), bf16)],
            compiler_params=pltpu.CompilerParams(vmem_limit_bytes=32 * 1024 * 1024),
            cost_estimate=pl.CostEstimate(
                flops=2 * hidden.size * 2 * RANK, bytes_accessed=5 * 2**20, transcendentals=0
            ),
            name="adapter_grads",
        )(c.astype(jnp.int32).reshape(1), hidden, low_grad, guq, guv)
    own_rows = hidden.reshape(-1, D)
    down = jnp.dot(own_rows.T, low_grad, preferred_element_type=f32).astype(bf16)
    down = down.reshape(shards, rp, down_rows, 2 * RANK)
    up = jnp.concatenate([guq, guv], axis=0).transpose(1, 2, 0, 3)
    up = up.reshape(rp, up_rows, shards, up_width).transpose(2, 0, 1, 3)
    up = up.reshape(shards, rp, -1, 2 * RANK)
    both = jnp.concatenate([down, up], axis=2).reshape(shards, rp // 2, 2, rows, 2 * RANK)
    send = lax.dynamic_index_in_dim(both, 1 - c, 2, keepdims=False)
    keep = lax.dynamic_index_in_dim(both, c, 2, keepdims=False)
    return send, keep


def finish_grads(send, keep, before):
    sp, fs, rp = (lax.axis_size(a) for a in ("sp", "fsdp", "rep"))
    z, x, r = (lax.axis_index(a) for a in ("sp", "fsdp", "rep"))
    shards, _, rows, lanes = send.shape
    got = partner(send, "rep", 1)
    for b in range(1, rp.bit_length() - 1):
        shape = (shards, rp >> (b + 1), 2, rows, lanes)
        mine = lax.rem(lax.div(r, 1 << b), 2)

        def half(i):
            return sum(
                lax.dynamic_index_in_dim(a.reshape(shape), i, 2, keepdims=False).astype(f32)
                for a in (keep, got)
            ).astype(bf16)

        send, keep = half(1 - mine), half(mine)
        send = tie(send, before[0])
        got = partner(send, "rep", 1 << b)
    shape = (sp, fs, rows, lanes)

    def over_fsdp(i):
        return sum(
            lax.dynamic_index_in_dim(a.reshape(shape), i, 1, keepdims=False).astype(f32)
            for a in (keep, got)
        ).astype(bf16)

    total = over_fsdp(x).astype(f32)
    for k in range(1, fs):
        send = tie(over_fsdp(lax.rem(x + k, fs)), *before[:2])
        total = total + cyclic(send, "fsdp", k).astype(f32)
    over_sp = tie(total.astype(bf16), *before)
    total = lax.dynamic_index_in_dim(over_sp, z, 0, keepdims=False).astype(f32)
    for k in range(1, sp):
        send = lax.dynamic_index_in_dim(over_sp, lax.rem(z + k, sp), 0, keepdims=False)
        total = total + cyclic(send, "sp", k).astype(f32)
    own = total.astype(bf16)
    parts = [own] + [partner(own, "rep", m) for m in range(1, rp)]
    ordered = []
    for q in range(rp):
        pick = parts[0]
        for m in range(1, rp):
            pick = jnp.where((r ^ m) == q, parts[m], pick)
        ordered.append(pick.astype(f32))
    down_rows, up_rows = D // (shards * rp), RANK // rp
    up_width = (D + KV) // shards
    grad_down = jnp.concatenate([p[:down_rows] for p in ordered], axis=0)
    ups = []
    for p in ordered:
        up = p[down_rows:]
        if up_width % HEAD_DIM == 0:
            up = [up[lo : lo + up_rows] for lo in range(0, up.shape[0], up_rows)]
            up = jnp.concatenate(up, axis=1)
        ups.append(up.reshape(up_rows, up_width))
    return grad_down, jnp.concatenate(ups, axis=0)


def body(
    hidden,
    query_base,
    key_span,
    value_base,
    past_keys,
    past_values,
    grad_out,
    adapter_down,
    adapter_up,
):
    sp, fs = lax.axis_size("sp"), lax.axis_size("fsdp")
    z = lax.axis_index("sp")
    seqs, tokens = hidden.shape[:2]
    past_len = past_keys.shape[1] * sp
    own_past = jnp.concatenate([past_keys, past_values], axis=2)
    own_kvs = []
    for first, last in CHUNKS:
        cols = slice(first * HEAD_DIM, last * HEAD_DIM)
        own_kvs.append(jnp.concatenate([key_span[:, :, cols], value_base[:, :, cols]], axis=2))
    early = [own_kvs[0]]
    for k in range(1, sp):
        early.append(along(early[k - 1], "sp", 1))

    even = adapter_up.shape[1] % HEAD_DIM == 0
    adapters = adapters_packed if even else adapters_plain
    down_full, up_blocks, low_own, past = adapters(
        hidden, adapter_down, adapter_up, own_past, (early[1], early[min(2, sp - 1)])
    )
    low_own = tie(low_own, early[-1])
    late = [own_kvs[1]] + [along(tie(own_kvs[1], low_own), "sp", k) for k in range(1, sp)]
    lows = [low_own] + [along(low_own, "sp", k) for k in range(1, sp)]
    cos, sin = rotary_tables(tokens, past_len + z * tokens)
    place = z.astype(jnp.int32).reshape(1)

    made = None
    for (first, last), kvs in zip(CHUNKS, (early, late)):
        made = attention_chunk(
            first, last, place, query_base, grad_out, up_blocks, past, cos, sin, lows, kvs, made
        )
    attended, grad_query, guq, guv = made[:4]
    gvs = made[4 : 4 + sp]
    low_grad_q, low_grad_v = made[4 + sp :]

    low_v_total = low_grad_v[:, :tokens]
    for k in range(1, sp):
        part = low_grad_v[:, k * tokens : (k + 1) * tokens].astype(bf16)
        low_v_total = low_v_total + along(part, "sp", -k).astype(f32)
    low_grad = (
        jnp.concatenate([low_grad_q, low_v_total], axis=2)
        .astype(bf16)
        .reshape(seqs * tokens, 2 * RANK)
    )
    send, keep = packed_grads(hidden, low_grad, guq, guv, sp * fs)
    value_parts = [along(gvs[k], "sp", -k) for k in range(1, sp)]
    grad_down, grad_up = finish_grads(send, keep, value_parts)
    grad_hidden = grad_hidden_of(low_grad, down_full, seqs, tokens)

    grad_value = gvs[0].astype(f32)
    for part in value_parts:
        grad_value = grad_value + part.astype(f32)
    return (
        attended,
        grad_query,
        grad_value.astype(bf16),
        grad_hidden,
        grad_down,
        grad_up,
    )


def solution(mesh):
    rows = P(("fsdp", "rep"), "sp", None)
    down, up = P(("sp", "fsdp"), None), P(None, ("sp", "fsdp"))
    return jax.shard_map(
        body,
        mesh=mesh,
        in_specs=(rows,) * 7 + (down, up),
        out_specs=(rows,) * 4 + (down, up),
        check_vma=False,
    )
```

```python
import functools
import math

import jax
import jax.numpy as jnp
from jax import lax
from jax.experimental import pallas as pl
from jax.experimental.pallas import tpu as pltpu
from jax.sharding import PartitionSpec as P

D = 4096
HEADS = 32
KV_HEADS = 8
HEAD_DIM = 128
RANK = 64
KV = 1024
GROUP = HEADS // KV_HEADS
WIDE = GROUP * HEAD_DIM
ROPE_BASE = 500000.0
HIDDEN_MASK = -1e30
CHUNKS = ((0, 5), (5, 8))
LOG2_E = 1.4426950408889634

f32 = jnp.float32
bf16 = jnp.bfloat16


def rotary_tables(row_count, offset):
    half = HEAD_DIM // 2
    position = (jnp.arange(row_count, dtype=jnp.int32) + offset).astype(f32)
    inverse = jnp.exp(jnp.arange(half, dtype=f32) * (-2.0 * math.log(ROPE_BASE) / HEAD_DIM))
    angle = position[:, None] * inverse[None, :]
    cosine, sine = jnp.cos(angle), jnp.sin(angle)
    return (
        jnp.concatenate([cosine, cosine], axis=1),
        jnp.concatenate([-sine, sine], axis=1),
    )


def cyclic(x, axis, shift):
    n = lax.axis_size(axis)
    return lax.ppermute(x, axis, [(i, (i + shift) % n) for i in range(n)])


def along(x, axis, shift):
    n = lax.axis_size(axis)
    return lax.ppermute(x, axis, [(i, i + shift) for i in range(n) if 0 <= i + shift < n])


def partner(x, axis, mask):
    n = lax.axis_size(axis)
    return lax.ppermute(x, axis, [(i, i ^ mask) for i in range(n)])


def tie(x, *others):
    return lax.optimization_barrier((x,) + others)[0]


def mm(a, b, ca, cb):
    return lax.dot_general(a, b, (((ca,), (cb,)), ((), ())), preferred_element_type=f32)


def attention_kernel(shards, earlier_count, place_ref, *refs):
    it = iter(refs)

    def take(n):
        return [next(it) for _ in range(n)]

    q_ref, g_ref, upq_ref, upv_ref, pk_ref, pv_ref, cos_ref, sin_ref = take(8)
    low_refs, k_refs, v_refs = take(shards), take(shards), take(shards)
    before = take(2) if earlier_count else None
    take(earlier_count)
    att_ref, gq_ref, guq_ref, guv_ref, lgq_ref, lgv_ref = take(6)
    gv_refs = take(shards)

    seqs, tokens = q_ref.shape[0], q_ref.shape[1]
    parts, part_rows = guq_ref.shape[1:3]
    span = shards * tokens
    past = pk_ref.shape[1]
    scale = 1.0 / math.sqrt(HEAD_DIM)
    place = place_ref[0]
    cos, sin = cos_ref[...], sin_ref[...]
    upq = jnp.concatenate([upq_ref[h] for h in range(GROUP)], axis=1)
    upv = upv_ref[0]

    @pl.when(pl.program_id(0) == 0)
    def _():
        if before is None:
            lgq_ref[...] = jnp.zeros_like(lgq_ref)
            lgv_ref[...] = jnp.zeros_like(lgv_ref)
        else:
            lgq_ref[...] = before[0][...]
            lgv_ref[...] = before[1][...]

    col = lax.broadcasted_iota(jnp.int32, (tokens, span + past), 1)
    row = lax.broadcasted_iota(jnp.int32, (tokens, span + past), 0)
    seen = (col <= row) | ((col >= tokens) & (col < (place + 1) * tokens)) | (col >= span)
    bias = jnp.where(seen, 0.0, HIDDEN_MASK)
    bias = jnp.concatenate([bias] * GROUP, axis=0)

    def heads(x):
        return jnp.concatenate(
            [x[:, h * HEAD_DIM : (h + 1) * HEAD_DIM] for h in range(GROUP)], axis=0
        )

    def lanes(x):
        return jnp.concatenate([x[h * tokens : (h + 1) * tokens] for h in range(GROUP)], axis=1)

    cos4 = jnp.concatenate([cos] * GROUP, axis=0)
    sin4 = jnp.concatenate([sin] * GROUP, axis=0)
    every = range(seqs)
    low_q = jnp.concatenate([low_refs[0][s][:, :RANK] for s in every], axis=0)
    low_v = jnp.concatenate([r[s][:, RANK:] for s in every for r in low_refs], axis=0)
    query_delta = mm(low_q, upq, 1, 0)
    value_delta = mm(low_v, upv, 1, 0)
    backs, gvs = [], []
    for s in every:
        delta = heads(query_delta[s * tokens : (s + 1) * tokens])
        delta = delta * cos4 + pltpu.roll(delta, HEAD_DIM // 2, 1) * sin4
        q = (heads(q_ref[s]).astype(f32) + delta).astype(bf16)
        g = heads(g_ref[s])
        keys = jnp.concatenate([r[s] for r in k_refs] + [pk_ref[s]], axis=0)
        base = jnp.concatenate([r[s] for r in v_refs], axis=0).astype(f32)
        vals = (base + value_delta[s * span : (s + 1) * span]).astype(bf16)
        vals = jnp.concatenate([vals, pv_ref[s]], axis=0)

        scores = mm(q, keys, 1, 1) * (scale * LOG2_E) + bias
        top = jnp.max(scores, axis=-1, keepdims=True)
        e = jnp.exp2(scores - top)
        inverse = 1.0 / jnp.sum(e, axis=-1, keepdims=True)
        weights = e.astype(bf16)
        out = (mm(weights, vals, 1, 0) * inverse).astype(bf16)
        att_ref[s] = lanes(out)
        g = (g.astype(f32) * inverse).astype(bf16)
        prob_grad = mm(g, vals, 1, 1)
        row_delta = jnp.sum(g.astype(f32) * out.astype(f32), axis=-1, keepdims=True)
        score_grad = (e * (prob_grad - row_delta)).astype(bf16)
        gq = (mm(score_grad, keys, 1, 0) * scale).astype(bf16)
        gq_ref[s] = lanes(gq)
        gq32 = gq.astype(f32)
        back = (gq32 * cos4 - pltpu.roll(gq32, HEAD_DIM // 2, 1) * sin4).astype(bf16)
        backs.append(lanes(back))
        gv = mm(weights[:, :span], g, 0, 0).astype(bf16)
        gvs.append(gv)
        for k in range(shards):
            gv_refs[k][s] = gv[k * tokens : (k + 1) * tokens]
    back = jnp.concatenate(backs, axis=0)
    gv = jnp.concatenate(gvs, axis=0)
    low_grad_q = mm(back, upq, 1, 1)
    low_grad_v = mm(gv, upv, 1, 1)
    for s in every:
        lgq_ref[s] += low_grad_q[s * tokens : (s + 1) * tokens]
        lgv_ref[s] += low_grad_v[s * span : (s + 1) * span]
    grad_up_q = mm(low_q, back, 0, 0)
    grad_up_v = mm(low_v, gv, 0, 0)
    grad_up_q, grad_up_v = grad_up_q.astype(bf16), grad_up_v.astype(bf16)
    for p in range(parts):
        rows = slice(p * part_rows, (p + 1) * part_rows)
        for h in range(GROUP):
            guq_ref[h, p] = grad_up_q[rows, h * HEAD_DIM : (h + 1) * HEAD_DIM]
        guv_ref[0, p] = grad_up_v[rows]


def attention_chunk(
    first, last, place, query_base, grad_out, up_blocks, past, cos, sin, lows, kvs, earlier
):
    shards = len(kvs)
    parts = lax.axis_size("rep")
    seqs, tokens = query_base.shape[:2]
    past_len = past.shape[1]
    groups = last - first

    def whole(x):
        return pl.BlockSpec(x.shape, lambda g: (0,) * len(x.shape))

    spec = pl.BlockSpec
    q_spec = spec((seqs, tokens, WIDE), lambda g: (0, 0, first + g))
    gv_spec = spec((seqs, tokens, HEAD_DIM), lambda g: (0, 0, g))
    past_block = (seqs, past_len, HEAD_DIM)
    in_specs = [
        spec(memory_space=pltpu.SMEM),
        q_spec,
        q_spec,
        spec((GROUP, RANK, HEAD_DIM), lambda g: (first + g, 0, 0)),
        spec((1, RANK, HEAD_DIM), lambda g: (HEADS + first + g, 0, 0)),
        spec(past_block, lambda g: (0, 0, first + g)),
        spec(past_block, lambda g: (0, 0, KV_HEADS + first + g)),
        whole(cos),
        whole(sin),
    ]
    in_specs += [whole(x) for x in lows]
    in_specs += [spec((seqs, tokens, HEAD_DIM), lambda g: (0, 0, g))] * shards
    in_specs += [spec((seqs, tokens, HEAD_DIM), lambda g: (0, 0, groups + g))] * shards
    operands = [place, query_base, grad_out, up_blocks, up_blocks, past, past, cos, sin]
    operands += list(lows) + list(kvs) + list(kvs)
    shape = jax.ShapeDtypeStruct
    low_q_shape = shape((seqs, tokens, RANK), f32)
    low_v_shape = shape((seqs, shards * tokens, RANK), f32)
    placed_shapes = [
        shape(query_base.shape, bf16),
        shape(query_base.shape, bf16),
        shape((HEADS, parts, RANK // parts, HEAD_DIM), bf16),
        shape((KV_HEADS, parts, RANK // parts, HEAD_DIM), bf16),
    ]
    placed_specs = [
        q_spec,
        q_spec,
        spec((GROUP, parts, RANK // parts, HEAD_DIM), lambda g: (first + g, 0, 0, 0)),
        spec((1, parts, RANK // parts, HEAD_DIM), lambda g: (first + g, 0, 0, 0)),
    ]
    aliases = {}
    placed = len(placed_shapes)
    if earlier is not None:
        in_specs += [whole(low_q_shape), whole(low_v_shape)]
        operands += list(earlier[placed : placed + 2])
        aliases = {len(operands) + i: i for i in range(placed)}
        in_specs += [spec(memory_space=pl.ANY)] * placed
        operands += list(earlier[:placed])
    scores = GROUP * tokens * (shards * tokens + past_len)
    pairs = seqs * groups * scores
    grant = min(12 * 2**20 + 96 * scores, 48 * 2**20)
    return pl.pallas_call(
        functools.partial(attention_kernel, shards, placed if earlier is not None else 0),
        grid=(groups,),
        in_specs=in_specs,
        out_specs=placed_specs + [whole(low_q_shape), whole(low_v_shape)] + [gv_spec] * shards,
        out_shape=placed_shapes
        + [low_q_shape, low_v_shape]
        + [shape((seqs, tokens, groups * HEAD_DIM), bf16)] * shards,
        input_output_aliases=aliases,
        compiler_params=pltpu.CompilerParams(vmem_limit_bytes=grant),
        cost_estimate=pl.CostEstimate(
            flops=pairs * HEAD_DIM * 28, bytes_accessed=16 * 1024 * 1024, transcendentals=pairs
        ),
        name="attention",
    )(*operands)


def low_rank_kernel(fs, index_ref, own_ref, other_ref, hidden_ref, down_ref, up_ref, low_ref):
    z, x, c = index_ref[0], index_ref[1], index_ref[2]
    pieces = own_ref.shape[0]
    sp = pieces // fs
    down_rows = D // (2 * pieces)
    blocks = up_ref.shape[0] // pieces
    up_rows = RANK // 2
    for r in range(pieces):
        shard = (z ^ (r % sp)) * fs + (x ^ (r // sp))
        for ref, half in ((own_ref, c), (other_ref, 1 - c)):
            at = pl.multiple_of((shard * 2 + half) * down_rows, down_rows)
            down_ref[pl.ds(at, down_rows), :] = ref[r, :down_rows]
            at = pl.multiple_of(half * up_rows, up_rows)
            for j in range(blocks):
                lo = down_rows + j * up_rows
                up_ref[shard * blocks + j, pl.ds(at, up_rows), :] = ref[r, lo : lo + up_rows]
    rows = jnp.concatenate([hidden_ref[s] for s in range(hidden_ref.shape[0])], axis=0)
    low = mm(rows, down_ref[...], 1, 0).astype(bf16)
    for s in range(low_ref.shape[0]):
        low_ref[s] = low[s * low_ref.shape[1] : (s + 1) * low_ref.shape[1]]


def pack_adapters(adapter_down, adapter_up, own_past):
    sp = lax.axis_size("sp")
    c = lax.rem(lax.axis_index("rep"), 2)
    down_rows, up_rows = adapter_down.shape[0] // 2, RANK // 2
    blocks = adapter_up.shape[1] // HEAD_DIM
    down = lax.dynamic_slice_in_dim(adapter_down, c * down_rows, down_rows, 0)
    up = lax.dynamic_slice_in_dim(adapter_up, c * up_rows, up_rows, 0)
    up = [up[:, j * HEAD_DIM : (j + 1) * HEAD_DIM] for j in range(blocks)]
    rows = down_rows + blocks * up_rows
    buf = jnp.concatenate([down] + up + [own_past.reshape(-1, 2 * RANK)], axis=0)[None]
    step = 1
    while step < sp:
        buf = jnp.concatenate([buf, partner(buf, "sp", step)], axis=0)
        step *= 2
    seqs, each = own_past.shape[:2]
    past = buf[:, rows:].reshape(sp, seqs, each, -1).swapaxes(0, 1).reshape(seqs, sp * each, -1)
    return buf[:, :rows], past


def adapters_packed(hidden, buf, before_swap):
    fs = lax.axis_size("fsdp")
    z, x, r = (lax.axis_index(a) for a in ("sp", "fsdp", "rep"))
    c = lax.rem(r, 2)
    step = 1
    while step < fs:
        buf = jnp.concatenate([buf, partner(buf, "fsdp", step)], axis=0)
        step *= 2
    other = partner(tie(buf, before_swap), "rep", 1)
    index = jnp.stack([z, x, c]).astype(jnp.int32)
    vmem = pl.BlockSpec(memory_space=pltpu.VMEM)
    seqs, tokens = hidden.shape[:2]
    down_full, up_blocks, low = pl.pallas_call(
        functools.partial(low_rank_kernel, fs),
        in_specs=[pl.BlockSpec(memory_space=pltpu.SMEM)] + [vmem] * 3,
        out_specs=[vmem] * 3,
        out_shape=[
            jax.ShapeDtypeStruct((D, 2 * RANK), bf16),
            jax.ShapeDtypeStruct((HEADS + KV_HEADS, RANK, HEAD_DIM), bf16),
            jax.ShapeDtypeStruct((seqs, tokens, 2 * RANK), bf16),
        ],
        compiler_params=pltpu.CompilerParams(vmem_limit_bytes=16 * 1024 * 1024),
        cost_estimate=pl.CostEstimate(
            flops=2 * seqs * tokens * D * 2 * RANK, bytes_accessed=5 * 2**20, transcendentals=0
        ),
        name="low_rank",
    )(index, buf, other, hidden)
    return down_full, up_blocks, low


def adapters_plain(hidden, adapter_down, adapter_up):
    seqs, tokens = hidden.shape[:2]
    down_full = lax.all_gather(adapter_down, ("sp", "fsdp"), axis=0, tiled=True)
    up_full = lax.all_gather(adapter_up, ("sp", "fsdp"), axis=1, tiled=True)
    rows = hidden.reshape(seqs * tokens, D)
    low = jnp.dot(rows, down_full, preferred_element_type=f32).astype(bf16)
    up_blocks = up_full.reshape(RANK, HEADS + KV_HEADS, HEAD_DIM).swapaxes(0, 1)
    return down_full, up_blocks, low.reshape(seqs, tokens, 2 * RANK)


def grad_hidden_kernel(low_ref, down_ref, out_ref):
    out = mm(low_ref[...], down_ref[...], 1, 1).astype(bf16)
    tokens = out_ref.shape[1]
    for s in range(out_ref.shape[0]):
        out_ref[s] = out[s * tokens : (s + 1) * tokens]


def grad_hidden_of(low_grad, down_full, seqs, tokens):
    columns = 1024
    return pl.pallas_call(
        grad_hidden_kernel,
        grid=(D // columns,),
        in_specs=[
            pl.BlockSpec(low_grad.shape, lambda i: (0, 0)),
            pl.BlockSpec((columns, 2 * RANK), lambda i: (i, 0)),
        ],
        out_specs=pl.BlockSpec((seqs, tokens, columns), lambda i: (0, 0, i)),
        out_shape=jax.ShapeDtypeStruct((seqs, tokens, D), bf16),
        compiler_params=pltpu.CompilerParams(vmem_limit_bytes=16 * 1024 * 1024),
        cost_estimate=pl.CostEstimate(
            flops=2 * seqs * tokens * D * 2 * RANK, bytes_accessed=2**21, transcendentals=0
        ),
        name="grad_hidden",
    )(low_grad, down_full)


def adapter_grads_kernel(core_ref, hidden_ref, low_ref, guq_ref, guv_ref, send_ref, keep_ref, gd_ref):
    c = core_ref[0]
    shards, pairs = send_ref.shape[:2]
    down_rows = gd_ref.shape[1]
    columns = 2 * pairs * down_rows
    blocks = (HEADS + KV_HEADS) // shards
    up_rows = guq_ref.shape[2]
    low = low_ref[...]
    for b in range(shards):
        cols = [hidden_ref[s, :, b * columns : (b + 1) * columns] for s in range(hidden_ref.shape[0])]
        part = mm(jnp.concatenate(cols, axis=0), low, 0, 0).astype(bf16)
        for q in range(2 * pairs):
            gd_ref[q] = part[q * down_rows : (q + 1) * down_rows]
        for hi in range(pairs):
            for ref, q in ((send_ref, 2 * hi + 1 - c), (keep_ref, 2 * hi + c)):
                ref[b, hi, :down_rows] = gd_ref[q]
                for j in range(blocks):
                    block = b * blocks + j
                    src = guq_ref[block, q] if block < HEADS else guv_ref[block - HEADS, q]
                    lo = down_rows + j * up_rows
                    ref[b, hi, lo : lo + up_rows] = src


def packed_grads(hidden, low_grad, guq, guv, shards):
    rp, r = lax.axis_size("rep"), lax.axis_index("rep")
    c = lax.rem(r, 2)
    down_rows, up_rows = D // (shards * rp), RANK // rp
    up_width = (D + KV) // shards
    rows = down_rows + up_rows * up_width // (2 * RANK)
    if up_width % HEAD_DIM == 0:
        vmem = pl.BlockSpec(memory_space=pltpu.VMEM)
        packed = jax.ShapeDtypeStruct((shards, rp // 2, rows, 2 * RANK), bf16)
        return pl.pallas_call(
            adapter_grads_kernel,
            in_specs=[pl.BlockSpec(memory_space=pltpu.SMEM)] + [vmem] * 4,
            out_specs=[vmem] * 2,
            out_shape=[packed] * 2,
            scratch_shapes=[pltpu.VMEM((rp, down_rows, 2 * RANK), bf16)],
            compiler_params=pltpu.CompilerParams(vmem_limit_bytes=16 * 1024 * 1024),
            cost_estimate=pl.CostEstimate(
                flops=2 * hidden.size * 2 * RANK, bytes_accessed=5 * 2**20, transcendentals=0
            ),
            name="adapter_grads",
        )(c.astype(jnp.int32).reshape(1), hidden, low_grad, guq, guv)
    own_rows = hidden.reshape(-1, D)
    down = jnp.dot(own_rows.T, low_grad, preferred_element_type=f32).astype(bf16)
    down = down.reshape(shards, rp, down_rows, 2 * RANK)
    up = jnp.concatenate([guq, guv], axis=0).transpose(1, 2, 0, 3)
    up = up.reshape(rp, up_rows, shards, up_width).transpose(2, 0, 1, 3)
    up = up.reshape(shards, rp, -1, 2 * RANK)
    both = jnp.concatenate([down, up], axis=2).reshape(shards, rp // 2, 2, rows, 2 * RANK)
    send = lax.dynamic_index_in_dim(both, 1 - c, 2, keepdims=False)
    keep = lax.dynamic_index_in_dim(both, c, 2, keepdims=False)
    return send, keep


def finish_grads(send, keep, values):
    sp, fs, rp = (lax.axis_size(a) for a in ("sp", "fsdp", "rep"))
    z, r = lax.axis_index("sp"), lax.axis_index("rep")
    shards, _, rows, lanes = send.shape
    got = partner(send, "rep", 1)
    then = [along(tie(v, got), "sp", -k) for k, v in enumerate(values, 1)]
    fs_bits, rep_bits = fs.bit_length() - 1, rp.bit_length() - 2
    labels = [("fsdp", b) for b in reversed(range(fs_bits))]
    labels += [("rep", b + 1) for b in reversed(range(rep_bits))]
    shape = (sp,) + (2,) * len(labels) + (rows, lanes)
    terms = [a.reshape(shape) for a in (keep, got)]

    def halve(terms, order, before):
        left = list(labels)
        for step, label in enumerate(order):
            axis, bit = label
            dim = 1 + left.index(label)
            left.remove(label)
            mine = lax.rem(lax.div(lax.axis_index(axis), 1 << bit), 2)

            def pick(i):
                parts = [lax.dynamic_index_in_dim(a, i, dim, keepdims=False) for a in terms]
                return sum(a.astype(f32) for a in parts).astype(bf16)

            send = pick(1 - mine)
            if step == 1:
                send = tie(send, *before)
            terms = [pick(mine), partner(send, axis, 1 << bit)]
        return sum(a.astype(f32) for a in terms).astype(bf16)

    cut = rows // 32 * 16
    first_rep, first_fsdp = labels[::-1], labels
    over_sp = halve([a[..., cut:, :] for a in terms], first_rep, then[:1])
    if cut:
        other = halve([a[..., :cut, :] for a in terms], first_fsdp, ())
        over_sp = jnp.concatenate([other, over_sp], axis=1)
    over_sp = tie(over_sp, *then)
    total = lax.dynamic_index_in_dim(over_sp, z, 0, keepdims=False).astype(f32)
    for k in range(1, sp):
        send = lax.dynamic_index_in_dim(over_sp, lax.rem(z + k, sp), 0, keepdims=False)
        total = total + cyclic(send, "sp", k).astype(f32)
    own = total.astype(bf16)
    parts = [own] + [partner(own, "rep", m) for m in range(1, rp)]
    ordered = []
    for q in range(rp):
        pick = parts[0]
        for m in range(1, rp):
            pick = jnp.where((r ^ m) == q, parts[m], pick)
        ordered.append(pick.astype(f32))
    down_rows, up_rows = D // (shards * rp), RANK // rp
    up_width = (D + KV) // shards
    grad_down = jnp.concatenate([p[:down_rows] for p in ordered], axis=0)
    ups = []
    for p in ordered:
        up = p[down_rows:]
        if up_width % HEAD_DIM == 0:
            up = [up[lo : lo + up_rows] for lo in range(0, up.shape[0], up_rows)]
            up = jnp.concatenate(up, axis=1)
        ups.append(up.reshape(up_rows, up_width))
    return grad_down, jnp.concatenate(ups, axis=0), then, over_sp


def body(
    hidden,
    query_base,
    key_span,
    value_base,
    past_keys,
    past_values,
    grad_out,
    adapter_down,
    adapter_up,
):
    sp, fs = lax.axis_size("sp"), lax.axis_size("fsdp")
    z = lax.axis_index("sp")
    seqs, tokens = hidden.shape[:2]
    past_len = past_keys.shape[1] * sp
    own_past = jnp.concatenate([past_keys, past_values], axis=2)
    own_kvs = []
    for first, last in CHUNKS:
        cols = slice(first * HEAD_DIM, last * HEAD_DIM)
        own_kvs.append(jnp.concatenate([key_span[:, :, cols], value_base[:, :, cols]], axis=2))
    early = [own_kvs[0]]
    even = adapter_up.shape[1] % HEAD_DIM == 0
    if even:
        buf, past = pack_adapters(adapter_down, adapter_up, own_past)
    else:
        buf = own_past
        past = [own_past] + [cyclic(own_past, "sp", k) for k in range(1, sp)]
        past = jnp.concatenate(past, axis=1)
    early.append(along(tie(early[0], buf), "sp", 1))
    for k in range(2, sp):
        early.append(along(early[k - 1], "sp", 1))
    if even:
        down_full, up_blocks, low_own = adapters_packed(hidden, buf, early[1])
    else:
        down_full, up_blocks, low_own = adapters_plain(hidden, adapter_down, adapter_up)
    low_sent = tie(low_own, early[min(2, sp - 1)])
    lows = [low_own] + [along(low_sent, "sp", k) for k in range(1, sp)]
    own_late = tie(own_kvs[1], low_own, early[-1])
    late = [own_kvs[1]] + [along(own_late, "sp", k) for k in range(1, sp)]
    cos, sin = rotary_tables(tokens, past_len + z * tokens)
    place = z.astype(jnp.int32).reshape(1)

    made = None
    value_own, value_got = [], []
    for (first, last), kvs in zip(CHUNKS, (early, late)):
        made = attention_chunk(
            first, last, place, query_base, grad_out, up_blocks, past, cos, sin, lows, kvs, made
        )
        gvs = made[6:]
        value_own.append(gvs[0])
        if last < KV_HEADS:
            value_got.append([along(gvs[k], "sp", -k) for k in range(1, sp)])
    attended, grad_query, guq, guv, low_grad_q, low_grad_v = made[:6]

    low_v_total = low_grad_v[:, :tokens]
    for k in range(1, sp):
        part = low_grad_v[:, k * tokens : (k + 1) * tokens].astype(bf16)
        part = tie(part, *value_got[0])
        low_v_total = low_v_total + along(part, "sp", -k).astype(f32)
    low_grad = (
        jnp.concatenate([low_grad_q, low_v_total], axis=2)
        .astype(bf16)
        .reshape(seqs * tokens, 2 * RANK)
    )
    send, keep = packed_grads(hidden, low_grad, guq, guv, sp * fs)
    grad_down, grad_up, got, mark = finish_grads(send, keep, gvs[1:])
    value_got.append(got)
    grad_hidden = grad_hidden_of(tie(low_grad, mark), down_full, seqs, tokens)

    sums = []
    for own, got in zip(value_own, value_got):
        total = own.astype(f32)
        for part in got:
            total = total + part.astype(f32)
        sums.append(total.astype(bf16))
    grad_value = jnp.concatenate(sums, axis=2)
    return (
        attended,
        grad_query,
        grad_value,
        grad_hidden,
        grad_down,
        grad_up,
    )


def solution(mesh):
    rows = P(("fsdp", "rep"), "sp", None)
    down, up = P(("sp", "fsdp"), None), P(None, ("sp", "fsdp"))
    return jax.shard_map(
        body,
        mesh=mesh,
        in_specs=(rows,) * 7 + (down, up),
        out_specs=(rows,) * 4 + (down, up),
        check_vma=False,
    )
```

```python
import functools
import math

import jax
import jax.numpy as jnp
from jax import lax
from jax.experimental import pallas as pl
from jax.experimental.pallas import tpu as pltpu
from jax.sharding import PartitionSpec as P

D = 4096
HEADS = 32
KV_HEADS = 8
HEAD_DIM = 128
RANK = 64
KV = 1024
GROUP = HEADS // KV_HEADS
WIDE = GROUP * HEAD_DIM
ROPE_BASE = 500000.0
HIDDEN_MASK = -1e30
CHUNKS = ((0, 5), (5, 8))
LOG2_E = 1.4426950408889634

f32 = jnp.float32
bf16 = jnp.bfloat16


def rotary_tables(row_count, offset):
    half = HEAD_DIM // 2
    position = (jnp.arange(row_count, dtype=jnp.int32) + offset).astype(f32)
    inverse = jnp.exp(jnp.arange(half, dtype=f32) * (-2.0 * math.log(ROPE_BASE) / HEAD_DIM))
    angle = position[:, None] * inverse[None, :]
    cosine, sine = jnp.cos(angle), jnp.sin(angle)
    return (
        jnp.concatenate([cosine, cosine], axis=1),
        jnp.concatenate([-sine, sine], axis=1),
    )


def cyclic(x, axis, shift):
    n = lax.axis_size(axis)
    return lax.ppermute(x, axis, [(i, (i + shift) % n) for i in range(n)])


def along(x, axis, shift, start=0):
    n = lax.axis_size(axis)
    return lax.ppermute(x, axis, [(i, i + shift) for i in range(start, n) if 0 <= i + shift < n])


def partner(x, axis, mask):
    n = lax.axis_size(axis)
    return lax.ppermute(x, axis, [(i, i ^ mask) for i in range(n)])


def tie(x, *others):
    return lax.optimization_barrier((x,) + others)[0]


def mm(a, b, ca, cb):
    return lax.dot_general(a, b, (((ca,), (cb,)), ((), ())), preferred_element_type=f32)


def attention_kernel(shards, earlier_count, first, place_ref, *refs):
    it = iter(refs)

    def take(n):
        return [next(it) for _ in range(n)]

    q_hbm, g_hbm, upq_ref, upv_ref, pk_ref, pv_ref, cos_ref, sin_ref = take(8)
    low_refs, k_refs, v_refs = take(shards), take(shards), take(shards)
    before = take(2) if earlier_count else None
    take(earlier_count)
    att_ref, gq_ref, guq_ref, guv_ref, lgq_ref, lgv_ref = take(6)
    gv_refs = take(shards)
    q_buf, g_buf, sems = take(3)

    group, slot = pl.program_id(0), lax.rem(pl.program_id(0), 2)

    def fetches(step, into):
        at = pl.multiple_of((first + step) * WIDE, WIDE)
        return [
            pltpu.make_async_copy(hbm.at[:, :, pl.ds(at, WIDE)], buf.at[into], sems.at[i, into])
            for i, (hbm, buf) in enumerate(((q_hbm, q_buf), (g_hbm, g_buf)))
        ]

    @pl.when(group == 0)
    def _():
        for copy in fetches(0, 0):
            copy.start()

    @pl.when(group + 1 < pl.num_programs(0))
    def _():
        for copy in fetches(group + 1, 1 - slot):
            copy.start()

    seqs, tokens = q_buf.shape[1:3]
    parts, part_rows = guq_ref.shape[1:3]
    span = shards * tokens
    past = pk_ref.shape[1]
    scale = 1.0 / math.sqrt(HEAD_DIM)
    place = place_ref[0]
    cos, sin = cos_ref[...], sin_ref[...]
    upq = jnp.concatenate([upq_ref[h] for h in range(GROUP)], axis=1)
    upv = upv_ref[0]

    @pl.when(pl.program_id(0) == 0)
    def _():
        if before is None:
            lgq_ref[...] = jnp.zeros_like(lgq_ref)
            lgv_ref[...] = jnp.zeros_like(lgv_ref)
        else:
            lgq_ref[...] = before[0][...]
            lgv_ref[...] = before[1][...]

    col = lax.broadcasted_iota(jnp.int32, (tokens, span + past), 1)
    row = lax.broadcasted_iota(jnp.int32, (tokens, span + past), 0)
    seen = (col <= row) | ((col >= tokens) & (col < (place + 1) * tokens)) | (col >= span)
    bias = jnp.where(seen, 0.0, HIDDEN_MASK)
    bias = jnp.concatenate([bias] * GROUP, axis=0)

    def heads(x):
        return jnp.concatenate(
            [x[:, h * HEAD_DIM : (h + 1) * HEAD_DIM] for h in range(GROUP)], axis=0
        )

    def lanes(x):
        return jnp.concatenate([x[h * tokens : (h + 1) * tokens] for h in range(GROUP)], axis=1)

    cos4 = jnp.concatenate([cos] * GROUP, axis=0)
    sin4 = jnp.concatenate([sin] * GROUP, axis=0)
    every = range(seqs)
    low_q = jnp.concatenate([low_refs[0][s][:, :RANK] for s in every], axis=0)
    low_v = jnp.concatenate([r[s][:, RANK:] for s in every for r in low_refs], axis=0)
    query_delta = mm(low_q, upq, 1, 0)
    value_delta = mm(low_v, upv, 1, 0)
    for copy in fetches(group, slot):
        copy.wait()
    backs, gvs = [], []
    for s in every:
        delta = heads(query_delta[s * tokens : (s + 1) * tokens])
        delta = delta * cos4 + pltpu.roll(delta, HEAD_DIM // 2, 1) * sin4
        q = (heads(q_buf[slot, s]).astype(f32) + delta).astype(bf16)
        g = heads(g_buf[slot, s])
        keys = jnp.concatenate([r[s] for r in k_refs] + [pk_ref[s]], axis=0)
        base = jnp.concatenate([r[s] for r in v_refs], axis=0).astype(f32)
        vals = (base + value_delta[s * span : (s + 1) * span]).astype(bf16)
        vals = jnp.concatenate([vals, pv_ref[s]], axis=0)

        scores = mm(q, keys, 1, 1) * (scale * LOG2_E) + bias
        top = jnp.max(scores, axis=-1, keepdims=True)
        e = jnp.exp2(scores - top)
        inverse = 1.0 / jnp.sum(e, axis=-1, keepdims=True)
        weights = e.astype(bf16)
        out = (mm(weights, vals, 1, 0) * inverse).astype(bf16)
        att_ref[s] = lanes(out)
        g = (g.astype(f32) * inverse).astype(bf16)
        prob_grad = mm(g, vals, 1, 1)
        row_delta = jnp.sum(g.astype(f32) * out.astype(f32), axis=-1, keepdims=True)
        score_grad = (e * (prob_grad - row_delta)).astype(bf16)
        gq = (mm(score_grad, keys, 1, 0) * scale).astype(bf16)
        gq_ref[s] = lanes(gq)
        gq32 = gq.astype(f32)
        back = (gq32 * cos4 - pltpu.roll(gq32, HEAD_DIM // 2, 1) * sin4).astype(bf16)
        backs.append(lanes(back))
        gv = mm(weights[:, :span], g, 0, 0).astype(bf16)
        gvs.append(gv)
        for k in range(shards):
            gv_refs[k][s] = gv[k * tokens : (k + 1) * tokens]
    back = jnp.concatenate(backs, axis=0)
    gv = jnp.concatenate(gvs, axis=0)
    low_grad_q = mm(back, upq, 1, 1)
    low_grad_v = mm(gv, upv, 1, 1)
    for s in every:
        lgq_ref[s] += low_grad_q[s * tokens : (s + 1) * tokens]
        lgv_ref[s] += low_grad_v[s * span : (s + 1) * span]
    grad_up_q = mm(low_q, back, 0, 0)
    grad_up_v = mm(low_v, gv, 0, 0)
    grad_up_q, grad_up_v = grad_up_q.astype(bf16), grad_up_v.astype(bf16)
    for p in range(parts):
        rows = slice(p * part_rows, (p + 1) * part_rows)
        for h in range(GROUP):
            guq_ref[h, p] = grad_up_q[rows, h * HEAD_DIM : (h + 1) * HEAD_DIM]
        guv_ref[0, p] = grad_up_v[rows]


def attention_chunk(
    first, last, place, query_base, grad_out, up_blocks, past, cos, sin, lows, kvs, earlier
):
    shards = len(kvs)
    parts = lax.axis_size("rep")
    seqs, tokens = query_base.shape[:2]
    past_len = past.shape[1]
    groups = last - first

    def whole(x):
        return pl.BlockSpec(x.shape, lambda g: (0,) * len(x.shape))

    spec = pl.BlockSpec
    q_spec = spec((seqs, tokens, WIDE), lambda g: (0, 0, first + g))
    gv_spec = spec((seqs, tokens, HEAD_DIM), lambda g: (0, 0, g))
    past_block = (seqs, past_len, HEAD_DIM)
    in_specs = [
        spec(memory_space=pltpu.SMEM),
        spec(memory_space=pltpu.HBM),
        spec(memory_space=pltpu.HBM),
        spec((GROUP, RANK, HEAD_DIM), lambda g: (first + g, 0, 0)),
        spec((1, RANK, HEAD_DIM), lambda g: (HEADS + first + g, 0, 0)),
        spec(past_block, lambda g: (0, 0, first + g)),
        spec(past_block, lambda g: (0, 0, KV_HEADS + first + g)),
        whole(cos),
        whole(sin),
    ]
    in_specs += [whole(x) for x in lows]
    in_specs += [spec((seqs, tokens, HEAD_DIM), lambda g: (0, 0, g))] * shards
    in_specs += [spec((seqs, tokens, HEAD_DIM), lambda g: (0, 0, groups + g))] * shards
    operands = [place, query_base, grad_out, up_blocks, up_blocks, past, past, cos, sin]
    operands += list(lows) + list(kvs) + list(kvs)
    shape = jax.ShapeDtypeStruct
    low_q_shape = shape((seqs, tokens, RANK), f32)
    low_v_shape = shape((seqs, shards * tokens, RANK), f32)
    placed_shapes = [
        shape(query_base.shape, bf16),
        shape(query_base.shape, bf16),
        shape((HEADS, parts, RANK // parts, HEAD_DIM), bf16),
        shape((KV_HEADS, parts, RANK // parts, HEAD_DIM), bf16),
    ]
    placed_specs = [
        q_spec,
        q_spec,
        spec((GROUP, parts, RANK // parts, HEAD_DIM), lambda g: (first + g, 0, 0, 0)),
        spec((1, parts, RANK // parts, HEAD_DIM), lambda g: (first + g, 0, 0, 0)),
    ]
    aliases = {}
    placed = len(placed_shapes)
    if earlier is not None:
        in_specs += [whole(low_q_shape), whole(low_v_shape)]
        operands += list(earlier[placed : placed + 2])
        aliases = {len(operands) + i: i for i in range(placed)}
        in_specs += [spec(memory_space=pl.ANY)] * placed
        operands += list(earlier[:placed])
    scores = GROUP * tokens * (shards * tokens + past_len)
    pairs = seqs * groups * scores
    grant = min(12 * 2**20 + 96 * scores, 48 * 2**20)
    return pl.pallas_call(
        functools.partial(attention_kernel, shards, placed if earlier else 0, first),
        grid=(groups,),
        in_specs=in_specs,
        out_specs=placed_specs + [whole(low_q_shape), whole(low_v_shape)] + [gv_spec] * shards,
        out_shape=placed_shapes
        + [low_q_shape, low_v_shape]
        + [shape((seqs, tokens, groups * HEAD_DIM), bf16)] * shards,
        scratch_shapes=[
            pltpu.VMEM((2, seqs, tokens, WIDE), bf16),
            pltpu.VMEM((2, seqs, tokens, WIDE), bf16),
            pltpu.SemaphoreType.DMA((2, 2)),
        ],
        input_output_aliases=aliases,
        compiler_params=pltpu.CompilerParams(vmem_limit_bytes=grant),
        cost_estimate=pl.CostEstimate(
            flops=pairs * HEAD_DIM * 28, bytes_accessed=16 * 1024 * 1024, transcendentals=pairs
        ),
        name="attention",
    )(*operands)


def low_rank_kernel(
    sp, fs, rp, index_ref, own_ref, other_ref, hidden_ref, down_out, up_ref, low_ref, down_ref, sem
):
    z, x, r = index_ref[0], index_ref[1], index_ref[2]
    shards = sp * fs
    down_rows, up_rows = D // (shards * rp), RANK // rp
    blocks = (HEADS + KV_HEADS) // shards
    for piece in range(own_ref.shape[0]):
        shard = (z ^ (piece % sp)) * fs + (x ^ (piece // sp % fs))
        for swap, ref in enumerate((own_ref, other_ref)):
            part = r ^ (piece // shards * 2 + swap)
            at = pl.multiple_of((shard * rp + part) * down_rows, down_rows)
            down_ref[pl.ds(at, down_rows), :] = ref[piece, :down_rows]
            at = pl.multiple_of(part * up_rows, up_rows)
            for j in range(blocks):
                lo = down_rows + j * up_rows
                up_ref[shard * blocks + j, pl.ds(at, up_rows), :] = ref[piece, lo : lo + up_rows]
    copy = pltpu.make_async_copy(down_ref, down_out, sem)
    copy.start()
    rows = jnp.concatenate([hidden_ref[s] for s in range(hidden_ref.shape[0])], axis=0)
    low = mm(rows, down_ref[...], 1, 0).astype(bf16)
    for s in range(low_ref.shape[0]):
        low_ref[s] = low[s * low_ref.shape[1] : (s + 1) * low_ref.shape[1]]
    copy.wait()


def pack_adapters(adapter_down, adapter_up, own_past):
    sp, rp, r = lax.axis_size("sp"), lax.axis_size("rep"), lax.axis_index("rep")
    down_rows, up_rows = adapter_down.shape[0] // rp, RANK // rp
    blocks = adapter_up.shape[1] // HEAD_DIM
    down = lax.dynamic_slice_in_dim(adapter_down, r * down_rows, down_rows, 0)
    up = lax.dynamic_slice_in_dim(adapter_up, r * up_rows, up_rows, 0)
    up = [up[:, j * HEAD_DIM : (j + 1) * HEAD_DIM] for j in range(blocks)]
    rows = down_rows + blocks * up_rows
    buf = jnp.concatenate([down] + up + [own_past.reshape(-1, 2 * RANK)], axis=0)[None]
    step = 1
    while step < sp:
        buf = jnp.concatenate([buf, partner(buf, "sp", step)], axis=0)
        step *= 2
    seqs, each = own_past.shape[:2]
    past = buf[:, rows:].reshape(sp, seqs, each, -1).swapaxes(0, 1).reshape(seqs, sp * each, -1)
    return buf[:, :rows], past


def adapters_packed(hidden, buf, before_rep, before_swap):
    sp, fs, rp = (lax.axis_size(a) for a in ("sp", "fsdp", "rep"))
    z, x, r = (lax.axis_index(a) for a in ("sp", "fsdp", "rep"))
    step = 1
    while step < fs:
        buf = jnp.concatenate([buf, partner(buf, "fsdp", step)], axis=0)
        step *= 2
    step = 2
    buf = tie(buf, before_rep)
    while step < rp:
        buf = jnp.concatenate([buf, partner(buf, "rep", step)], axis=0)
        step *= 2
    other = partner(tie(buf, before_swap), "rep", 1)
    index = jnp.stack([z, x, r]).astype(jnp.int32)
    vmem = pl.BlockSpec(memory_space=pltpu.VMEM)
    seqs, tokens = hidden.shape[:2]
    down_full, up_blocks, low = pl.pallas_call(
        functools.partial(low_rank_kernel, sp, fs, rp),
        in_specs=[pl.BlockSpec(memory_space=pltpu.SMEM)] + [vmem] * 3,
        out_specs=[pl.BlockSpec(memory_space=pltpu.HBM), vmem, vmem],
        scratch_shapes=[pltpu.VMEM((D, 2 * RANK), bf16), pltpu.SemaphoreType.DMA],
        out_shape=[
            jax.ShapeDtypeStruct((D, 2 * RANK), bf16),
            jax.ShapeDtypeStruct((HEADS + KV_HEADS, RANK, HEAD_DIM), bf16),
            jax.ShapeDtypeStruct((seqs, tokens, 2 * RANK), bf16),
        ],
        compiler_params=pltpu.CompilerParams(vmem_limit_bytes=16 * 1024 * 1024),
        cost_estimate=pl.CostEstimate(
            flops=2 * seqs * tokens * D * 2 * RANK, bytes_accessed=5 * 2**20, transcendentals=0
        ),
        name="low_rank",
    )(index, buf, other, hidden)
    return down_full, up_blocks, low


def adapters_plain(hidden, adapter_down, adapter_up):
    seqs, tokens = hidden.shape[:2]
    down_full = lax.all_gather(adapter_down, ("sp", "fsdp"), axis=0, tiled=True)
    up_full = lax.all_gather(adapter_up, ("sp", "fsdp"), axis=1, tiled=True)
    rows = hidden.reshape(seqs * tokens, D)
    low = jnp.dot(rows, down_full, preferred_element_type=f32).astype(bf16)
    up_blocks = up_full.reshape(RANK, HEADS + KV_HEADS, HEAD_DIM).swapaxes(0, 1)
    return down_full, up_blocks, low.reshape(seqs, tokens, 2 * RANK)


def grad_hidden_kernel(low_ref, down_ref, out_ref):
    out = mm(low_ref[...], down_ref[...], 1, 1).astype(bf16)
    tokens = out_ref.shape[1]
    for s in range(out_ref.shape[0]):
        out_ref[s] = out[s * tokens : (s + 1) * tokens]


def grad_hidden_of(low_grad, down_full, seqs, tokens):
    columns = 1024
    return pl.pallas_call(
        grad_hidden_kernel,
        grid=(D // columns,),
        in_specs=[
            pl.BlockSpec(low_grad.shape, lambda i: (0, 0)),
            pl.BlockSpec((columns, 2 * RANK), lambda i: (i, 0)),
        ],
        out_specs=pl.BlockSpec((seqs, tokens, columns), lambda i: (0, 0, i)),
        out_shape=jax.ShapeDtypeStruct((seqs, tokens, D), bf16),
        compiler_params=pltpu.CompilerParams(vmem_limit_bytes=16 * 1024 * 1024),
        cost_estimate=pl.CostEstimate(
            flops=2 * seqs * tokens * D * 2 * RANK, bytes_accessed=2**21, transcendentals=0
        ),
        name="grad_hidden",
    )(low_grad, down_full)


def adapter_grads_kernel(core_ref, hidden_ref, low_ref, guq_ref, guv_ref, send_ref, keep_ref, gd_ref):
    c = core_ref[0]
    shards, pairs = send_ref.shape[:2]
    down_rows = gd_ref.shape[1]
    columns = 2 * pairs * down_rows
    blocks = (HEADS + KV_HEADS) // shards
    up_rows = guq_ref.shape[2]
    low = low_ref[...]
    for b in range(shards):
        cols = [hidden_ref[s, :, b * columns : (b + 1) * columns] for s in range(hidden_ref.shape[0])]
        part = mm(jnp.concatenate(cols, axis=0), low, 0, 0).astype(bf16)
        for q in range(2 * pairs):
            gd_ref[q] = part[q * down_rows : (q + 1) * down_rows]
        for hi in range(pairs):
            for ref, q in ((send_ref, 2 * hi + 1 - c), (keep_ref, 2 * hi + c)):
                ref[b, hi, :down_rows] = gd_ref[q]
                for j in range(blocks):
                    block = b * blocks + j
                    src = guq_ref[block, q] if block < HEADS else guv_ref[block - HEADS, q]
                    lo = down_rows + j * up_rows
                    ref[b, hi, lo : lo + up_rows] = src


def packed_grads(hidden, low_grad, guq, guv, shards):
    rp, r = lax.axis_size("rep"), lax.axis_index("rep")
    c = lax.rem(r, 2)
    down_rows, up_rows = D // (shards * rp), RANK // rp
    up_width = (D + KV) // shards
    rows = down_rows + up_rows * up_width // (2 * RANK)
    if up_width % HEAD_DIM == 0:
        vmem = pl.BlockSpec(memory_space=pltpu.VMEM)
        packed = jax.ShapeDtypeStruct((shards, rp // 2, rows, 2 * RANK), bf16)
        return pl.pallas_call(
            adapter_grads_kernel,
            in_specs=[pl.BlockSpec(memory_space=pltpu.SMEM)] + [vmem] * 4,
            out_specs=[vmem] * 2,
            out_shape=[packed] * 2,
            scratch_shapes=[pltpu.VMEM((rp, down_rows, 2 * RANK), bf16)],
            compiler_params=pltpu.CompilerParams(vmem_limit_bytes=16 * 1024 * 1024),
            cost_estimate=pl.CostEstimate(
                flops=2 * hidden.size * 2 * RANK, bytes_accessed=5 * 2**20, transcendentals=0
            ),
            name="adapter_grads",
        )(c.astype(jnp.int32).reshape(1), hidden, low_grad, guq, guv)
    own_rows = hidden.reshape(-1, D)
    down = jnp.dot(own_rows.T, low_grad, preferred_element_type=f32).astype(bf16)
    down = down.reshape(shards, rp, down_rows, 2 * RANK)
    up = jnp.concatenate([guq, guv], axis=0).transpose(1, 2, 0, 3)
    up = up.reshape(rp, up_rows, shards, up_width).transpose(2, 0, 1, 3)
    up = up.reshape(shards, rp, -1, 2 * RANK)
    both = jnp.concatenate([down, up], axis=2).reshape(shards, rp // 2, 2, rows, 2 * RANK)
    send = lax.dynamic_index_in_dim(both, 1 - c, 2, keepdims=False)
    keep = lax.dynamic_index_in_dim(both, c, 2, keepdims=False)
    return send, keep


def finish_grads(send, keep, before, values, low_grad, hidden_of):
    sp, fs, rp = (lax.axis_size(a) for a in ("sp", "fsdp", "rep"))
    z, r = lax.axis_index("sp"), lax.axis_index("rep")
    shards, _, rows, lanes = send.shape
    got = partner(tie(send, *before), "rep", 1)
    then = [along(tie(v, got), "sp", -k) for k, v in enumerate(values, 1)]
    fs_bits, rep_bits = fs.bit_length() - 1, rp.bit_length() - 2
    labels = [("fsdp", b) for b in reversed(range(fs_bits))]
    labels += [("rep", b + 1) for b in reversed(range(rep_bits))]
    shape = (sp,) + (2,) * len(labels) + (rows, lanes)
    terms = [a.reshape(shape) for a in (keep, got)]

    def halve(terms, order, before):
        left = list(labels)
        for step, label in enumerate(order):
            axis, bit = label
            dim = 1 + left.index(label)
            left.remove(label)
            mine = lax.rem(lax.div(lax.axis_index(axis), 1 << bit), 2)

            def pick(i):
                parts = [lax.dynamic_index_in_dim(a, i, dim, keepdims=False) for a in terms]
                return sum(a.astype(f32) for a in parts).astype(bf16)

            send = pick(1 - mine)
            if step == 1:
                send = tie(send, *before)
            terms = [pick(mine), partner(send, axis, 1 << bit)]
        return sum(a.astype(f32) for a in terms).astype(bf16)

    cut = rows // 32 * 16
    first_rep, first_fsdp = labels[::-1], labels
    over_sp = halve([a[..., cut:, :] for a in terms], first_rep, then[:1])
    if cut:
        other = halve([a[..., :cut, :] for a in terms], first_fsdp, ())
        over_sp = jnp.concatenate([other, over_sp], axis=1)
    over_sp = tie(over_sp, *then)
    total = lax.dynamic_index_in_dim(over_sp, z, 0, keepdims=False).astype(f32)
    for k in range(1, sp):
        send = lax.dynamic_index_in_dim(over_sp, lax.rem(z + k, sp), 0, keepdims=False)
        total = total + cyclic(send, "sp", k).astype(f32)
    grad_hidden = hidden_of(tie(low_grad, over_sp))
    own = tie(total.astype(bf16), grad_hidden)
    parts = [own] + [partner(own, "rep", m) for m in range(1, rp)]
    ordered = []
    for q in range(rp):
        pick = parts[0]
        for m in range(1, rp):
            pick = jnp.where((r ^ m) == q, parts[m], pick)
        ordered.append(pick.astype(f32))
    down_rows, up_rows = D // (shards * rp), RANK // rp
    up_width = (D + KV) // shards
    grad_down = jnp.concatenate([p[:down_rows] for p in ordered], axis=0)
    ups = []
    for p in ordered:
        up = p[down_rows:]
        if up_width % HEAD_DIM == 0:
            up = [up[lo : lo + up_rows] for lo in range(0, up.shape[0], up_rows)]
            up = jnp.concatenate(up, axis=1)
        ups.append(up.reshape(up_rows, up_width))
    return grad_down, jnp.concatenate(ups, axis=0), then, grad_hidden


def body(
    hidden,
    query_base,
    key_span,
    value_base,
    past_keys,
    past_values,
    grad_out,
    adapter_down,
    adapter_up,
):
    sp, fs = lax.axis_size("sp"), lax.axis_size("fsdp")
    z = lax.axis_index("sp")
    seqs, tokens = hidden.shape[:2]
    past_len = past_keys.shape[1] * sp
    own_past = jnp.concatenate([past_keys, past_values], axis=2)
    own_kvs = []
    for first, last in CHUNKS:
        cols = slice(first * HEAD_DIM, last * HEAD_DIM)
        own_kvs.append(jnp.concatenate([key_span[:, :, cols], value_base[:, :, cols]], axis=2))
    early = [own_kvs[0]]
    even = adapter_up.shape[1] % HEAD_DIM == 0
    if even:
        buf, past = pack_adapters(adapter_down, adapter_up, own_past)
    else:
        buf = own_past
        past = [own_past] + [cyclic(own_past, "sp", k) for k in range(1, sp)]
        past = jnp.concatenate(past, axis=1)
    early.append(along(tie(early[0], buf), "sp", 1))
    for k in range(2, sp):
        early.append(along(early[k - 1], "sp", 1, k - 1))
    if even:
        down_full, up_blocks, low_own = adapters_packed(hidden, buf, early[1], early[min(2, sp - 1)])
    else:
        down_full, up_blocks, low_own = adapters_plain(hidden, adapter_down, adapter_up)
    lows = [low_own] + [along(low_own, "sp", k) for k in range(1, sp)]
    own_late = tie(own_kvs[1], low_own, early[-1])
    late = [own_kvs[1]] + [along(own_late, "sp", k) for k in range(1, sp)]
    cos, sin = rotary_tables(tokens, past_len + z * tokens)
    place = z.astype(jnp.int32).reshape(1)

    made = None
    value_own, value_got = [], []
    for (first, last), kvs in zip(CHUNKS, (early, late)):
        made = attention_chunk(
            first, last, place, query_base, grad_out, up_blocks, past, cos, sin, lows, kvs, made
        )
        gvs = made[6:]
        value_own.append(gvs[0])
        if last < KV_HEADS:
            value_got.append([along(gvs[k], "sp", -k) for k in range(1, sp)])
    attended, grad_query, guq, guv, low_grad_q, low_grad_v = made[:6]

    low_v_total = low_grad_v[:, :tokens]
    for k in range(1, sp):
        part = low_grad_v[:, k * tokens : (k + 1) * tokens].astype(bf16)
        part = tie(part, value_got[0][0], value_got[0][-1])
        low_v_total = low_v_total + along(part, "sp", -k).astype(f32)
    low_grad = (
        jnp.concatenate([low_grad_q, low_v_total], axis=2)
        .astype(bf16)
        .reshape(seqs * tokens, 2 * RANK)
    )
    send, keep = packed_grads(hidden, low_grad, guq, guv, sp * fs)
    grad_down, grad_up, got, grad_hidden = finish_grads(
        send, keep, value_got[0], gvs[1:], low_grad, lambda x: grad_hidden_of(x, down_full, seqs, tokens)
    )
    value_got.append(got)

    sums = []
    for own, got in zip(value_own, value_got):
        total = own.astype(f32)
        for part in got:
            total = total + part.astype(f32)
        sums.append(total.astype(bf16))
    grad_value = jnp.concatenate(sums, axis=2)
    return (
        attended,
        grad_query,
        grad_value,
        grad_hidden,
        grad_down,
        grad_up,
    )


def solution(mesh):
    rows = P(("fsdp", "rep"), "sp", None)
    down, up = P(("sp", "fsdp"), None), P(None, ("sp", "fsdp"))
    return jax.shard_map(
        body,
        mesh=mesh,
        in_specs=(rows,) * 7 + (down, up),
        out_specs=(rows,) * 4 + (down, up),
        check_vma=False,
    )
```

```python
import functools
import math

import jax
import jax.numpy as jnp
from jax import lax
from jax.experimental import pallas as pl
from jax.experimental.pallas import tpu as pltpu
from jax.sharding import PartitionSpec as P

D = 4096
HEADS = 32
KV_HEADS = 8
HEAD_DIM = 128
RANK = 64
KV = 1024
GROUP = HEADS // KV_HEADS
WIDE = GROUP * HEAD_DIM
ROPE_BASE = 500000.0
HIDDEN_MASK = -1e30
LOG2_E = 1.4426950408889634

f32 = jnp.float32
bf16 = jnp.bfloat16


def rotary_tables(row_count, offset):
    half = HEAD_DIM // 2
    position = (jnp.arange(row_count, dtype=jnp.int32) + offset).astype(f32)
    inverse = jnp.exp(jnp.arange(half, dtype=f32) * (-2.0 * math.log(ROPE_BASE) / HEAD_DIM))
    angle = position[:, None] * inverse[None, :]
    cosine, sine = jnp.cos(angle), jnp.sin(angle)
    return (
        jnp.concatenate([cosine, cosine], axis=1),
        jnp.concatenate([-sine, sine], axis=1),
    )


def cyclic(x, axis, shift):
    n = lax.axis_size(axis)
    return lax.ppermute(x, axis, [(i, (i + shift) % n) for i in range(n)])


def along(x, axis, shift, start=0):
    n = lax.axis_size(axis)
    return lax.ppermute(x, axis, [(i, i + shift) for i in range(start, n) if 0 <= i + shift < n])


def partner(x, axis, mask):
    n = lax.axis_size(axis)
    return lax.ppermute(x, axis, [(i, i ^ mask) for i in range(n)])


def tie(x, *others):
    return lax.optimization_barrier((x,) + others)[0]


def mm(a, b, ca, cb):
    return lax.dot_general(a, b, (((ca,), (cb,)), ((), ())), preferred_element_type=f32)


def attention_kernel(shards, place_ref, *refs):
    it = iter(refs)

    def take(n):
        return [next(it) for _ in range(n)]

    q_hbm, g_hbm, upq_ref, upv_ref, pk_ref, pv_ref, cos_ref, sin_ref = take(8)
    low_refs, k_refs, v_refs = take(shards), take(shards), take(shards)
    att_ref, gq_ref, guq_ref, guv_ref, lgq_ref, lgv_ref = take(6)
    gv_refs = take(shards)
    q_buf, g_buf, sems = take(3)

    group, slot = pl.program_id(0), lax.rem(pl.program_id(0), 2)

    def fetches(step, into):
        at = pl.multiple_of(step * WIDE, WIDE)
        return [
            pltpu.make_async_copy(hbm.at[:, :, pl.ds(at, WIDE)], buf.at[into], sems.at[i, into])
            for i, (hbm, buf) in enumerate(((q_hbm, q_buf), (g_hbm, g_buf)))
        ]

    @pl.when(group == 0)
    def _():
        for copy in fetches(0, 0):
            copy.start()

    @pl.when(group + 1 < pl.num_programs(0))
    def _():
        for copy in fetches(group + 1, 1 - slot):
            copy.start()

    seqs, tokens = q_buf.shape[1:3]
    parts, part_rows = guq_ref.shape[1:3]
    span = shards * tokens
    past = pk_ref.shape[1]
    scale = 1.0 / math.sqrt(HEAD_DIM)
    place = place_ref[0]
    cos, sin = cos_ref[...], sin_ref[...]
    upq = jnp.concatenate([upq_ref[h] for h in range(GROUP)], axis=1)
    upv = upv_ref[0]

    @pl.when(pl.program_id(0) == 0)
    def _():
        lgq_ref[...] = jnp.zeros_like(lgq_ref)
        lgv_ref[...] = jnp.zeros_like(lgv_ref)

    col = lax.broadcasted_iota(jnp.int32, (tokens, span + past), 1)
    row = lax.broadcasted_iota(jnp.int32, (tokens, span + past), 0)
    seen = (col <= row) | ((col >= tokens) & (col < (place + 1) * tokens)) | (col >= span)
    bias = jnp.where(seen, 0.0, HIDDEN_MASK)
    bias = jnp.concatenate([bias] * GROUP, axis=0)

    def heads(x):
        return jnp.concatenate(
            [x[:, h * HEAD_DIM : (h + 1) * HEAD_DIM] for h in range(GROUP)], axis=0
        )

    def lanes(x):
        return jnp.concatenate([x[h * tokens : (h + 1) * tokens] for h in range(GROUP)], axis=1)

    cos4 = jnp.concatenate([cos] * GROUP, axis=0)
    sin4 = jnp.concatenate([sin] * GROUP, axis=0)
    every = range(seqs)
    low_q = jnp.concatenate([low_refs[0][s][:, :RANK] for s in every], axis=0)
    low_v = jnp.concatenate([r[s][:, RANK:] for s in every for r in low_refs], axis=0)
    query_delta = mm(low_q, upq, 1, 0)
    value_delta = mm(low_v, upv, 1, 0)
    for copy in fetches(group, slot):
        copy.wait()
    backs, gvs = [], []
    for s in every:
        delta = heads(query_delta[s * tokens : (s + 1) * tokens])
        delta = delta * cos4 + pltpu.roll(delta, HEAD_DIM // 2, 1) * sin4
        q = (heads(q_buf[slot, s]).astype(f32) + delta).astype(bf16)
        g = heads(g_buf[slot, s])
        keys = jnp.concatenate([r[s] for r in k_refs] + [pk_ref[s]], axis=0)
        base = jnp.concatenate([r[s] for r in v_refs], axis=0).astype(f32)
        vals = (base + value_delta[s * span : (s + 1) * span]).astype(bf16)
        vals = jnp.concatenate([vals, pv_ref[s]], axis=0)

        scores = mm(q, keys, 1, 1) * (scale * LOG2_E) + bias
        top = jnp.max(scores, axis=-1, keepdims=True)
        e = jnp.exp2(scores - top)
        inverse = 1.0 / jnp.sum(e, axis=-1, keepdims=True)
        weights = e.astype(bf16)
        out = (mm(weights, vals, 1, 0) * inverse).astype(bf16)
        att_ref[s] = lanes(out)
        g = (g.astype(f32) * inverse).astype(bf16)
        prob_grad = mm(g, vals, 1, 1)
        row_delta = jnp.sum(g.astype(f32) * out.astype(f32), axis=-1, keepdims=True)
        score_grad = (e * (prob_grad - row_delta)).astype(bf16)
        gq = (mm(score_grad, keys, 1, 0) * scale).astype(bf16)
        gq_ref[s] = lanes(gq)
        gq32 = gq.astype(f32)
        back = (gq32 * cos4 - pltpu.roll(gq32, HEAD_DIM // 2, 1) * sin4).astype(bf16)
        backs.append(lanes(back))
        gv = mm(weights[:, :span], g, 0, 0).astype(bf16)
        gvs.append(gv)
        for k in range(shards):
            gv_refs[k][s] = gv[k * tokens : (k + 1) * tokens]
    back = jnp.concatenate(backs, axis=0)
    gv = jnp.concatenate(gvs, axis=0)
    low_grad_q = mm(back, upq, 1, 1)
    low_grad_v = mm(gv, upv, 1, 1)
    for s in every:
        lgq_ref[s] += low_grad_q[s * tokens : (s + 1) * tokens]
        lgv_ref[s] += low_grad_v[s * span : (s + 1) * span]
    grad_up_q = mm(low_q, back, 0, 0)
    grad_up_v = mm(low_v, gv, 0, 0)
    grad_up_q, grad_up_v = grad_up_q.astype(bf16), grad_up_v.astype(bf16)
    for p in range(parts):
        rows = slice(p * part_rows, (p + 1) * part_rows)
        for h in range(GROUP):
            guq_ref[h, p] = grad_up_q[rows, h * HEAD_DIM : (h + 1) * HEAD_DIM]
        guv_ref[0, p] = grad_up_v[rows]


def attention(place, query_base, grad_out, up_blocks, past, cos, sin, lows, kvs):
    shards = len(kvs)
    parts = lax.axis_size("rep")
    seqs, tokens = query_base.shape[:2]
    past_len = past.shape[1]

    def whole(x):
        return pl.BlockSpec(x.shape, lambda g: (0,) * len(x.shape))

    spec = pl.BlockSpec
    q_spec = spec((seqs, tokens, WIDE), lambda g: (0, 0, g))
    gv_spec = spec((seqs, tokens, HEAD_DIM), lambda g: (0, 0, g))
    past_block = (seqs, past_len, HEAD_DIM)
    in_specs = [
        spec(memory_space=pltpu.SMEM),
        spec(memory_space=pltpu.HBM),
        spec(memory_space=pltpu.HBM),
        spec((GROUP, RANK, HEAD_DIM), lambda g: (g, 0, 0)),
        spec((1, RANK, HEAD_DIM), lambda g: (HEADS + g, 0, 0)),
        spec(past_block, lambda g: (0, 0, g)),
        spec(past_block, lambda g: (0, 0, KV_HEADS + g)),
        whole(cos),
        whole(sin),
    ]
    in_specs += [whole(x) for x in lows]
    in_specs += [gv_spec] * shards
    in_specs += [spec((seqs, tokens, HEAD_DIM), lambda g: (0, 0, KV_HEADS + g))] * shards
    shape = jax.ShapeDtypeStruct
    low_q_shape = shape((seqs, tokens, RANK), f32)
    low_v_shape = shape((seqs, shards * tokens, RANK), f32)
    part_rows = RANK // parts
    scores = GROUP * tokens * (shards * tokens + past_len)
    pairs = seqs * KV_HEADS * scores
    return pl.pallas_call(
        functools.partial(attention_kernel, shards),
        grid=(KV_HEADS,),
        in_specs=in_specs,
        out_specs=[
            q_spec,
            q_spec,
            spec((GROUP, parts, part_rows, HEAD_DIM), lambda g: (g, 0, 0, 0)),
            spec((1, parts, part_rows, HEAD_DIM), lambda g: (g, 0, 0, 0)),
            whole(low_q_shape),
            whole(low_v_shape),
        ]
        + [gv_spec] * shards,
        out_shape=[
            shape(query_base.shape, bf16),
            shape(query_base.shape, bf16),
            shape((HEADS, parts, part_rows, HEAD_DIM), bf16),
            shape((KV_HEADS, parts, part_rows, HEAD_DIM), bf16),
            low_q_shape,
            low_v_shape,
        ]
        + [shape((seqs, tokens, KV), bf16)] * shards,
        scratch_shapes=[
            pltpu.VMEM((2, seqs, tokens, WIDE), bf16),
            pltpu.VMEM((2, seqs, tokens, WIDE), bf16),
            pltpu.SemaphoreType.DMA((2, 2)),
        ],
        compiler_params=pltpu.CompilerParams(
            vmem_limit_bytes=min(8 * 2**20 + 96 * scores, 48 * 2**20)
        ),
        cost_estimate=pl.CostEstimate(
            flops=pairs * HEAD_DIM * 120, bytes_accessed=2**16, transcendentals=pairs
        ),
        name="attention",
    )(place, query_base, grad_out, up_blocks, up_blocks, past, past, cos, sin, *lows, *kvs, *kvs)


def low_rank_kernel(
    sp, fs, rp, index_ref, own_ref, other_ref, hidden_ref, down_out, up_ref, low_ref, down_ref, sem
):
    z, x, r = index_ref[0], index_ref[1], index_ref[2]
    shards = sp * fs
    down_rows, up_rows = D // (shards * rp), RANK // rp
    blocks = (HEADS + KV_HEADS) // shards
    for piece in range(own_ref.shape[0]):
        shard = (z ^ (piece % sp)) * fs + (x ^ (piece // sp % fs))
        for swap, ref in enumerate((own_ref, other_ref)):
            part = r ^ (piece // shards * 2 + swap)
            at = pl.multiple_of((shard * rp + part) * down_rows, down_rows)
            down_ref[pl.ds(at, down_rows), :] = ref[piece, :down_rows]
            at = pl.multiple_of(part * up_rows, up_rows)
            for j in range(blocks):
                lo = down_rows + j * up_rows
                up_ref[shard * blocks + j, pl.ds(at, up_rows), :] = ref[piece, lo : lo + up_rows]
    copy = pltpu.make_async_copy(down_ref, down_out, sem)
    copy.start()
    rows = jnp.concatenate([hidden_ref[s] for s in range(hidden_ref.shape[0])], axis=0)
    low = mm(rows, down_ref[...], 1, 0).astype(bf16)
    for s in range(low_ref.shape[0]):
        low_ref[s] = low[s * low_ref.shape[1] : (s + 1) * low_ref.shape[1]]
    copy.wait()


def pack_kernel(rp, part_ref, down_ref, up_ref, past_ref, out_ref):
    r = part_ref[0]
    down_rows, up_rows = down_ref.shape[0] // rp, RANK // rp
    out_ref[0, :down_rows] = down_ref[pl.ds(pl.multiple_of(r * down_rows, down_rows), down_rows)]
    at = pl.multiple_of(r * up_rows, up_rows)
    lo = down_rows
    for j in range(up_ref.shape[1] // HEAD_DIM):
        cols = slice(j * HEAD_DIM, (j + 1) * HEAD_DIM)
        out_ref[0, lo : lo + up_rows] = up_ref[pl.ds(at, up_rows), cols]
        lo += up_rows
    out_ref[0, lo:] = past_ref[...]


def pack_adapters(adapter_down, adapter_up, own_past):
    sp, rp, r = lax.axis_size("sp"), lax.axis_size("rep"), lax.axis_index("rep")
    down_rows, up_rows = adapter_down.shape[0] // rp, RANK // rp
    blocks = adapter_up.shape[1] // HEAD_DIM
    rows = down_rows + adapter_up.shape[1] // HEAD_DIM * up_rows
    packed_past = own_past.reshape(-1, 2 * RANK)
    vmem = pl.BlockSpec(memory_space=pltpu.VMEM)
    buf = pl.pallas_call(
        functools.partial(pack_kernel, rp),
        in_specs=[pl.BlockSpec(memory_space=pltpu.SMEM)] + [vmem] * 3,
        out_specs=vmem,
        out_shape=jax.ShapeDtypeStruct((1, rows + packed_past.shape[0], 2 * RANK), bf16),
        compiler_params=pltpu.CompilerParams(vmem_limit_bytes=8 * 1024 * 1024),
        cost_estimate=pl.CostEstimate(flops=0, bytes_accessed=2**19, transcendentals=0),
        name="pack",
    )(r.astype(jnp.int32).reshape(1), adapter_down, adapter_up, packed_past)
    step = 1
    while step < sp:
        buf = jnp.concatenate([buf, partner(buf, "sp", step)], axis=0)
        step *= 2
    seqs, each = own_past.shape[:2]
    past = buf[:, rows:].reshape(sp, seqs, each, -1).swapaxes(0, 1).reshape(seqs, sp * each, -1)
    return buf[:, :rows], past


def adapters_packed(hidden, buf, before_rep, before_swap):
    sp, fs, rp = (lax.axis_size(a) for a in ("sp", "fsdp", "rep"))
    z, x, r = (lax.axis_index(a) for a in ("sp", "fsdp", "rep"))
    step = 1
    while step < fs:
        buf = jnp.concatenate([buf, partner(buf, "fsdp", step)], axis=0)
        step *= 2
    step = 2
    buf = tie(buf, before_rep)
    while step < rp:
        buf = jnp.concatenate([buf, partner(buf, "rep", step)], axis=0)
        step *= 2
    other = partner(tie(buf, before_swap), "rep", 1)
    index = jnp.stack([z, x, r]).astype(jnp.int32)
    vmem = pl.BlockSpec(memory_space=pltpu.VMEM)
    seqs, tokens = hidden.shape[:2]
    down_full, up_blocks, low = pl.pallas_call(
        functools.partial(low_rank_kernel, sp, fs, rp),
        in_specs=[pl.BlockSpec(memory_space=pltpu.SMEM)] + [vmem] * 3,
        out_specs=[pl.BlockSpec(memory_space=pltpu.HBM), vmem, vmem],
        scratch_shapes=[pltpu.VMEM((D, 2 * RANK), bf16), pltpu.SemaphoreType.DMA],
        out_shape=[
            jax.ShapeDtypeStruct((D, 2 * RANK), bf16),
            jax.ShapeDtypeStruct((HEADS + KV_HEADS, RANK, HEAD_DIM), bf16),
            jax.ShapeDtypeStruct((seqs, tokens, 2 * RANK), bf16),
        ],
        compiler_params=pltpu.CompilerParams(vmem_limit_bytes=12 * 1024 * 1024),
        cost_estimate=pl.CostEstimate(
            flops=2 * seqs * tokens * D * 2 * RANK, bytes_accessed=2**16, transcendentals=0
        ),
        name="low_rank",
    )(index, buf, other, hidden)
    return down_full, up_blocks, low


def adapters_plain(hidden, adapter_down, adapter_up):
    seqs, tokens = hidden.shape[:2]
    down_full = lax.all_gather(adapter_down, ("sp", "fsdp"), axis=0, tiled=True)
    up_full = lax.all_gather(adapter_up, ("sp", "fsdp"), axis=1, tiled=True)
    rows = hidden.reshape(seqs * tokens, D)
    low = jnp.dot(rows, down_full, preferred_element_type=f32).astype(bf16)
    up_blocks = up_full.reshape(RANK, HEADS + KV_HEADS, HEAD_DIM).swapaxes(0, 1)
    return down_full, up_blocks, low.reshape(seqs, tokens, 2 * RANK)


def grad_hidden_kernel(low_ref, down_ref, out_ref):
    out = mm(low_ref[...], down_ref[...], 1, 1).astype(bf16)
    tokens = out_ref.shape[1]
    for s in range(out_ref.shape[0]):
        out_ref[s] = out[s * tokens : (s + 1) * tokens]


def grad_hidden_of(low_grad, down_full, seqs, tokens):
    columns = 1024
    return pl.pallas_call(
        grad_hidden_kernel,
        grid=(D // columns,),
        in_specs=[
            pl.BlockSpec(low_grad.shape, lambda i: (0, 0)),
            pl.BlockSpec((columns, 2 * RANK), lambda i: (i, 0)),
        ],
        out_specs=pl.BlockSpec((seqs, tokens, columns), lambda i: (0, 0, i)),
        out_shape=jax.ShapeDtypeStruct((seqs, tokens, D), bf16),
        compiler_params=pltpu.CompilerParams(vmem_limit_bytes=12 * 1024 * 1024),
        cost_estimate=pl.CostEstimate(
            flops=16 * seqs * tokens * D * 2 * RANK, bytes_accessed=2**16, transcendentals=0
        ),
        name="grad_hidden",
    )(low_grad, down_full)


def adapter_grads_kernel(core_ref, hidden_ref, low_ref, guq_ref, guv_ref, send_ref, keep_ref, gd_ref):
    c = core_ref[0]
    shards, pairs = send_ref.shape[:2]
    down_rows = gd_ref.shape[1]
    columns = 2 * pairs * down_rows
    blocks = (HEADS + KV_HEADS) // shards
    up_rows = guq_ref.shape[2]
    low = low_ref[...]
    for b in range(shards):
        cols = [hidden_ref[s, :, b * columns : (b + 1) * columns] for s in range(hidden_ref.shape[0])]
        part = mm(jnp.concatenate(cols, axis=0), low, 0, 0).astype(bf16)
        for q in range(2 * pairs):
            gd_ref[q] = part[q * down_rows : (q + 1) * down_rows]
        for hi in range(pairs):
            for ref, q in ((send_ref, 2 * hi + 1 - c), (keep_ref, 2 * hi + c)):
                ref[b, hi, :down_rows] = gd_ref[q]
                for j in range(blocks):
                    block = b * blocks + j
                    src = guq_ref[block, q] if block < HEADS else guv_ref[block - HEADS, q]
                    lo = down_rows + j * up_rows
                    ref[b, hi, lo : lo + up_rows] = src


def packed_grads(hidden, low_grad, guq, guv, shards):
    rp, r = lax.axis_size("rep"), lax.axis_index("rep")
    c = lax.rem(r, 2)
    down_rows, up_rows = D // (shards * rp), RANK // rp
    up_width = (D + KV) // shards
    rows = down_rows + up_rows * up_width // (2 * RANK)
    if up_width % HEAD_DIM == 0:
        vmem = pl.BlockSpec(memory_space=pltpu.VMEM)
        packed = jax.ShapeDtypeStruct((shards, rp // 2, rows, 2 * RANK), bf16)
        return pl.pallas_call(
            adapter_grads_kernel,
            in_specs=[pl.BlockSpec(memory_space=pltpu.SMEM)] + [vmem] * 4,
            out_specs=[vmem] * 2,
            out_shape=[packed] * 2,
            scratch_shapes=[pltpu.VMEM((rp, down_rows, 2 * RANK), bf16)],
            compiler_params=pltpu.CompilerParams(vmem_limit_bytes=12 * 1024 * 1024),
            cost_estimate=pl.CostEstimate(
                flops=2 * hidden.size * 2 * RANK, bytes_accessed=5 * 2**20, transcendentals=0
            ),
            name="adapter_grads",
        )(c.astype(jnp.int32).reshape(1), hidden, low_grad, guq, guv)
    own_rows = hidden.reshape(-1, D)
    down = jnp.dot(own_rows.T, low_grad, preferred_element_type=f32).astype(bf16)
    down = down.reshape(shards, rp, down_rows, 2 * RANK)
    up = jnp.concatenate([guq, guv], axis=0).transpose(1, 2, 0, 3)
    up = up.reshape(rp, up_rows, shards, up_width).transpose(2, 0, 1, 3)
    up = up.reshape(shards, rp, -1, 2 * RANK)
    both = jnp.concatenate([down, up], axis=2).reshape(shards, rp // 2, 2, rows, 2 * RANK)
    send = lax.dynamic_index_in_dim(both, 1 - c, 2, keepdims=False)
    keep = lax.dynamic_index_in_dim(both, c, 2, keepdims=False)
    return send, keep


def finish_grads(send, keep, values, low_grad, hidden_of):
    sp, fs, rp = (lax.axis_size(a) for a in ("sp", "fsdp", "rep"))
    z, r = lax.axis_index("sp"), lax.axis_index("rep")
    shards, _, rows, lanes = send.shape
    got = partner(tie(send, values[0]), "rep", 1)
    fs_bits, rep_bits = fs.bit_length() - 1, rp.bit_length() - 2
    labels = [("fsdp", b) for b in reversed(range(fs_bits))]
    labels += [("rep", b + 1) for b in reversed(range(rep_bits))]
    shape = (sp,) + (2,) * len(labels) + (rows, lanes)
    terms = [a.reshape(shape) for a in (keep, got)]

    def halve(terms, order):
        left = list(labels)
        for step, label in enumerate(order):
            axis, bit = label
            dim = 1 + left.index(label)
            left.remove(label)
            mine = lax.rem(lax.div(lax.axis_index(axis), 1 << bit), 2)

            def pick(i):
                parts = [lax.dynamic_index_in_dim(a, i, dim, keepdims=False) for a in terms]
                return sum(a.astype(f32) for a in parts).astype(bf16)

            send = pick(1 - mine)
            if step == 0:
                send = tie(send, *values[2:])
            terms = [pick(mine), partner(send, axis, 1 << bit)]
        return sum(a.astype(f32) for a in terms).astype(bf16)

    cut = rows // 32 * 16
    first_rep, first_fsdp = labels[::-1], labels
    over_sp = halve([a[..., cut:, :] for a in terms], first_rep)
    if cut:
        other = halve([a[..., :cut, :] for a in terms], first_fsdp)
        over_sp = jnp.concatenate([other, over_sp], axis=1)
    over_sp = tie(over_sp, *values)
    total = lax.dynamic_index_in_dim(over_sp, z, 0, keepdims=False).astype(f32)
    for k in range(1, sp):
        send = lax.dynamic_index_in_dim(over_sp, lax.rem(z + k, sp), 0, keepdims=False)
        total = total + cyclic(send, "sp", k).astype(f32)
    grad_hidden = hidden_of(tie(low_grad, over_sp))
    own = tie(total.astype(bf16), grad_hidden)
    parts = [own] + [partner(own, "rep", m) for m in range(1, rp)]
    ordered = []
    for q in range(rp):
        pick = parts[0]
        for m in range(1, rp):
            pick = jnp.where((r ^ m) == q, parts[m], pick)
        ordered.append(pick.astype(f32))
    down_rows, up_rows = D // (shards * rp), RANK // rp
    up_width = (D + KV) // shards
    grad_down = jnp.concatenate([p[:down_rows] for p in ordered], axis=0)
    ups = []
    for p in ordered:
        up = p[down_rows:]
        if up_width % HEAD_DIM == 0:
            up = [up[lo : lo + up_rows] for lo in range(0, up.shape[0], up_rows)]
            up = jnp.concatenate(up, axis=1)
        ups.append(up.reshape(up_rows, up_width))
    return grad_down, jnp.concatenate(ups, axis=0), grad_hidden


def body(
    hidden,
    query_base,
    key_span,
    value_base,
    past_keys,
    past_values,
    grad_out,
    adapter_down,
    adapter_up,
):
    sp, fs = lax.axis_size("sp"), lax.axis_size("fsdp")
    z = lax.axis_index("sp")
    seqs, tokens = hidden.shape[:2]
    past_len = past_keys.shape[1] * sp
    own_past = jnp.concatenate([past_keys, past_values], axis=2)
    kvs = [jnp.concatenate([key_span, value_base], axis=2)]
    even = adapter_up.shape[1] % HEAD_DIM == 0
    if even:
        buf, past = pack_adapters(adapter_down, adapter_up, own_past)
    else:
        buf = own_past
        past = [own_past] + [cyclic(own_past, "sp", k) for k in range(1, sp)]
        past = jnp.concatenate(past, axis=1)
    kvs.append(along(tie(kvs[0], buf), "sp", 1))
    for k in range(2, sp):
        kvs.append(along(kvs[k - 1], "sp", 1, k - 1))
    if even:
        down_full, up_blocks, low_own = adapters_packed(hidden, buf, kvs[1], kvs[min(2, sp - 1)])
    else:
        down_full, up_blocks, low_own = adapters_plain(hidden, adapter_down, adapter_up)
    lows = [low_own] + [along(low_own, "sp", k) for k in range(1, sp)]
    cos, sin = rotary_tables(tokens, past_len + z * tokens)
    place = z.astype(jnp.int32).reshape(1)

    made = attention(place, query_base, grad_out, up_blocks, past, cos, sin, lows, kvs)
    attended, grad_query, guq, guv, low_grad_q, low_grad_v = made[:6]
    value_own, value_got = made[6], [along(made[6 + k], "sp", -k) for k in range(1, sp)]

    low_v_total = low_grad_v[:, :tokens]
    for k in range(1, sp):
        part = low_grad_v[:, k * tokens : (k + 1) * tokens].astype(bf16)
        low_v_total = low_v_total + along(part, "sp", -k).astype(f32)
    low_grad = (
        jnp.concatenate([low_grad_q, low_v_total], axis=2)
        .astype(bf16)
        .reshape(seqs * tokens, 2 * RANK)
    )
    send, keep = packed_grads(hidden, low_grad, guq, guv, sp * fs)
    grad_down, grad_up, grad_hidden = finish_grads(
        send, keep, value_got, low_grad, lambda x: grad_hidden_of(x, down_full, seqs, tokens)
    )
    grad_value = value_own.astype(f32)
    for part in value_got:
        grad_value = grad_value + part.astype(f32)
    return (
        attended,
        grad_query,
        grad_value.astype(bf16),
        grad_hidden,
        grad_down,
        grad_up,
    )


def solution(mesh):
    rows = P(("fsdp", "rep"), "sp", None)
    down, up = P(("sp", "fsdp"), None), P(None, ("sp", "fsdp"))
    return jax.shard_map(
        body,
        mesh=mesh,
        in_specs=(rows,) * 7 + (down, up),
        out_specs=(rows,) * 4 + (down, up),
        check_vma=False,
    )
```

```python
import functools
import math

import jax
import jax.numpy as jnp
from jax import lax
from jax.experimental import pallas as pl
from jax.experimental.pallas import tpu as pltpu
from jax.sharding import PartitionSpec as P

D = 4096
HEADS = 32
KV_HEADS = 8
HEAD_DIM = 128
RANK = 64
KV = 1024
GROUP = HEADS // KV_HEADS
WIDE = GROUP * HEAD_DIM
ROPE_BASE = 500000.0
HIDDEN_MASK = -1e30
LOG2_E = 1.4426950408889634

f32 = jnp.float32
bf16 = jnp.bfloat16


def rotary_tables(row_count, offset):
    half = HEAD_DIM // 2
    position = (jnp.arange(row_count, dtype=jnp.int32) + offset).astype(f32)
    inverse = jnp.exp(jnp.arange(half, dtype=f32) * (-2.0 * math.log(ROPE_BASE) / HEAD_DIM))
    angle = position[:, None] * inverse[None, :]
    cosine, sine = jnp.cos(angle), jnp.sin(angle)
    return (
        jnp.concatenate([cosine, cosine], axis=1),
        jnp.concatenate([-sine, sine], axis=1),
    )


def cyclic(x, axis, shift):
    n = lax.axis_size(axis)
    return lax.ppermute(x, axis, [(i, (i + shift) % n) for i in range(n)])


def along(x, axis, shift, start=0):
    n = lax.axis_size(axis)
    return lax.ppermute(x, axis, [(i, i + shift) for i in range(start, n) if 0 <= i + shift < n])


def partner(x, axis, mask):
    n = lax.axis_size(axis)
    return lax.ppermute(x, axis, [(i, i ^ mask) for i in range(n)])


def tie(x, *others):
    return lax.optimization_barrier((x,) + others)[0]


def mm(a, b, ca, cb):
    return lax.dot_general(a, b, (((ca,), (cb,)), ((), ())), preferred_element_type=f32)


def attention_kernel(shards, place_ref, *refs):
    it = iter(refs)

    def take(n):
        return [next(it) for _ in range(n)]

    q_hbm, g_hbm, upq_ref, upv_ref, pk_ref, pv_ref, cos_ref, sin_ref = take(8)
    low_refs, k_refs, v_refs = take(shards), take(shards), take(shards)
    att_ref, gq_ref, guq_ref, guv_ref, lgq_ref, lgv_ref = take(6)
    gv_refs = take(shards)
    q_buf, g_buf, sems = take(3)

    group, slot = pl.program_id(0), lax.rem(pl.program_id(0), 2)

    def fetches(step, into):
        at = pl.multiple_of(step * WIDE, WIDE)
        return [
            pltpu.make_async_copy(hbm.at[:, :, pl.ds(at, WIDE)], buf.at[into], sems.at[i, into])
            for i, (hbm, buf) in enumerate(((q_hbm, q_buf), (g_hbm, g_buf)))
        ]

    @pl.when(group == 0)
    def _():
        for copy in fetches(0, 0):
            copy.start()

    @pl.when(group + 1 < pl.num_programs(0))
    def _():
        for copy in fetches(group + 1, 1 - slot):
            copy.start()

    seqs, tokens = q_buf.shape[1:3]
    parts, part_rows = guq_ref.shape[1:3]
    span = shards * tokens
    past = pk_ref.shape[1]
    scale = 1.0 / math.sqrt(HEAD_DIM)
    place = place_ref[0]
    cos, sin = cos_ref[...], sin_ref[...]
    upq = jnp.concatenate([upq_ref[h] for h in range(GROUP)], axis=1)
    upv = upv_ref[0]

    @pl.when(pl.program_id(0) == 0)
    def _():
        lgq_ref[...] = jnp.zeros_like(lgq_ref)
        lgv_ref[...] = jnp.zeros_like(lgv_ref)

    col = lax.broadcasted_iota(jnp.int32, (tokens, span + past), 1)
    row = lax.broadcasted_iota(jnp.int32, (tokens, span + past), 0)
    seen = (col <= row) | ((col >= tokens) & (col < (place + 1) * tokens)) | (col >= span)
    bias = jnp.where(seen, 0.0, HIDDEN_MASK)
    bias = jnp.concatenate([bias] * GROUP, axis=0)

    def heads(x):
        return jnp.concatenate(
            [x[:, h * HEAD_DIM : (h + 1) * HEAD_DIM] for h in range(GROUP)], axis=0
        )

    def lanes(x):
        return jnp.concatenate([x[h * tokens : (h + 1) * tokens] for h in range(GROUP)], axis=1)

    cos4 = jnp.concatenate([cos] * GROUP, axis=0)
    sin4 = jnp.concatenate([sin] * GROUP, axis=0)
    every = range(seqs)
    low_q = jnp.concatenate([low_refs[0][s][:, :RANK] for s in every], axis=0)
    low_v = jnp.concatenate([r[s][:, RANK:] for s in every for r in low_refs], axis=0)
    query_delta = mm(low_q, upq, 1, 0)
    value_delta = mm(low_v, upv, 1, 0)
    for copy in fetches(group, slot):
        copy.wait()
    backs, gvs = [], []
    for s in every:
        delta = heads(query_delta[s * tokens : (s + 1) * tokens])
        delta = delta * cos4 + pltpu.roll(delta, HEAD_DIM // 2, 1) * sin4
        q = (heads(q_buf[slot, s]).astype(f32) + delta).astype(bf16)
        g = heads(g_buf[slot, s])
        keys = jnp.concatenate([r[s] for r in k_refs] + [pk_ref[s]], axis=0)
        base = jnp.concatenate([r[s] for r in v_refs], axis=0).astype(f32)
        vals = (base + value_delta[s * span : (s + 1) * span]).astype(bf16)
        vals = jnp.concatenate([vals, pv_ref[s]], axis=0)

        scores = mm(q, keys, 1, 1) * (scale * LOG2_E) + bias
        top = jnp.max(scores, axis=-1, keepdims=True)
        e = jnp.exp2(scores - top)
        inverse = 1.0 / jnp.sum(e, axis=-1, keepdims=True)
        weights = e.astype(bf16)
        out = (mm(weights, vals, 1, 0) * inverse).astype(bf16)
        att_ref[s] = lanes(out)
        g = (g.astype(f32) * inverse).astype(bf16)
        prob_grad = mm(g, vals, 1, 1)
        row_delta = jnp.sum(g.astype(f32) * out.astype(f32), axis=-1, keepdims=True)
        score_grad = (e * (prob_grad - row_delta)).astype(bf16)
        gq = (mm(score_grad, keys, 1, 0) * scale).astype(bf16)
        gq_ref[s] = lanes(gq)
        gq32 = gq.astype(f32)
        back = (gq32 * cos4 - pltpu.roll(gq32, HEAD_DIM // 2, 1) * sin4).astype(bf16)
        backs.append(lanes(back))
        gv = mm(weights[:, :span], g, 0, 0).astype(bf16)
        gvs.append(gv)
        for k in range(shards):
            gv_refs[k][s] = gv[k * tokens : (k + 1) * tokens]
    back = jnp.concatenate(backs, axis=0)
    gv = jnp.concatenate(gvs, axis=0)
    low_grad_q = mm(back, upq, 1, 1)
    low_grad_v = mm(gv, upv, 1, 1)
    for s in every:
        lgq_ref[s] += low_grad_q[s * tokens : (s + 1) * tokens]
        lgv_ref[s] += low_grad_v[s * span : (s + 1) * span]
    grad_up_q = mm(low_q, back, 0, 0)
    grad_up_v = mm(low_v, gv, 0, 0)
    grad_up_q, grad_up_v = grad_up_q.astype(bf16), grad_up_v.astype(bf16)
    for p in range(parts):
        rows = slice(p * part_rows, (p + 1) * part_rows)
        for h in range(GROUP):
            guq_ref[h, p] = grad_up_q[rows, h * HEAD_DIM : (h + 1) * HEAD_DIM]
        guv_ref[0, p] = grad_up_v[rows]


def attention(place, query_base, grad_out, up_blocks, past, cos, sin, lows, keys, bases):
    shards = len(keys)
    parts = lax.axis_size("rep")
    seqs, tokens = query_base.shape[:2]
    past_len = past.shape[1]

    def whole(x):
        return pl.BlockSpec(x.shape, lambda g: (0,) * len(x.shape))

    spec = pl.BlockSpec
    q_spec = spec((seqs, tokens, WIDE), lambda g: (0, 0, g))
    gv_spec = spec((seqs, tokens, HEAD_DIM), lambda g: (0, 0, g))
    past_block = (seqs, past_len, HEAD_DIM)
    in_specs = [
        spec(memory_space=pltpu.SMEM),
        spec(memory_space=pltpu.HBM),
        spec(memory_space=pltpu.HBM),
        spec((GROUP, RANK, HEAD_DIM), lambda g: (g, 0, 0)),
        spec((1, RANK, HEAD_DIM), lambda g: (HEADS + g, 0, 0)),
        spec(past_block, lambda g: (0, 0, g)),
        spec(past_block, lambda g: (0, 0, KV_HEADS + g)),
        whole(cos),
        whole(sin),
    ]
    in_specs += [whole(x) for x in lows]
    in_specs += [gv_spec] * (2 * shards)
    shape = jax.ShapeDtypeStruct
    low_q_shape = shape((seqs, tokens, RANK), f32)
    low_v_shape = shape((seqs, shards * tokens, RANK), f32)
    part_rows = RANK // parts
    scores = GROUP * tokens * (shards * tokens + past_len)
    pairs = seqs * KV_HEADS * scores
    return pl.pallas_call(
        functools.partial(attention_kernel, shards),
        grid=(KV_HEADS,),
        in_specs=in_specs,
        out_specs=[
            q_spec,
            q_spec,
            spec((GROUP, parts, part_rows, HEAD_DIM), lambda g: (g, 0, 0, 0)),
            spec((1, parts, part_rows, HEAD_DIM), lambda g: (g, 0, 0, 0)),
            whole(low_q_shape),
            whole(low_v_shape),
        ]
        + [gv_spec] * shards,
        out_shape=[
            shape(query_base.shape, bf16),
            shape(query_base.shape, bf16),
            shape((HEADS, parts, part_rows, HEAD_DIM), bf16),
            shape((KV_HEADS, parts, part_rows, HEAD_DIM), bf16),
            low_q_shape,
            low_v_shape,
        ]
        + [shape((seqs, tokens, KV), bf16)] * shards,
        scratch_shapes=[
            pltpu.VMEM((2, seqs, tokens, WIDE), bf16),
            pltpu.VMEM((2, seqs, tokens, WIDE), bf16),
            pltpu.SemaphoreType.DMA((2, 2)),
        ],
        compiler_params=pltpu.CompilerParams(
            vmem_limit_bytes=min(8 * 2**20 + 96 * scores, 48 * 2**20)
        ),
        cost_estimate=pl.CostEstimate(
            flops=pairs * HEAD_DIM * 120, bytes_accessed=2**16, transcendentals=pairs
        ),
        name="attention",
    )(place, query_base, grad_out, up_blocks, up_blocks, past, past, cos, sin, *lows, *keys, *bases)


def low_rank_kernel(
    sp, fs, rp, index_ref, own_ref, other_ref, hidden_ref, down_out, up_ref, low_ref, down_ref, sem
):
    z, x, r = index_ref[0], index_ref[1], index_ref[2]
    shards = sp * fs
    down_rows, up_rows = D // (shards * rp), RANK // rp
    blocks = (HEADS + KV_HEADS) // shards
    for piece in range(own_ref.shape[0]):
        shard = (z ^ (piece % sp)) * fs + (x ^ (piece // sp % fs))
        for swap, ref in enumerate((own_ref, other_ref)):
            part = r ^ (piece // shards * 2 + swap)
            at = pl.multiple_of((shard * rp + part) * down_rows, down_rows)
            down_ref[pl.ds(at, down_rows), :] = ref[piece, :down_rows]
            at = pl.multiple_of(part * up_rows, up_rows)
            for j in range(blocks):
                lo = down_rows + j * up_rows
                up_ref[shard * blocks + j, pl.ds(at, up_rows), :] = ref[piece, lo : lo + up_rows]
    copy = pltpu.make_async_copy(down_ref, down_out, sem)
    copy.start()
    rows = jnp.concatenate([hidden_ref[s] for s in range(hidden_ref.shape[0])], axis=0)
    low = mm(rows, down_ref[...], 1, 0).astype(bf16)
    for s in range(low_ref.shape[0]):
        low_ref[s] = low[s * low_ref.shape[1] : (s + 1) * low_ref.shape[1]]
    copy.wait()


def pack_kernel(rp, part_ref, down_ref, up_ref, past_ref, out_ref):
    r = part_ref[0]
    down_rows, up_rows = down_ref.shape[0] // rp, RANK // rp
    out_ref[0, :down_rows] = down_ref[pl.ds(pl.multiple_of(r * down_rows, down_rows), down_rows)]
    at = pl.multiple_of(r * up_rows, up_rows)
    lo = down_rows
    for j in range(up_ref.shape[1] // HEAD_DIM):
        cols = slice(j * HEAD_DIM, (j + 1) * HEAD_DIM)
        out_ref[0, lo : lo + up_rows] = up_ref[pl.ds(at, up_rows), cols]
        lo += up_rows
    out_ref[0, lo:] = past_ref[...]


def pack_adapters(adapter_down, adapter_up, own_past):
    sp, rp, r = lax.axis_size("sp"), lax.axis_size("rep"), lax.axis_index("rep")
    down_rows, up_rows = adapter_down.shape[0] // rp, RANK // rp
    blocks = adapter_up.shape[1] // HEAD_DIM
    rows = down_rows + adapter_up.shape[1] // HEAD_DIM * up_rows
    packed_past = own_past.reshape(-1, 2 * RANK)
    vmem = pl.BlockSpec(memory_space=pltpu.VMEM)
    buf = pl.pallas_call(
        functools.partial(pack_kernel, rp),
        in_specs=[pl.BlockSpec(memory_space=pltpu.SMEM)] + [vmem] * 3,
        out_specs=vmem,
        out_shape=jax.ShapeDtypeStruct((1, rows + packed_past.shape[0], 2 * RANK), bf16),
        compiler_params=pltpu.CompilerParams(vmem_limit_bytes=8 * 1024 * 1024),
        cost_estimate=pl.CostEstimate(flops=0, bytes_accessed=2**19, transcendentals=0),
        name="pack",
    )(r.astype(jnp.int32).reshape(1), adapter_down, adapter_up, packed_past)
    step = 1
    while step < sp:
        buf = jnp.concatenate([buf, partner(buf, "sp", step)], axis=0)
        step *= 2
    seqs, each = own_past.shape[:2]
    past = buf[:, rows:].reshape(sp, seqs, each, -1).swapaxes(0, 1).reshape(seqs, sp * each, -1)
    return buf[:, :rows], past


def adapters_packed(hidden, buf, before_rep, before_swap):
    sp, fs, rp = (lax.axis_size(a) for a in ("sp", "fsdp", "rep"))
    z, x, r = (lax.axis_index(a) for a in ("sp", "fsdp", "rep"))
    step = 1
    while step < fs:
        buf = jnp.concatenate([buf, partner(buf, "fsdp", step)], axis=0)
        step *= 2
    step = 2
    buf = tie(buf, *before_rep)
    while step < rp:
        buf = jnp.concatenate([buf, partner(buf, "rep", step)], axis=0)
        step *= 2
    other = partner(tie(buf, *before_swap), "rep", 1)
    index = jnp.stack([z, x, r]).astype(jnp.int32)
    vmem = pl.BlockSpec(memory_space=pltpu.VMEM)
    seqs, tokens = hidden.shape[:2]
    down_full, up_blocks, low = pl.pallas_call(
        functools.partial(low_rank_kernel, sp, fs, rp),
        in_specs=[pl.BlockSpec(memory_space=pltpu.SMEM)] + [vmem] * 3,
        out_specs=[pl.BlockSpec(memory_space=pltpu.HBM), vmem, vmem],
        scratch_shapes=[pltpu.VMEM((D, 2 * RANK), bf16), pltpu.SemaphoreType.DMA],
        out_shape=[
            jax.ShapeDtypeStruct((D, 2 * RANK), bf16),
            jax.ShapeDtypeStruct((HEADS + KV_HEADS, RANK, HEAD_DIM), bf16),
            jax.ShapeDtypeStruct((seqs, tokens, 2 * RANK), bf16),
        ],
        compiler_params=pltpu.CompilerParams(vmem_limit_bytes=12 * 1024 * 1024),
        cost_estimate=pl.CostEstimate(
            flops=2 * seqs * tokens * D * 2 * RANK, bytes_accessed=2**16, transcendentals=0
        ),
        name="low_rank",
    )(index, buf, other, hidden)
    return down_full, up_blocks, low


def adapters_plain(hidden, adapter_down, adapter_up):
    seqs, tokens = hidden.shape[:2]
    down_full = lax.all_gather(adapter_down, ("sp", "fsdp"), axis=0, tiled=True)
    up_full = lax.all_gather(adapter_up, ("sp", "fsdp"), axis=1, tiled=True)
    rows = hidden.reshape(seqs * tokens, D)
    low = jnp.dot(rows, down_full, preferred_element_type=f32).astype(bf16)
    up_blocks = up_full.reshape(RANK, HEADS + KV_HEADS, HEAD_DIM).swapaxes(0, 1)
    return down_full, up_blocks, low.reshape(seqs, tokens, 2 * RANK)


def grad_hidden_kernel(low_ref, down_ref, out_ref):
    out = mm(low_ref[...], down_ref[...], 1, 1).astype(bf16)
    tokens = out_ref.shape[1]
    for s in range(out_ref.shape[0]):
        out_ref[s] = out[s * tokens : (s + 1) * tokens]


def grad_hidden_of(low_grad, down_full, seqs, tokens):
    columns = 1024
    return pl.pallas_call(
        grad_hidden_kernel,
        grid=(D // columns,),
        in_specs=[
            pl.BlockSpec(low_grad.shape, lambda i: (0, 0)),
            pl.BlockSpec((columns, 2 * RANK), lambda i: (i, 0)),
        ],
        out_specs=pl.BlockSpec((seqs, tokens, columns), lambda i: (0, 0, i)),
        out_shape=jax.ShapeDtypeStruct((seqs, tokens, D), bf16),
        compiler_params=pltpu.CompilerParams(vmem_limit_bytes=12 * 1024 * 1024),
        cost_estimate=pl.CostEstimate(
            flops=16 * seqs * tokens * D * 2 * RANK, bytes_accessed=2**16, transcendentals=0
        ),
        name="grad_hidden",
    )(low_grad, down_full)


def adapter_grads_kernel(core_ref, hidden_ref, low_ref, guq_ref, guv_ref, send_ref, keep_ref, gd_ref):
    c = core_ref[0]
    shards, pairs = send_ref.shape[:2]
    down_rows = gd_ref.shape[1]
    columns = 2 * pairs * down_rows
    blocks = (HEADS + KV_HEADS) // shards
    up_rows = guq_ref.shape[2]
    low = low_ref[...]
    for b in range(shards):
        cols = [hidden_ref[s, :, b * columns : (b + 1) * columns] for s in range(hidden_ref.shape[0])]
        part = mm(jnp.concatenate(cols, axis=0), low, 0, 0).astype(bf16)
        for q in range(2 * pairs):
            gd_ref[q] = part[q * down_rows : (q + 1) * down_rows]
        for hi in range(pairs):
            for ref, q in ((send_ref, 2 * hi + 1 - c), (keep_ref, 2 * hi + c)):
                ref[b, hi, :down_rows] = gd_ref[q]
                for j in range(blocks):
                    block = b * blocks + j
                    src = guq_ref[block, q] if block < HEADS else guv_ref[block - HEADS, q]
                    lo = down_rows + j * up_rows
                    ref[b, hi, lo : lo + up_rows] = src


def packed_grads(hidden, low_grad, guq, guv, shards):
    rp, r = lax.axis_size("rep"), lax.axis_index("rep")
    c = lax.rem(r, 2)
    down_rows, up_rows = D // (shards * rp), RANK // rp
    up_width = (D + KV) // shards
    rows = down_rows + up_rows * up_width // (2 * RANK)
    if up_width % HEAD_DIM == 0:
        vmem = pl.BlockSpec(memory_space=pltpu.VMEM)
        packed = jax.ShapeDtypeStruct((shards, rp // 2, rows, 2 * RANK), bf16)
        return pl.pallas_call(
            adapter_grads_kernel,
            in_specs=[pl.BlockSpec(memory_space=pltpu.SMEM)] + [vmem] * 4,
            out_specs=[vmem] * 2,
            out_shape=[packed] * 2,
            scratch_shapes=[pltpu.VMEM((rp, down_rows, 2 * RANK), bf16)],
            compiler_params=pltpu.CompilerParams(vmem_limit_bytes=12 * 1024 * 1024),
            cost_estimate=pl.CostEstimate(
                flops=2 * hidden.size * 2 * RANK, bytes_accessed=5 * 2**20, transcendentals=0
            ),
            name="adapter_grads",
        )(c.astype(jnp.int32).reshape(1), hidden, low_grad, guq, guv)
    own_rows = hidden.reshape(-1, D)
    down = jnp.dot(own_rows.T, low_grad, preferred_element_type=f32).astype(bf16)
    down = down.reshape(shards, rp, down_rows, 2 * RANK)
    up = jnp.concatenate([guq, guv], axis=0).transpose(1, 2, 0, 3)
    up = up.reshape(rp, up_rows, shards, up_width).transpose(2, 0, 1, 3)
    up = up.reshape(shards, rp, -1, 2 * RANK)
    both = jnp.concatenate([down, up], axis=2).reshape(shards, rp // 2, 2, rows, 2 * RANK)
    send = lax.dynamic_index_in_dim(both, 1 - c, 2, keepdims=False)
    keep = lax.dynamic_index_in_dim(both, c, 2, keepdims=False)
    return send, keep


def finish_grads(send, keep, values, low_grad, hidden_of):
    sp, fs, rp = (lax.axis_size(a) for a in ("sp", "fsdp", "rep"))
    z, r = lax.axis_index("sp"), lax.axis_index("rep")
    shards, _, rows, lanes = send.shape
    far = [along(values[k - 1], "sp", -k) for k in range(3, sp)]
    got = partner(tie(send, *far), "rep", 1)
    values = [along(tie(values[1], got), "sp", -2)] + far
    fs_bits, rep_bits = fs.bit_length() - 1, rp.bit_length() - 2
    labels = [("fsdp", b) for b in reversed(range(fs_bits))]
    labels += [("rep", b + 1) for b in reversed(range(rep_bits))]
    shape = (sp,) + (2,) * len(labels) + (rows, lanes)
    terms = [a.reshape(shape) for a in (keep, got)]

    def halve(terms, order):
        left = list(labels)
        for label in order:
            axis, bit = label
            dim = 1 + left.index(label)
            left.remove(label)
            mine = lax.rem(lax.div(lax.axis_index(axis), 1 << bit), 2)

            def pick(i):
                parts = [lax.dynamic_index_in_dim(a, i, dim, keepdims=False) for a in terms]
                return sum(a.astype(f32) for a in parts).astype(bf16)

            send = pick(1 - mine)
            terms = [pick(mine), partner(send, axis, 1 << bit)]
        return sum(a.astype(f32) for a in terms).astype(bf16)

    cut = rows // 32 * 16
    first_rep, first_fsdp = labels[::-1], labels
    over_sp = halve([a[..., cut:, :] for a in terms], first_rep)
    if cut:
        other = halve([a[..., :cut, :] for a in terms], first_fsdp)
        over_sp = jnp.concatenate([other, over_sp], axis=1)
    over_sp = tie(over_sp, *values)
    total = lax.dynamic_index_in_dim(over_sp, z, 0, keepdims=False).astype(f32)
    for k in range(1, sp):
        send = lax.dynamic_index_in_dim(over_sp, lax.rem(z + k, sp), 0, keepdims=False)
        total = total + cyclic(send, "sp", k).astype(f32)
    grad_hidden = hidden_of(tie(low_grad, over_sp))
    own = tie(total.astype(bf16), grad_hidden)
    parts = [own] + [partner(own, "rep", m) for m in range(1, rp)]
    ordered = []
    for q in range(rp):
        pick = parts[0]
        for m in range(1, rp):
            pick = jnp.where((r ^ m) == q, parts[m], pick)
        ordered.append(pick.astype(f32))
    down_rows, up_rows = D // (shards * rp), RANK // rp
    up_width = (D + KV) // shards
    grad_down = jnp.concatenate([p[:down_rows] for p in ordered], axis=0)
    ups = []
    for p in ordered:
        up = p[down_rows:]
        if up_width % HEAD_DIM == 0:
            up = [up[lo : lo + up_rows] for lo in range(0, up.shape[0], up_rows)]
            up = jnp.concatenate(up, axis=1)
        ups.append(up.reshape(up_rows, up_width))
    return grad_down, jnp.concatenate(ups, axis=0), grad_hidden, values


def body(
    hidden,
    query_base,
    key_span,
    value_base,
    past_keys,
    past_values,
    grad_out,
    adapter_down,
    adapter_up,
):
    sp, fs = lax.axis_size("sp"), lax.axis_size("fsdp")
    z = lax.axis_index("sp")
    seqs, tokens = hidden.shape[:2]
    past_len = past_keys.shape[1] * sp
    own_past = jnp.concatenate([past_keys, past_values], axis=2)
    even = adapter_up.shape[1] % HEAD_DIM == 0
    if even:
        buf, past = pack_adapters(adapter_down, adapter_up, own_past)
    else:
        buf = own_past
        past = [own_past] + [cyclic(own_past, "sp", k) for k in range(1, sp)]
        past = jnp.concatenate(past, axis=1)
    keys, bases = [key_span], [value_base]
    for line in (keys, bases):
        line.append(along(tie(line[0], buf), "sp", 1))
        for k in range(2, sp):
            line.append(along(line[k - 1], "sp", 1, k - 1))
    second = min(2, sp - 1)
    if even:
        down_full, up_blocks, low_own = adapters_packed(
            hidden, buf, (keys[1], bases[1]), (keys[second], bases[second])
        )
    else:
        down_full, up_blocks, low_own = adapters_plain(hidden, adapter_down, adapter_up)
    lows = [low_own] + [along(low_own, "sp", k) for k in range(1, sp)]
    cos, sin = rotary_tables(tokens, past_len + z * tokens)
    place = z.astype(jnp.int32).reshape(1)

    made = attention(place, query_base, grad_out, up_blocks, past, cos, sin, lows, keys, bases)
    attended, grad_query, guq, guv, low_grad_q, low_grad_v = made[:6]
    value_own, values = made[6], made[7:]

    low_v_total = low_grad_v[:, :tokens]
    for k in range(1, sp):
        part = low_grad_v[:, k * tokens : (k + 1) * tokens].astype(bf16)
        low_v_total = low_v_total + along(part, "sp", -k).astype(f32)
    low_grad = (
        jnp.concatenate([low_grad_q, low_v_total], axis=2)
        .astype(bf16)
        .reshape(seqs * tokens, 2 * RANK)
    )
    first_got = along(values[0], "sp", -1)
    send, keep = packed_grads(hidden, tie(low_grad, first_got), guq, guv, sp * fs)
    grad_down, grad_up, grad_hidden, got = finish_grads(
        send, keep, values, low_grad, lambda x: grad_hidden_of(x, down_full, seqs, tokens)
    )
    grad_value = value_own.astype(f32)
    for part in (first_got, *got):
        grad_value = grad_value + part.astype(f32)
    return (
        attended,
        grad_query,
        grad_value.astype(bf16),
        grad_hidden,
        grad_down,
        grad_up,
    )


def solution(mesh):
    rows = P(("fsdp", "rep"), "sp", None)
    down, up = P(("sp", "fsdp"), None), P(None, ("sp", "fsdp"))
    return jax.shard_map(
        body,
        mesh=mesh,
        in_specs=(rows,) * 7 + (down, up),
        out_specs=(rows,) * 4 + (down, up),
        check_vma=False,
    )
```

```python
import functools
import math

import jax
import jax.numpy as jnp
from jax import lax
from jax.experimental import pallas as pl
from jax.experimental.pallas import tpu as pltpu
from jax.sharding import PartitionSpec as P

D = 4096
HEADS = 32
KV_HEADS = 8
HEAD_DIM = 128
RANK = 64
KV = 1024
GROUP = HEADS // KV_HEADS
WIDE = GROUP * HEAD_DIM
ROPE_BASE = 500000.0
HIDDEN_MASK = -1e30
LOG2_E = 1.4426950408889634

f32 = jnp.float32
bf16 = jnp.bfloat16


def rotary_tables(row_count, offset):
    half = HEAD_DIM // 2
    position = (jnp.arange(row_count, dtype=jnp.int32) + offset).astype(f32)
    inverse = jnp.exp(jnp.arange(half, dtype=f32) * (-2.0 * math.log(ROPE_BASE) / HEAD_DIM))
    angle = position[:, None] * inverse[None, :]
    cosine, sine = jnp.cos(angle), jnp.sin(angle)
    return (
        jnp.concatenate([cosine, cosine], axis=1),
        jnp.concatenate([-sine, sine], axis=1),
    )


def cyclic(x, axis, shift):
    n = lax.axis_size(axis)
    return lax.ppermute(x, axis, [(i, (i + shift) % n) for i in range(n)])


def along(x, axis, shift, start=0):
    n = lax.axis_size(axis)
    return lax.ppermute(x, axis, [(i, i + shift) for i in range(start, n) if 0 <= i + shift < n])


def partner(x, axis, mask):
    n = lax.axis_size(axis)
    return lax.ppermute(x, axis, [(i, i ^ mask) for i in range(n)])


def tie(x, *others):
    return lax.optimization_barrier((x,) + others)[0]


def mm(a, b, ca, cb):
    return lax.dot_general(a, b, (((ca,), (cb,)), ((), ())), preferred_element_type=f32)


def attention_kernel(shards, place_ref, *refs):
    it = iter(refs)

    def take(n):
        return [next(it) for _ in range(n)]

    q_hbm, g_hbm, upq_ref, upv_ref, pk_ref, pv_ref, cos_ref, sin_ref = take(8)
    low_refs, k_refs, v_refs = take(shards), take(shards), take(shards)
    att_ref, gq_ref, guq_ref, guv_ref, lgq_ref, lgv_ref = take(6)
    gv_refs = take(shards)
    q_buf, g_buf, sems = take(3)

    group, slot = pl.program_id(0), lax.rem(pl.program_id(0), 2)

    def fetches(step, into):
        at = pl.multiple_of(step * WIDE, WIDE)
        return [
            pltpu.make_async_copy(hbm.at[:, :, pl.ds(at, WIDE)], buf.at[into], sems.at[i, into])
            for i, (hbm, buf) in enumerate(((q_hbm, q_buf), (g_hbm, g_buf)))
        ]

    @pl.when(group == 0)
    def _():
        for copy in fetches(0, 0):
            copy.start()

    @pl.when(group + 1 < pl.num_programs(0))
    def _():
        for copy in fetches(group + 1, 1 - slot):
            copy.start()

    seqs, tokens = q_buf.shape[1:3]
    parts, part_rows = guq_ref.shape[1:3]
    span = shards * tokens
    past = pk_ref.shape[1]
    scale = 1.0 / math.sqrt(HEAD_DIM)
    place = place_ref[0]
    cos, sin = cos_ref[...], sin_ref[...]
    upq = jnp.concatenate([upq_ref[h] for h in range(GROUP)], axis=1)
    upv = upv_ref[0]

    @pl.when(pl.program_id(0) == 0)
    def _():
        lgq_ref[...] = jnp.zeros_like(lgq_ref)
        lgv_ref[...] = jnp.zeros_like(lgv_ref)

    col = lax.broadcasted_iota(jnp.int32, (tokens, span + past), 1)
    row = lax.broadcasted_iota(jnp.int32, (tokens, span + past), 0)
    seen = (col <= row) | ((col >= tokens) & (col < (place + 1) * tokens)) | (col >= span)
    bias = jnp.where(seen, 0.0, HIDDEN_MASK)
    bias = jnp.concatenate([bias] * GROUP, axis=0)

    def heads(x):
        return jnp.concatenate(
            [x[:, h * HEAD_DIM : (h + 1) * HEAD_DIM] for h in range(GROUP)], axis=0
        )

    def lanes(x):
        return jnp.concatenate([x[h * tokens : (h + 1) * tokens] for h in range(GROUP)], axis=1)

    cos4 = jnp.concatenate([cos] * GROUP, axis=0)
    sin4 = jnp.concatenate([sin] * GROUP, axis=0)
    every = range(seqs)
    low_q = jnp.concatenate([low_refs[0][s][:, :RANK] for s in every], axis=0)
    low_v = jnp.concatenate([r[s][:, RANK:] for s in every for r in low_refs], axis=0)
    query_delta = mm(low_q, upq, 1, 0)
    value_delta = mm(low_v, upv, 1, 0)
    for copy in fetches(group, slot):
        copy.wait()
    backs, gvs = [], []
    for s in every:
        delta = heads(query_delta[s * tokens : (s + 1) * tokens])
        delta = delta * cos4 + pltpu.roll(delta, HEAD_DIM // 2, 1) * sin4
        q = (heads(q_buf[slot, s]).astype(f32) + delta).astype(bf16)
        g = heads(g_buf[slot, s])
        keys = jnp.concatenate([r[s] for r in k_refs] + [pk_ref[s]], axis=0)
        base = jnp.concatenate([r[s] for r in v_refs], axis=0).astype(f32)
        vals = (base + value_delta[s * span : (s + 1) * span]).astype(bf16)
        vals = jnp.concatenate([vals, pv_ref[s]], axis=0)

        scores = mm(q, keys, 1, 1) * (scale * LOG2_E) + bias
        top = jnp.max(scores, axis=-1, keepdims=True)
        e = jnp.exp2(scores - top)
        inverse = 1.0 / jnp.sum(e, axis=-1, keepdims=True)
        weights = e.astype(bf16)
        out = (mm(weights, vals, 1, 0) * inverse).astype(bf16)
        att_ref[s] = lanes(out)
        g = (g.astype(f32) * inverse).astype(bf16)
        prob_grad = mm(g, vals, 1, 1)
        row_delta = jnp.sum(g.astype(f32) * out.astype(f32), axis=-1, keepdims=True)
        score_grad = (e * (prob_grad - row_delta)).astype(bf16)
        gq = (mm(score_grad, keys, 1, 0) * scale).astype(bf16)
        gq_ref[s] = lanes(gq)
        gq32 = gq.astype(f32)
        back = (gq32 * cos4 - pltpu.roll(gq32, HEAD_DIM // 2, 1) * sin4).astype(bf16)
        backs.append(lanes(back))
        gv = mm(weights[:, :span], g, 0, 0).astype(bf16)
        gvs.append(gv)
        for k in range(shards):
            gv_refs[k][s] = gv[k * tokens : (k + 1) * tokens]
    back = jnp.concatenate(backs, axis=0)
    gv = jnp.concatenate(gvs, axis=0)
    low_grad_q = mm(back, upq, 1, 1)
    low_grad_v = mm(gv, upv, 1, 1)
    for s in every:
        lgq_ref[s] += low_grad_q[s * tokens : (s + 1) * tokens]
        lgv_ref[s] += low_grad_v[s * span : (s + 1) * span]
    grad_up_q = mm(low_q, back, 0, 0)
    grad_up_v = mm(low_v, gv, 0, 0)
    grad_up_q, grad_up_v = grad_up_q.astype(bf16), grad_up_v.astype(bf16)
    for p in range(parts):
        rows = slice(p * part_rows, (p + 1) * part_rows)
        for h in range(GROUP):
            guq_ref[h, p] = grad_up_q[rows, h * HEAD_DIM : (h + 1) * HEAD_DIM]
        guv_ref[0, p] = grad_up_v[rows]


def attention(place, query_base, grad_out, up_blocks, past, cos, sin, lows, keys, bases):
    shards = len(keys)
    parts = lax.axis_size("rep")
    seqs, tokens = query_base.shape[:2]
    past_len = past.shape[1]

    def whole(x):
        return pl.BlockSpec(x.shape, lambda g: (0,) * len(x.shape))

    spec = pl.BlockSpec
    q_spec = spec((seqs, tokens, WIDE), lambda g: (0, 0, g))
    gv_spec = spec((seqs, tokens, HEAD_DIM), lambda g: (0, 0, g))
    past_block = (seqs, past_len, HEAD_DIM)
    in_specs = [
        spec(memory_space=pltpu.SMEM),
        spec(memory_space=pltpu.HBM),
        spec(memory_space=pltpu.HBM),
        spec((GROUP, RANK, HEAD_DIM), lambda g: (g, 0, 0)),
        spec((1, RANK, HEAD_DIM), lambda g: (HEADS + g, 0, 0)),
        spec(past_block, lambda g: (0, 0, g)),
        spec(past_block, lambda g: (0, 0, KV_HEADS + g)),
        whole(cos),
        whole(sin),
    ]
    in_specs += [whole(x) for x in lows]
    in_specs += [gv_spec] * (2 * shards)
    shape = jax.ShapeDtypeStruct
    low_q_shape = shape((seqs, tokens, RANK), f32)
    low_v_shape = shape((seqs, shards * tokens, RANK), f32)
    part_rows = RANK // parts
    scores = GROUP * tokens * (shards * tokens + past_len)
    pairs = seqs * KV_HEADS * scores
    return pl.pallas_call(
        functools.partial(attention_kernel, shards),
        grid=(KV_HEADS,),
        in_specs=in_specs,
        out_specs=[
            q_spec,
            q_spec,
            spec((GROUP, parts, part_rows, HEAD_DIM), lambda g: (g, 0, 0, 0)),
            spec((1, parts, part_rows, HEAD_DIM), lambda g: (g, 0, 0, 0)),
            whole(low_q_shape),
            whole(low_v_shape),
        ]
        + [gv_spec] * shards,
        out_shape=[
            shape(query_base.shape, bf16),
            shape(query_base.shape, bf16),
            shape((HEADS, parts, part_rows, HEAD_DIM), bf16),
            shape((KV_HEADS, parts, part_rows, HEAD_DIM), bf16),
            low_q_shape,
            low_v_shape,
        ]
        + [shape((seqs, tokens, KV), bf16)] * shards,
        scratch_shapes=[
            pltpu.VMEM((2, seqs, tokens, WIDE), bf16),
            pltpu.VMEM((2, seqs, tokens, WIDE), bf16),
            pltpu.SemaphoreType.DMA((2, 2)),
        ],
        compiler_params=pltpu.CompilerParams(
            vmem_limit_bytes=min(8 * 2**20 + 96 * scores, 48 * 2**20)
        ),
        cost_estimate=pl.CostEstimate(
            flops=pairs * HEAD_DIM * 120, bytes_accessed=2**16, transcendentals=pairs
        ),
        name="attention",
    )(place, query_base, grad_out, up_blocks, up_blocks, past, past, cos, sin, *lows, *keys, *bases)


def low_rank_kernel(
    sp, fs, rp, index_ref, own_ref, other_ref, hidden_ref, down_out, up_ref, low_ref, down_ref, sem
):
    z, x, r = index_ref[0], index_ref[1], index_ref[2]
    shards = sp * fs
    down_rows, up_rows = D // (shards * rp), RANK // rp
    blocks = (HEADS + KV_HEADS) // shards
    for piece in range(own_ref.shape[0]):
        shard = (z ^ (piece % sp)) * fs + (x ^ (piece // sp % fs))
        for swap, ref in enumerate((own_ref, other_ref)):
            part = r ^ (piece // shards * 2 + swap)
            at = pl.multiple_of((shard * rp + part) * down_rows, down_rows)
            down_ref[pl.ds(at, down_rows), :] = ref[piece, :down_rows]
            at = pl.multiple_of(part * up_rows, up_rows)
            for j in range(blocks):
                lo = down_rows + j * up_rows
                up_ref[shard * blocks + j, pl.ds(at, up_rows), :] = ref[piece, lo : lo + up_rows]
    copy = pltpu.make_async_copy(down_ref, down_out, sem)
    copy.start()
    rows = jnp.concatenate([hidden_ref[s] for s in range(hidden_ref.shape[0])], axis=0)
    low = mm(rows, down_ref[...], 1, 0).astype(bf16)
    for s in range(low_ref.shape[0]):
        low_ref[s] = low[s * low_ref.shape[1] : (s + 1) * low_ref.shape[1]]
    copy.wait()


def pack_kernel(rp, part_ref, down_ref, up_ref, past_ref, out_ref):
    r = part_ref[0]
    down_rows, up_rows = down_ref.shape[0] // rp, RANK // rp
    out_ref[0, :down_rows] = down_ref[pl.ds(pl.multiple_of(r * down_rows, down_rows), down_rows)]
    at = pl.multiple_of(r * up_rows, up_rows)
    lo = down_rows
    for j in range(up_ref.shape[1] // HEAD_DIM):
        cols = slice(j * HEAD_DIM, (j + 1) * HEAD_DIM)
        out_ref[0, lo : lo + up_rows] = up_ref[pl.ds(at, up_rows), cols]
        lo += up_rows
    out_ref[0, lo:] = past_ref[...]


def pack_adapters(adapter_down, adapter_up, own_past, before):
    sp, rp, r = lax.axis_size("sp"), lax.axis_size("rep"), lax.axis_index("rep")
    down_rows, up_rows = adapter_down.shape[0] // rp, RANK // rp
    blocks = adapter_up.shape[1] // HEAD_DIM
    rows = down_rows + adapter_up.shape[1] // HEAD_DIM * up_rows
    packed_past = own_past.reshape(-1, 2 * RANK)
    vmem = pl.BlockSpec(memory_space=pltpu.VMEM)
    buf = pl.pallas_call(
        functools.partial(pack_kernel, rp),
        in_specs=[pl.BlockSpec(memory_space=pltpu.SMEM)] + [vmem] * 3,
        out_specs=vmem,
        out_shape=jax.ShapeDtypeStruct((1, rows + packed_past.shape[0], 2 * RANK), bf16),
        compiler_params=pltpu.CompilerParams(vmem_limit_bytes=8 * 1024 * 1024),
        cost_estimate=pl.CostEstimate(flops=0, bytes_accessed=2**19, transcendentals=0),
        name="pack",
    )(r.astype(jnp.int32).reshape(1), adapter_down, adapter_up, packed_past)
    step = 1
    while step < sp:
        buf = jnp.concatenate([buf, partner(buf, "sp", step)], axis=0)
        if step == 1:
            buf = tie(buf, before)
        step *= 2
    seqs, each = own_past.shape[:2]
    past = buf[:, rows:].reshape(sp, seqs, each, -1).swapaxes(0, 1).reshape(seqs, sp * each, -1)
    return buf[:, :rows], past


def adapters_packed(hidden, buf, before_fsdp, before_rep, before_swap):
    sp, fs, rp = (lax.axis_size(a) for a in ("sp", "fsdp", "rep"))
    z, x, r = (lax.axis_index(a) for a in ("sp", "fsdp", "rep"))
    buf = tie(buf, before_fsdp)
    step = 1
    while step < fs:
        buf = jnp.concatenate([buf, partner(buf, "fsdp", step)], axis=0)
        step *= 2
    step = 2
    buf = tie(buf, before_rep)
    while step < rp:
        buf = jnp.concatenate([buf, partner(buf, "rep", step)], axis=0)
        step *= 2
    other = partner(tie(buf, *before_swap), "rep", 1)
    index = jnp.stack([z, x, r]).astype(jnp.int32)
    vmem = pl.BlockSpec(memory_space=pltpu.VMEM)
    seqs, tokens = hidden.shape[:2]
    down_full, up_blocks, low = pl.pallas_call(
        functools.partial(low_rank_kernel, sp, fs, rp),
        in_specs=[pl.BlockSpec(memory_space=pltpu.SMEM)] + [vmem] * 3,
        out_specs=[pl.BlockSpec(memory_space=pltpu.HBM), vmem, vmem],
        scratch_shapes=[pltpu.VMEM((D, 2 * RANK), bf16), pltpu.SemaphoreType.DMA],
        out_shape=[
            jax.ShapeDtypeStruct((D, 2 * RANK), bf16),
            jax.ShapeDtypeStruct((HEADS + KV_HEADS, RANK, HEAD_DIM), bf16),
            jax.ShapeDtypeStruct((seqs, tokens, 2 * RANK), bf16),
        ],
        compiler_params=pltpu.CompilerParams(vmem_limit_bytes=12 * 1024 * 1024),
        cost_estimate=pl.CostEstimate(
            flops=2 * seqs * tokens * D * 2 * RANK, bytes_accessed=2**16, transcendentals=0
        ),
        name="low_rank",
    )(index, buf, other, hidden)
    return down_full, up_blocks, low


def adapters_plain(hidden, adapter_down, adapter_up):
    seqs, tokens = hidden.shape[:2]
    down_full = lax.all_gather(adapter_down, ("sp", "fsdp"), axis=0, tiled=True)
    up_full = lax.all_gather(adapter_up, ("sp", "fsdp"), axis=1, tiled=True)
    rows = hidden.reshape(seqs * tokens, D)
    low = jnp.dot(rows, down_full, preferred_element_type=f32).astype(bf16)
    up_blocks = up_full.reshape(RANK, HEADS + KV_HEADS, HEAD_DIM).swapaxes(0, 1)
    return down_full, up_blocks, low.reshape(seqs, tokens, 2 * RANK)


def grad_hidden_kernel(low_ref, down_ref, out_ref):
    out = mm(low_ref[...], down_ref[...], 1, 1).astype(bf16)
    tokens = out_ref.shape[1]
    for s in range(out_ref.shape[0]):
        out_ref[s] = out[s * tokens : (s + 1) * tokens]


def grad_hidden_of(low_grad, down_full, seqs, tokens):
    columns = 1024
    return pl.pallas_call(
        grad_hidden_kernel,
        grid=(D // columns,),
        in_specs=[
            pl.BlockSpec(low_grad.shape, lambda i: (0, 0)),
            pl.BlockSpec((columns, 2 * RANK), lambda i: (i, 0)),
        ],
        out_specs=pl.BlockSpec((seqs, tokens, columns), lambda i: (0, 0, i)),
        out_shape=jax.ShapeDtypeStruct((seqs, tokens, D), bf16),
        compiler_params=pltpu.CompilerParams(vmem_limit_bytes=12 * 1024 * 1024),
        cost_estimate=pl.CostEstimate(
            flops=16 * seqs * tokens * D * 2 * RANK, bytes_accessed=2**16, transcendentals=0
        ),
        name="grad_hidden",
    )(low_grad, down_full)


def adapter_grads_kernel(core_ref, hidden_ref, low_ref, guq_ref, guv_ref, send_ref, keep_ref, gd_ref):
    c = core_ref[0]
    shards, pairs = send_ref.shape[:2]
    down_rows = gd_ref.shape[1]
    columns = 2 * pairs * down_rows
    blocks = (HEADS + KV_HEADS) // shards
    up_rows = guq_ref.shape[2]
    low = low_ref[...]
    for b in range(shards):
        cols = [hidden_ref[s, :, b * columns : (b + 1) * columns] for s in range(hidden_ref.shape[0])]
        part = mm(jnp.concatenate(cols, axis=0), low, 0, 0).astype(bf16)
        for q in range(2 * pairs):
            gd_ref[q] = part[q * down_rows : (q + 1) * down_rows]
        for hi in range(pairs):
            for ref, q in ((send_ref, 2 * hi + 1 - c), (keep_ref, 2 * hi + c)):
                ref[b, hi, :down_rows] = gd_ref[q]
                for j in range(blocks):
                    block = b * blocks + j
                    src = guq_ref[block, q] if block < HEADS else guv_ref[block - HEADS, q]
                    lo = down_rows + j * up_rows
                    ref[b, hi, lo : lo + up_rows] = src


def packed_grads(hidden, low_grad, guq, guv, shards):
    rp, r = lax.axis_size("rep"), lax.axis_index("rep")
    c = lax.rem(r, 2)
    down_rows, up_rows = D // (shards * rp), RANK // rp
    up_width = (D + KV) // shards
    rows = down_rows + up_rows * up_width // (2 * RANK)
    if up_width % HEAD_DIM == 0:
        vmem = pl.BlockSpec(memory_space=pltpu.VMEM)
        packed = jax.ShapeDtypeStruct((shards, rp // 2, rows, 2 * RANK), bf16)
        return pl.pallas_call(
            adapter_grads_kernel,
            in_specs=[pl.BlockSpec(memory_space=pltpu.SMEM)] + [vmem] * 4,
            out_specs=[vmem] * 2,
            out_shape=[packed] * 2,
            scratch_shapes=[pltpu.VMEM((rp, down_rows, 2 * RANK), bf16)],
            compiler_params=pltpu.CompilerParams(vmem_limit_bytes=12 * 1024 * 1024),
            cost_estimate=pl.CostEstimate(
                flops=2 * hidden.size * 2 * RANK, bytes_accessed=5 * 2**20, transcendentals=0
            ),
            name="adapter_grads",
        )(c.astype(jnp.int32).reshape(1), hidden, low_grad, guq, guv)
    own_rows = hidden.reshape(-1, D)
    down = jnp.dot(own_rows.T, low_grad, preferred_element_type=f32).astype(bf16)
    down = down.reshape(shards, rp, down_rows, 2 * RANK)
    up = jnp.concatenate([guq, guv], axis=0).transpose(1, 2, 0, 3)
    up = up.reshape(rp, up_rows, shards, up_width).transpose(2, 0, 1, 3)
    up = up.reshape(shards, rp, -1, 2 * RANK)
    both = jnp.concatenate([down, up], axis=2).reshape(shards, rp // 2, 2, rows, 2 * RANK)
    send = lax.dynamic_index_in_dim(both, 1 - c, 2, keepdims=False)
    keep = lax.dynamic_index_in_dim(both, c, 2, keepdims=False)
    return send, keep


def finish_grads(send, keep, values, low_grad, hidden_of):
    sp, fs, rp = (lax.axis_size(a) for a in ("sp", "fsdp", "rep"))
    z, r = lax.axis_index("sp"), lax.axis_index("rep")
    shards, _, rows, lanes = send.shape
    far = [along(values[k - 1], "sp", -k) for k in range(3, sp)]
    got = partner(send, "rep", 1)
    values = [along(tie(values[1], got), "sp", -2)] + far
    fs_bits, rep_bits = fs.bit_length() - 1, rp.bit_length() - 2
    labels = [("fsdp", b) for b in reversed(range(fs_bits))]
    labels += [("rep", b + 1) for b in reversed(range(rep_bits))]
    shape = (sp,) + (2,) * len(labels) + (rows, lanes)
    terms = [a.reshape(shape) for a in (keep, got)]

    def halve(terms, order):
        left = list(labels)
        for label in order:
            axis, bit = label
            dim = 1 + left.index(label)
            left.remove(label)
            mine = lax.rem(lax.div(lax.axis_index(axis), 1 << bit), 2)

            def pick(i):
                parts = [lax.dynamic_index_in_dim(a, i, dim, keepdims=False) for a in terms]
                return sum(a.astype(f32) for a in parts).astype(bf16)

            send = tie(pick(1 - mine), *far)
            terms = [pick(mine), partner(send, axis, 1 << bit)]
        return sum(a.astype(f32) for a in terms).astype(bf16)

    cut = rows // 32 * 16
    first_rep, first_fsdp = labels[::-1], labels
    over_sp = halve([a[..., cut:, :] for a in terms], first_rep)
    if cut:
        other = halve([a[..., :cut, :] for a in terms], first_fsdp)
        over_sp = jnp.concatenate([other, over_sp], axis=1)
    over_sp = tie(over_sp, *values)
    total = lax.dynamic_index_in_dim(over_sp, z, 0, keepdims=False).astype(f32)
    for k in range(1, sp):
        send = lax.dynamic_index_in_dim(over_sp, lax.rem(z + k, sp), 0, keepdims=False)
        total = total + cyclic(send, "sp", k).astype(f32)
    grad_hidden = hidden_of(tie(low_grad, over_sp))
    own = tie(total.astype(bf16), grad_hidden)
    parts = [own] + [partner(own, "rep", m) for m in range(1, rp)]
    ordered = []
    for q in range(rp):
        pick = parts[0]
        for m in range(1, rp):
            pick = jnp.where((r ^ m) == q, parts[m], pick)
        ordered.append(pick.astype(f32))
    down_rows, up_rows = D // (shards * rp), RANK // rp
    up_width = (D + KV) // shards
    grad_down = jnp.concatenate([p[:down_rows] for p in ordered], axis=0)
    ups = []
    for p in ordered:
        up = p[down_rows:]
        if up_width % HEAD_DIM == 0:
            up = [up[lo : lo + up_rows] for lo in range(0, up.shape[0], up_rows)]
            up = jnp.concatenate(up, axis=1)
        ups.append(up.reshape(up_rows, up_width))
    return grad_down, jnp.concatenate(ups, axis=0), grad_hidden, values


def body(
    hidden,
    query_base,
    key_span,
    value_base,
    past_keys,
    past_values,
    grad_out,
    adapter_down,
    adapter_up,
):
    sp, fs = lax.axis_size("sp"), lax.axis_size("fsdp")
    z = lax.axis_index("sp")
    seqs, tokens = hidden.shape[:2]
    past_len = past_keys.shape[1] * sp
    own_past = jnp.concatenate([past_keys, past_values], axis=2)
    keys, bases = [key_span], [value_base]
    for line in (keys, bases):
        for k in range(1, sp):
            line.append(along(line[k - 1], "sp", 1, k - 1))
    even = adapter_up.shape[1] % HEAD_DIM == 0
    if even:
        buf, past = pack_adapters(adapter_down, adapter_up, own_past, keys[1])
    else:
        past = [own_past] + [cyclic(own_past, "sp", k) for k in range(1, sp)]
        past = jnp.concatenate(past, axis=1)
    second = min(2, sp - 1)
    if even:
        down_full, up_blocks, low_own = adapters_packed(
            hidden, buf, bases[1], keys[second], (bases[second], keys[min(3, sp - 1)])
        )
    else:
        down_full, up_blocks, low_own = adapters_plain(hidden, adapter_down, adapter_up)
    lows = [low_own] + [along(low_own, "sp", k) for k in range(1, sp)]
    cos, sin = rotary_tables(tokens, past_len + z * tokens)
    place = z.astype(jnp.int32).reshape(1)

    made = attention(place, query_base, grad_out, up_blocks, past, cos, sin, lows, keys, bases)
    attended, grad_query, guq, guv, low_grad_q, low_grad_v = made[:6]
    value_own, values = made[6], made[7:]

    low_v_total = low_grad_v[:, :tokens]
    for k in range(1, sp):
        part = low_grad_v[:, k * tokens : (k + 1) * tokens].astype(bf16)
        low_v_total = low_v_total + along(part, "sp", -k).astype(f32)
    low_grad = (
        jnp.concatenate([low_grad_q, low_v_total], axis=2)
        .astype(bf16)
        .reshape(seqs * tokens, 2 * RANK)
    )
    first_got = along(values[0], "sp", -1)
    send, keep = packed_grads(hidden, low_grad, guq, guv, sp * fs)
    send = tie(send, first_got)
    grad_down, grad_up, grad_hidden, got = finish_grads(
        send, keep, values, low_grad, lambda x: grad_hidden_of(x, down_full, seqs, tokens)
    )
    grad_value = value_own.astype(f32)
    for part in (first_got, *got):
        grad_value = grad_value + part.astype(f32)
    return (
        attended,
        grad_query,
        grad_value.astype(bf16),
        grad_hidden,
        grad_down,
        grad_up,
    )


def solution(mesh):
    rows = P(("fsdp", "rep"), "sp", None)
    down, up = P(("sp", "fsdp"), None), P(None, ("sp", "fsdp"))
    return jax.shard_map(
        body,
        mesh=mesh,
        in_specs=(rows,) * 7 + (down, up),
        out_specs=(rows,) * 4 + (down, up),
        check_vma=False,
    )
```

```python
import functools
import math

import jax
import jax.numpy as jnp
from jax import lax
from jax.experimental import pallas as pl
from jax.experimental.pallas import tpu as pltpu
from jax.sharding import PartitionSpec as P

D = 4096
HEADS = 32
KV_HEADS = 8
HEAD_DIM = 128
RANK = 64
KV = 1024
GROUP = HEADS // KV_HEADS
WIDE = GROUP * HEAD_DIM
ROPE_BASE = 500000.0
HIDDEN_MASK = -1e30
LOG2_E = 1.4426950408889634

f32 = jnp.float32
bf16 = jnp.bfloat16


def rotary_tables(row_count, offset):
    half = HEAD_DIM // 2
    position = (jnp.arange(row_count, dtype=jnp.int32) + offset).astype(f32)
    inverse = jnp.exp(jnp.arange(half, dtype=f32) * (-2.0 * math.log(ROPE_BASE) / HEAD_DIM))
    angle = position[:, None] * inverse[None, :]
    cosine, sine = jnp.cos(angle), jnp.sin(angle)
    return (
        jnp.concatenate([cosine, cosine], axis=1),
        jnp.concatenate([-sine, sine], axis=1),
    )


def cyclic(x, axis, shift):
    n = lax.axis_size(axis)
    return lax.ppermute(x, axis, [(i, (i + shift) % n) for i in range(n)])


def along(x, axis, shift, start=0):
    n = lax.axis_size(axis)
    return lax.ppermute(x, axis, [(i, i + shift) for i in range(start, n) if 0 <= i + shift < n])


def partner(x, axis, mask):
    n = lax.axis_size(axis)
    return lax.ppermute(x, axis, [(i, i ^ mask) for i in range(n)])


def tie(x, *others):
    return lax.optimization_barrier((x,) + others)[0]


def mm(a, b, ca, cb):
    return lax.dot_general(a, b, (((ca,), (cb,)), ((), ())), preferred_element_type=f32)


def attention_kernel(shards, place_ref, *refs):
    it = iter(refs)

    def take(n):
        return [next(it) for _ in range(n)]

    q_hbm, g_hbm, upq_ref, upv_ref, pk_ref, pv_ref, cos_ref, sin_ref = take(8)
    low_refs, k_refs, v_refs = take(shards), take(shards), take(shards)
    att_ref, gq_ref, guq_ref, guv_ref, lgq_ref, lgv_ref = take(6)
    gv_refs = take(shards)
    q_buf, g_buf, sems = take(3)

    group, slot = pl.program_id(0), lax.rem(pl.program_id(0), 2)

    def fetches(step, into):
        at = pl.multiple_of(step * WIDE, WIDE)
        return [
            pltpu.make_async_copy(hbm.at[:, :, pl.ds(at, WIDE)], buf.at[into], sems.at[i, into])
            for i, (hbm, buf) in enumerate(((q_hbm, q_buf), (g_hbm, g_buf)))
        ]

    @pl.when(group == 0)
    def _():
        for copy in fetches(0, 0):
            copy.start()

    @pl.when(group + 1 < pl.num_programs(0))
    def _():
        for copy in fetches(group + 1, 1 - slot):
            copy.start()

    seqs, tokens = q_buf.shape[1:3]
    parts, part_rows = guq_ref.shape[1:3]
    span = shards * tokens
    past = pk_ref.shape[1]
    scale = 1.0 / math.sqrt(HEAD_DIM)
    place = place_ref[0]
    cos, sin = cos_ref[...], sin_ref[...]
    upq = jnp.concatenate([upq_ref[h] for h in range(GROUP)], axis=1)
    upv = upv_ref[0]

    @pl.when(pl.program_id(0) == 0)
    def _():
        lgq_ref[...] = jnp.zeros_like(lgq_ref)
        lgv_ref[...] = jnp.zeros_like(lgv_ref)

    col = lax.broadcasted_iota(jnp.int32, (tokens, span + past), 1)
    row = lax.broadcasted_iota(jnp.int32, (tokens, span + past), 0)
    seen = (col <= row) | ((col >= tokens) & (col < (place + 1) * tokens)) | (col >= span)
    bias = jnp.where(seen, 0.0, HIDDEN_MASK)
    bias = jnp.concatenate([bias] * GROUP, axis=0)

    def heads(x):
        return jnp.concatenate(
            [x[:, h * HEAD_DIM : (h + 1) * HEAD_DIM] for h in range(GROUP)], axis=0
        )

    def lanes(x):
        return jnp.concatenate([x[h * tokens : (h + 1) * tokens] for h in range(GROUP)], axis=1)

    cos4 = jnp.concatenate([cos] * GROUP, axis=0)
    sin4 = jnp.concatenate([sin] * GROUP, axis=0)
    every = range(seqs)
    low_q = jnp.concatenate([low_refs[0][s][:, :RANK] for s in every], axis=0)
    low_v = jnp.concatenate([r[s][:, RANK:] for s in every for r in low_refs], axis=0)
    query_delta = mm(low_q, upq, 1, 0)
    value_delta = mm(low_v, upv, 1, 0)
    for copy in fetches(group, slot):
        copy.wait()
    backs, gvs = [], []
    for s in every:
        delta = heads(query_delta[s * tokens : (s + 1) * tokens])
        delta = delta * cos4 + pltpu.roll(delta, HEAD_DIM // 2, 1) * sin4
        q = (heads(q_buf[slot, s]).astype(f32) + delta).astype(bf16)
        g = heads(g_buf[slot, s])
        keys = jnp.concatenate([r[s] for r in k_refs] + [pk_ref[s]], axis=0)
        base = jnp.concatenate([r[s] for r in v_refs], axis=0).astype(f32)
        vals = (base + value_delta[s * span : (s + 1) * span]).astype(bf16)
        vals = jnp.concatenate([vals, pv_ref[s]], axis=0)

        scores = mm(q, keys, 1, 1) * (scale * LOG2_E) + bias
        top = jnp.max(scores, axis=-1, keepdims=True)
        e = jnp.exp2(scores - top)
        inverse = 1.0 / jnp.sum(e, axis=-1, keepdims=True)
        weights = e.astype(bf16)
        out = (mm(weights, vals, 1, 0) * inverse).astype(bf16)
        att_ref[s] = lanes(out)
        g = (g.astype(f32) * inverse).astype(bf16)
        prob_grad = mm(g, vals, 1, 1)
        row_delta = jnp.sum(g.astype(f32) * out.astype(f32), axis=-1, keepdims=True)
        score_grad = (e * (prob_grad - row_delta)).astype(bf16)
        gq = (mm(score_grad, keys, 1, 0) * scale).astype(bf16)
        gq_ref[s] = lanes(gq)
        gq32 = gq.astype(f32)
        back = (gq32 * cos4 - pltpu.roll(gq32, HEAD_DIM // 2, 1) * sin4).astype(bf16)
        backs.append(lanes(back))
        gv = mm(weights[:, :span], g, 0, 0).astype(bf16)
        gvs.append(gv)
        for k in range(shards):
            gv_refs[k][s] = gv[k * tokens : (k + 1) * tokens]
    back = jnp.concatenate(backs, axis=0)
    gv = jnp.concatenate(gvs, axis=0)
    low_grad_q = mm(back, upq, 1, 1)
    low_grad_v = mm(gv, upv, 1, 1)
    for s in every:
        lgq_ref[s] += low_grad_q[s * tokens : (s + 1) * tokens]
        lgv_ref[s] += low_grad_v[s * span : (s + 1) * span]
    grad_up_q = mm(low_q, back, 0, 0)
    grad_up_v = mm(low_v, gv, 0, 0)
    grad_up_q, grad_up_v = grad_up_q.astype(bf16), grad_up_v.astype(bf16)
    for p in range(parts):
        rows = slice(p * part_rows, (p + 1) * part_rows)
        for h in range(GROUP):
            guq_ref[h, p] = grad_up_q[rows, h * HEAD_DIM : (h + 1) * HEAD_DIM]
        guv_ref[0, p] = grad_up_v[rows]


def attention(place, query_base, grad_out, up_blocks, past, cos, sin, lows, kvs):
    shards = len(kvs)
    parts = lax.axis_size("rep")
    seqs, tokens = query_base.shape[:2]
    past_len = past.shape[1]

    def whole(x):
        return pl.BlockSpec(x.shape, lambda g: (0,) * len(x.shape))

    spec = pl.BlockSpec
    q_spec = spec((seqs, tokens, WIDE), lambda g: (0, 0, g))
    gv_spec = spec((seqs, tokens, HEAD_DIM), lambda g: (0, 0, g))
    past_block = (seqs, past_len, HEAD_DIM)
    in_specs = [
        spec(memory_space=pltpu.SMEM),
        spec(memory_space=pltpu.HBM),
        spec(memory_space=pltpu.HBM),
        spec((GROUP, RANK, HEAD_DIM), lambda g: (g, 0, 0)),
        spec((1, RANK, HEAD_DIM), lambda g: (HEADS + g, 0, 0)),
        spec(past_block, lambda g: (0, 0, g)),
        spec(past_block, lambda g: (0, 0, KV_HEADS + g)),
        whole(cos),
        whole(sin),
    ]
    in_specs += [whole(x) for x in lows]
    in_specs += [gv_spec] * shards
    in_specs += [spec((seqs, tokens, HEAD_DIM), lambda g: (0, 0, KV_HEADS + g))] * shards
    shape = jax.ShapeDtypeStruct
    low_q_shape = shape((seqs, tokens, RANK), f32)
    low_v_shape = shape((seqs, shards * tokens, RANK), f32)
    part_rows = RANK // parts
    scores = GROUP * tokens * (shards * tokens + past_len)
    pairs = seqs * KV_HEADS * scores
    return pl.pallas_call(
        functools.partial(attention_kernel, shards),
        grid=(KV_HEADS,),
        in_specs=in_specs,
        out_specs=[
            q_spec,
            q_spec,
            spec((GROUP, parts, part_rows, HEAD_DIM), lambda g: (g, 0, 0, 0)),
            spec((1, parts, part_rows, HEAD_DIM), lambda g: (g, 0, 0, 0)),
            whole(low_q_shape),
            whole(low_v_shape),
        ]
        + [gv_spec] * shards,
        out_shape=[
            shape(query_base.shape, bf16),
            shape(query_base.shape, bf16),
            shape((HEADS, parts, part_rows, HEAD_DIM), bf16),
            shape((KV_HEADS, parts, part_rows, HEAD_DIM), bf16),
            low_q_shape,
            low_v_shape,
        ]
        + [shape((seqs, tokens, KV), bf16)] * shards,
        scratch_shapes=[
            pltpu.VMEM((2, seqs, tokens, WIDE), bf16),
            pltpu.VMEM((2, seqs, tokens, WIDE), bf16),
            pltpu.SemaphoreType.DMA((2, 2)),
        ],
        compiler_params=pltpu.CompilerParams(
            vmem_limit_bytes=min(8 * 2**20 + 96 * scores, 48 * 2**20)
        ),
        cost_estimate=pl.CostEstimate(
            flops=pairs * HEAD_DIM * 120, bytes_accessed=2**16, transcendentals=pairs
        ),
        name="attention",
    )(place, query_base, grad_out, up_blocks, up_blocks, past, past, cos, sin, *lows, *kvs, *kvs)


def low_rank_kernel(
    sp, fs, rp, index_ref, own_ref, other_ref, hidden_ref, *refs
):
    down_out, up_ref, low_ref, down_ref, sem = refs[-5:]
    z, x, r = index_ref[0], index_ref[1], index_ref[2]
    shards = sp * fs
    down_rows, up_rows = D // (shards * rp), RANK // rp
    blocks = (HEADS + KV_HEADS) // shards
    for piece in range(own_ref.shape[0]):
        shard = (z ^ (piece % sp)) * fs + (x ^ (piece // sp % fs))
        for swap, ref in enumerate((own_ref, other_ref)):
            part = r ^ (piece // shards * 2 + swap)
            at = pl.multiple_of((shard * rp + part) * down_rows, down_rows)
            down_ref[pl.ds(at, down_rows), :] = ref[piece, :down_rows]
            at = pl.multiple_of(part * up_rows, up_rows)
            for j in range(blocks):
                lo = down_rows + j * up_rows
                up_ref[shard * blocks + j, pl.ds(at, up_rows), :] = ref[piece, lo : lo + up_rows]
    copy = pltpu.make_async_copy(down_ref, down_out, sem)
    copy.start()
    rows = jnp.concatenate([hidden_ref[s] for s in range(hidden_ref.shape[0])], axis=0)
    low = mm(rows, down_ref[...], 1, 0).astype(bf16)
    for s in range(low_ref.shape[0]):
        low_ref[s] = low[s * low_ref.shape[1] : (s + 1) * low_ref.shape[1]]
    copy.wait()


def pack_kernel(rp, part_ref, down_ref, up_ref, past_ref, out_ref):
    r = part_ref[0]
    down_rows, up_rows = down_ref.shape[0] // rp, RANK // rp
    out_ref[0, :down_rows] = down_ref[pl.ds(pl.multiple_of(r * down_rows, down_rows), down_rows)]
    at = pl.multiple_of(r * up_rows, up_rows)
    lo = down_rows
    for j in range(up_ref.shape[1] // HEAD_DIM):
        cols = slice(j * HEAD_DIM, (j + 1) * HEAD_DIM)
        out_ref[0, lo : lo + up_rows] = up_ref[pl.ds(at, up_rows), cols]
        lo += up_rows
    out_ref[0, lo:] = past_ref[...]


def pack_adapters(adapter_down, adapter_up, own_past):
    sp, rp, r = lax.axis_size("sp"), lax.axis_size("rep"), lax.axis_index("rep")
    down_rows, up_rows = adapter_down.shape[0] // rp, RANK // rp
    blocks = adapter_up.shape[1] // HEAD_DIM
    rows = down_rows + adapter_up.shape[1] // HEAD_DIM * up_rows
    packed_past = own_past.reshape(-1, 2 * RANK)
    vmem = pl.BlockSpec(memory_space=pltpu.VMEM)
    buf = pl.pallas_call(
        functools.partial(pack_kernel, rp),
        in_specs=[pl.BlockSpec(memory_space=pltpu.SMEM)] + [vmem] * 3,
        out_specs=vmem,
        out_shape=jax.ShapeDtypeStruct((1, rows + packed_past.shape[0], 2 * RANK), bf16),
        compiler_params=pltpu.CompilerParams(vmem_limit_bytes=8 * 1024 * 1024),
        cost_estimate=pl.CostEstimate(flops=0, bytes_accessed=2**19, transcendentals=0),
        name="pack",
    )(r.astype(jnp.int32).reshape(1), adapter_down, adapter_up, packed_past)
    step = 1
    while step < sp:
        buf = jnp.concatenate([buf, partner(buf, "sp", step)], axis=0)
        step *= 2
    seqs, each = own_past.shape[:2]
    past = buf[:, rows:].reshape(sp, seqs, each, -1).swapaxes(0, 1).reshape(seqs, sp * each, -1)
    return buf[:, :rows], past


def adapters_packed(hidden, buf, before_rep, before_swap, staged):
    sp, fs, rp = (lax.axis_size(a) for a in ("sp", "fsdp", "rep"))
    z, x, r = (lax.axis_index(a) for a in ("sp", "fsdp", "rep"))
    step = 1
    while step < fs:
        buf = jnp.concatenate([buf, partner(buf, "fsdp", step)], axis=0)
        step *= 2
    step = 2
    buf = tie(buf, before_rep)
    while step < rp:
        buf = jnp.concatenate([buf, partner(buf, "rep", step)], axis=0)
        step *= 2
    other = partner(tie(buf, before_swap), "rep", 1)
    index = jnp.stack([z, x, r]).astype(jnp.int32)
    vmem = pl.BlockSpec(memory_space=pltpu.VMEM)
    seqs, tokens = hidden.shape[:2]
    down_full, up_blocks, low = pl.pallas_call(
        functools.partial(low_rank_kernel, sp, fs, rp),
        in_specs=[pl.BlockSpec(memory_space=pltpu.SMEM)]
        + [vmem] * 3
        + [pl.BlockSpec(memory_space=pl.ANY)] * len(staged),
        out_specs=[pl.BlockSpec(memory_space=pltpu.HBM), vmem, vmem],
        scratch_shapes=[pltpu.VMEM((D, 2 * RANK), bf16), pltpu.SemaphoreType.DMA],
        out_shape=[
            jax.ShapeDtypeStruct((D, 2 * RANK), bf16),
            jax.ShapeDtypeStruct((HEADS + KV_HEADS, RANK, HEAD_DIM), bf16),
            jax.ShapeDtypeStruct((seqs, tokens, 2 * RANK), bf16),
        ],
        compiler_params=pltpu.CompilerParams(vmem_limit_bytes=12 * 1024 * 1024),
        cost_estimate=pl.CostEstimate(
            flops=2 * seqs * tokens * D * 2 * RANK, bytes_accessed=2**16, transcendentals=0
        ),
        name="low_rank",
    )(index, buf, other, hidden, *staged)
    return down_full, up_blocks, low


def adapters_plain(hidden, adapter_down, adapter_up):
    seqs, tokens = hidden.shape[:2]
    down_full = lax.all_gather(adapter_down, ("sp", "fsdp"), axis=0, tiled=True)
    up_full = lax.all_gather(adapter_up, ("sp", "fsdp"), axis=1, tiled=True)
    rows = hidden.reshape(seqs * tokens, D)
    low = jnp.dot(rows, down_full, preferred_element_type=f32).astype(bf16)
    up_blocks = up_full.reshape(RANK, HEADS + KV_HEADS, HEAD_DIM).swapaxes(0, 1)
    return down_full, up_blocks, low.reshape(seqs, tokens, 2 * RANK)


def grad_hidden_kernel(low_ref, down_ref, out_ref):
    out = mm(low_ref[...], down_ref[...], 1, 1).astype(bf16)
    tokens = out_ref.shape[1]
    for s in range(out_ref.shape[0]):
        out_ref[s] = out[s * tokens : (s + 1) * tokens]


def grad_hidden_of(low_grad, down_full, seqs, tokens):
    columns = 1024
    return pl.pallas_call(
        grad_hidden_kernel,
        grid=(D // columns,),
        in_specs=[
            pl.BlockSpec(low_grad.shape, lambda i: (0, 0)),
            pl.BlockSpec((columns, 2 * RANK), lambda i: (i, 0)),
        ],
        out_specs=pl.BlockSpec((seqs, tokens, columns), lambda i: (0, 0, i)),
        out_shape=jax.ShapeDtypeStruct((seqs, tokens, D), bf16),
        compiler_params=pltpu.CompilerParams(vmem_limit_bytes=12 * 1024 * 1024),
        cost_estimate=pl.CostEstimate(
            flops=16 * seqs * tokens * D * 2 * RANK, bytes_accessed=2**16, transcendentals=0
        ),
        name="grad_hidden",
    )(low_grad, down_full)


def adapter_grads_kernel(core_ref, hidden_ref, low_ref, guq_ref, guv_ref, send_ref, keep_ref, gd_ref):
    c = core_ref[0]
    shards, pairs = send_ref.shape[:2]
    down_rows = gd_ref.shape[1]
    columns = 2 * pairs * down_rows
    blocks = (HEADS + KV_HEADS) // shards
    up_rows = guq_ref.shape[2]
    low = low_ref[...]
    for b in range(shards):
        cols = [hidden_ref[s, :, b * columns : (b + 1) * columns] for s in range(hidden_ref.shape[0])]
        part = mm(jnp.concatenate(cols, axis=0), low, 0, 0).astype(bf16)
        for q in range(2 * pairs):
            gd_ref[q] = part[q * down_rows : (q + 1) * down_rows]
        for hi in range(pairs):
            for ref, q in ((send_ref, 2 * hi + 1 - c), (keep_ref, 2 * hi + c)):
                ref[b, hi, :down_rows] = gd_ref[q]
                for j in range(blocks):
                    block = b * blocks + j
                    src = guq_ref[block, q] if block < HEADS else guv_ref[block - HEADS, q]
                    lo = down_rows + j * up_rows
                    ref[b, hi, lo : lo + up_rows] = src


def packed_grads(hidden, low_grad, guq, guv, shards):
    rp, r = lax.axis_size("rep"), lax.axis_index("rep")
    c = lax.rem(r, 2)
    down_rows, up_rows = D // (shards * rp), RANK // rp
    up_width = (D + KV) // shards
    rows = down_rows + up_rows * up_width // (2 * RANK)
    if up_width % HEAD_DIM == 0:
        vmem = pl.BlockSpec(memory_space=pltpu.VMEM)
        packed = jax.ShapeDtypeStruct((shards, rp // 2, rows, 2 * RANK), bf16)
        return pl.pallas_call(
            adapter_grads_kernel,
            in_specs=[pl.BlockSpec(memory_space=pltpu.SMEM)] + [vmem] * 4,
            out_specs=[vmem] * 2,
            out_shape=[packed] * 2,
            scratch_shapes=[pltpu.VMEM((rp, down_rows, 2 * RANK), bf16)],
            compiler_params=pltpu.CompilerParams(vmem_limit_bytes=12 * 1024 * 1024),
            cost_estimate=pl.CostEstimate(
                flops=2 * hidden.size * 2 * RANK, bytes_accessed=5 * 2**20, transcendentals=0
            ),
            name="adapter_grads",
        )(c.astype(jnp.int32).reshape(1), hidden, low_grad, guq, guv)
    own_rows = hidden.reshape(-1, D)
    down = jnp.dot(own_rows.T, low_grad, preferred_element_type=f32).astype(bf16)
    down = down.reshape(shards, rp, down_rows, 2 * RANK)
    up = jnp.concatenate([guq, guv], axis=0).transpose(1, 2, 0, 3)
    up = up.reshape(rp, up_rows, shards, up_width).transpose(2, 0, 1, 3)
    up = up.reshape(shards, rp, -1, 2 * RANK)
    both = jnp.concatenate([down, up], axis=2).reshape(shards, rp // 2, 2, rows, 2 * RANK)
    send = lax.dynamic_index_in_dim(both, 1 - c, 2, keepdims=False)
    keep = lax.dynamic_index_in_dim(both, c, 2, keepdims=False)
    return send, keep


def finish_grads(send, keep, values, low_grad, hidden_of):
    sp, fs, rp = (lax.axis_size(a) for a in ("sp", "fsdp", "rep"))
    z, r = lax.axis_index("sp"), lax.axis_index("rep")
    shards, _, rows, lanes = send.shape
    part, hops = values[-1], []
    for k in range(sp - 1, 1, -1):
        if hops:
            part = (values[k].astype(f32) + hops[-1].astype(f32)).astype(bf16)
        hops.append(along(part, "sp", -1, k))
    got = partner(tie(send, *hops[:1]), "rep", 1)
    marks = []
    fs_bits, rep_bits = fs.bit_length() - 1, rp.bit_length() - 2
    labels = [("fsdp", b) for b in reversed(range(fs_bits))]
    labels += [("rep", b + 1) for b in reversed(range(rep_bits))]
    shape = (sp,) + (2,) * len(labels) + (rows, lanes)
    terms = [a.reshape(shape) for a in (keep, got)]

    def halve(terms, order):
        left = list(labels)
        for step, label in enumerate(order):
            axis, bit = label
            dim = 1 + left.index(label)
            left.remove(label)
            mine = lax.rem(lax.div(lax.axis_index(axis), 1 << bit), 2)

            def pick(i):
                parts = [lax.dynamic_index_in_dim(a, i, dim, keepdims=False) for a in terms]
                return sum(a.astype(f32) for a in parts).astype(bf16)

            send = pick(1 - mine)
            if step == 1:
                send = tie(send, *hops[1:])
            terms = [pick(mine), partner(send, axis, 1 << bit)]
            if step == 0:
                marks.append(terms[1])
        return sum(a.astype(f32) for a in terms).astype(bf16)

    cut = rows // 32 * 16
    first_rep, first_fsdp = labels[::-1], labels
    over_sp = halve([a[..., cut:, :] for a in terms], first_rep)
    if cut:
        other = halve([a[..., :cut, :] for a in terms], first_fsdp)
        over_sp = jnp.concatenate([other, over_sp], axis=1)
    part = values[1]
    if hops:
        part = (part.astype(f32) + tie(hops[-1], *marks).astype(f32)).astype(bf16)
    last = along(part, "sp", -1, 1)
    grad_value = (values[0].astype(f32) + last.astype(f32)).astype(bf16)
    over_sp = tie(over_sp, last)
    total = lax.dynamic_index_in_dim(over_sp, z, 0, keepdims=False).astype(f32)
    for k in range(1, sp):
        send = lax.dynamic_index_in_dim(over_sp, lax.rem(z + k, sp), 0, keepdims=False)
        total = total + cyclic(send, "sp", k).astype(f32)
    grad_hidden = hidden_of(tie(low_grad, over_sp))
    own = tie(total.astype(bf16), grad_hidden)
    parts = [own] + [partner(own, "rep", m) for m in range(1, rp)]
    ordered = []
    for q in range(rp):
        pick = parts[0]
        for m in range(1, rp):
            pick = jnp.where((r ^ m) == q, parts[m], pick)
        ordered.append(pick.astype(f32))
    down_rows, up_rows = D // (shards * rp), RANK // rp
    up_width = (D + KV) // shards
    grad_down = jnp.concatenate([p[:down_rows] for p in ordered], axis=0)
    ups = []
    for p in ordered:
        up = p[down_rows:]
        if up_width % HEAD_DIM == 0:
            up = [up[lo : lo + up_rows] for lo in range(0, up.shape[0], up_rows)]
            up = jnp.concatenate(up, axis=1)
        ups.append(up.reshape(up_rows, up_width))
    return grad_down, jnp.concatenate(ups, axis=0), grad_hidden, grad_value


def body(
    hidden,
    query_base,
    key_span,
    value_base,
    past_keys,
    past_values,
    grad_out,
    adapter_down,
    adapter_up,
):
    sp, fs = lax.axis_size("sp"), lax.axis_size("fsdp")
    z = lax.axis_index("sp")
    seqs, tokens = hidden.shape[:2]
    past_len = past_keys.shape[1] * sp
    own_past = jnp.concatenate([past_keys, past_values], axis=2)
    kvs = [jnp.concatenate([key_span, value_base], axis=2)]
    even = adapter_up.shape[1] % HEAD_DIM == 0
    if even:
        buf, past = pack_adapters(adapter_down, adapter_up, own_past)
    else:
        buf = own_past
        past = [own_past] + [cyclic(own_past, "sp", k) for k in range(1, sp)]
        past = jnp.concatenate(past, axis=1)
    kvs.append(along(tie(kvs[0], buf), "sp", 1))
    for k in range(2, sp):
        kvs.append(along(kvs[k - 1], "sp", 1, k - 1))
    if even:
        down_full, up_blocks, low_own = adapters_packed(
            hidden, buf, kvs[1], kvs[min(2, sp - 1)], (query_base, grad_out, *kvs[:3])
        )
    else:
        down_full, up_blocks, low_own = adapters_plain(hidden, adapter_down, adapter_up)
    lows = [low_own] + [along(low_own, "sp", k) for k in range(1, sp)]
    cos, sin = rotary_tables(tokens, past_len + z * tokens)
    place = z.astype(jnp.int32).reshape(1)

    made = attention(place, query_base, grad_out, up_blocks, past, cos, sin, lows, kvs)
    attended, grad_query, guq, guv, low_grad_q, low_grad_v = made[:6]
    values = made[6:]

    low_v_total = low_grad_v[:, :tokens]
    for k in range(1, sp):
        part = low_grad_v[:, k * tokens : (k + 1) * tokens].astype(bf16)
        low_v_total = low_v_total + along(part, "sp", -k).astype(f32)
    low_grad = (
        jnp.concatenate([low_grad_q, low_v_total], axis=2)
        .astype(bf16)
        .reshape(seqs * tokens, 2 * RANK)
    )
    send, keep = packed_grads(hidden, low_grad, guq, guv, sp * fs)
    grad_down, grad_up, grad_hidden, grad_value = finish_grads(
        send, keep, values, low_grad, lambda x: grad_hidden_of(x, down_full, seqs, tokens)
    )
    return (
        attended,
        grad_query,
        grad_value,
        grad_hidden,
        grad_down,
        grad_up,
    )


def solution(mesh):
    rows = P(("fsdp", "rep"), "sp", None)
    down, up = P(("sp", "fsdp"), None), P(None, ("sp", "fsdp"))
    return jax.shard_map(
        body,
        mesh=mesh,
        in_specs=(rows,) * 7 + (down, up),
        out_specs=(rows,) * 4 + (down, up),
        check_vma=False,
    )
```

```python
import functools
import math

import jax
import jax.numpy as jnp
from jax import lax
from jax.experimental import pallas as pl
from jax.experimental.pallas import tpu as pltpu
from jax.sharding import PartitionSpec as P

D = 4096
HEADS = 32
KV_HEADS = 8
HEAD_DIM = 128
RANK = 64
KV = 1024
GROUP = HEADS // KV_HEADS
WIDE = GROUP * HEAD_DIM
ROPE_BASE = 500000.0
HIDDEN_MASK = -1e30
LOG2_E = 1.4426950408889634

f32 = jnp.float32
bf16 = jnp.bfloat16


def rotary_tables(row_count, offset):
    half = HEAD_DIM // 2
    position = (jnp.arange(row_count, dtype=jnp.int32) + offset).astype(f32)
    inverse = jnp.exp(jnp.arange(half, dtype=f32) * (-2.0 * math.log(ROPE_BASE) / HEAD_DIM))
    angle = position[:, None] * inverse[None, :]
    cosine, sine = jnp.cos(angle), jnp.sin(angle)
    return (
        jnp.concatenate([cosine, cosine], axis=1),
        jnp.concatenate([-sine, sine], axis=1),
    )


def cyclic(x, axis, shift):
    n = lax.axis_size(axis)
    return lax.ppermute(x, axis, [(i, (i + shift) % n) for i in range(n)])


def along(x, axis, shift, start=0):
    n = lax.axis_size(axis)
    return lax.ppermute(x, axis, [(i, i + shift) for i in range(start, n) if 0 <= i + shift < n])


def partner(x, axis, mask):
    n = lax.axis_size(axis)
    return lax.ppermute(x, axis, [(i, i ^ mask) for i in range(n)])


def tie(x, *others):
    return lax.optimization_barrier((x,) + others)[0]


def mm(a, b, ca, cb):
    return lax.dot_general(a, b, (((ca,), (cb,)), ((), ())), preferred_element_type=f32)


def attention_kernel(shards, place_ref, *refs):
    it = iter(refs)

    def take(n):
        return [next(it) for _ in range(n)]

    q_hbm, g_hbm, upq_ref, upv_ref, pk_ref, pv_ref, cos_ref, sin_ref = take(8)
    low_refs, k_refs, v_refs = take(shards), take(shards), take(shards)
    att_ref, gq_ref, guq_ref, guv_ref, lgq_ref, lgv_ref = take(6)
    gv_refs = take(shards)
    q_buf, g_buf, sems = take(3)

    group, slot = pl.program_id(0), lax.rem(pl.program_id(0), 2)

    def fetches(step, into):
        at = pl.multiple_of(step * WIDE, WIDE)
        return [
            pltpu.make_async_copy(hbm.at[:, :, pl.ds(at, WIDE)], buf.at[into], sems.at[i, into])
            for i, (hbm, buf) in enumerate(((q_hbm, q_buf), (g_hbm, g_buf)))
        ]

    @pl.when(group == 0)
    def _():
        for copy in fetches(0, 0):
            copy.start()

    @pl.when(group + 1 < pl.num_programs(0))
    def _():
        for copy in fetches(group + 1, 1 - slot):
            copy.start()

    seqs, tokens = q_buf.shape[1:3]
    parts, part_rows = guq_ref.shape[1:3]
    span = shards * tokens
    past = pk_ref.shape[1]
    scale = 1.0 / math.sqrt(HEAD_DIM)
    place = place_ref[0]
    cos, sin = cos_ref[...], sin_ref[...]
    upq = jnp.concatenate([upq_ref[h] for h in range(GROUP)], axis=1)
    upv = upv_ref[0]

    @pl.when(pl.program_id(0) == 0)
    def _():
        lgq_ref[...] = jnp.zeros_like(lgq_ref)
        lgv_ref[...] = jnp.zeros_like(lgv_ref)

    col = lax.broadcasted_iota(jnp.int32, (tokens, span + past), 1)
    row = lax.broadcasted_iota(jnp.int32, (tokens, span + past), 0)
    seen = (col <= row) | ((col >= tokens) & (col < (place + 1) * tokens)) | (col >= span)
    bias = jnp.where(seen, 0.0, HIDDEN_MASK)
    bias = jnp.concatenate([bias] * GROUP, axis=0)

    def heads(x):
        return jnp.concatenate(
            [x[:, h * HEAD_DIM : (h + 1) * HEAD_DIM] for h in range(GROUP)], axis=0
        )

    def lanes(x):
        return jnp.concatenate([x[h * tokens : (h + 1) * tokens] for h in range(GROUP)], axis=1)

    cos4 = jnp.concatenate([cos] * GROUP, axis=0)
    sin4 = jnp.concatenate([sin] * GROUP, axis=0)
    every = range(seqs)
    low_q = jnp.concatenate([low_refs[0][s][:, :RANK] for s in every], axis=0)
    low_v = jnp.concatenate([r[s][:, RANK:] for s in every for r in low_refs], axis=0)
    query_delta = mm(low_q, upq, 1, 0)
    value_delta = mm(low_v, upv, 1, 0)
    for copy in fetches(group, slot):
        copy.wait()
    backs, gvs = [], []
    for s in every:
        delta = heads(query_delta[s * tokens : (s + 1) * tokens])
        delta = delta * cos4 + pltpu.roll(delta, HEAD_DIM // 2, 1) * sin4
        q = (heads(q_buf[slot, s]).astype(f32) + delta).astype(bf16)
        g = heads(g_buf[slot, s])
        keys = jnp.concatenate([r[s] for r in k_refs] + [pk_ref[s]], axis=0)
        base = jnp.concatenate([r[s] for r in v_refs], axis=0).astype(f32)
        vals = (base + value_delta[s * span : (s + 1) * span]).astype(bf16)
        vals = jnp.concatenate([vals, pv_ref[s]], axis=0)

        scores = mm(q, keys, 1, 1) * (scale * LOG2_E) + bias
        top = jnp.max(scores, axis=-1, keepdims=True)
        e = jnp.exp2(scores - top)
        inverse = 1.0 / jnp.sum(e, axis=-1, keepdims=True)
        weights = e.astype(bf16)
        out = (mm(weights, vals, 1, 0) * inverse).astype(bf16)
        att_ref[s] = lanes(out)
        g = (g.astype(f32) * inverse).astype(bf16)
        prob_grad = mm(g, vals, 1, 1)
        row_delta = jnp.sum(g.astype(f32) * out.astype(f32), axis=-1, keepdims=True)
        score_grad = (e * (prob_grad - row_delta)).astype(bf16)
        gq = (mm(score_grad, keys, 1, 0) * scale).astype(bf16)
        gq_ref[s] = lanes(gq)
        gq32 = gq.astype(f32)
        back = (gq32 * cos4 - pltpu.roll(gq32, HEAD_DIM // 2, 1) * sin4).astype(bf16)
        backs.append(lanes(back))
        gv = mm(weights[:, :span], g, 0, 0).astype(bf16)
        gvs.append(gv)
        for k in range(shards):
            gv_refs[k][s] = gv[k * tokens : (k + 1) * tokens]
    back = jnp.concatenate(backs, axis=0)
    gv = jnp.concatenate(gvs, axis=0)
    low_grad_q = mm(back, upq, 1, 1)
    low_grad_v = mm(gv, upv, 1, 1)
    for s in every:
        lgq_ref[s] += low_grad_q[s * tokens : (s + 1) * tokens]
        lgv_ref[s] += low_grad_v[s * span : (s + 1) * span]
    grad_up_q = mm(low_q, back, 0, 0)
    grad_up_v = mm(low_v, gv, 0, 0)
    grad_up_q, grad_up_v = grad_up_q.astype(bf16), grad_up_v.astype(bf16)
    for p in range(parts):
        rows = slice(p * part_rows, (p + 1) * part_rows)
        for h in range(GROUP):
            guq_ref[h, p] = grad_up_q[rows, h * HEAD_DIM : (h + 1) * HEAD_DIM]
        guv_ref[0, p] = grad_up_v[rows]


def attention(place, query_base, grad_out, up_blocks, past, cos, sin, lows, kvs):
    shards = len(kvs)
    parts = lax.axis_size("rep")
    seqs, tokens = query_base.shape[:2]
    past_len = past.shape[1]

    def whole(x):
        return pl.BlockSpec(x.shape, lambda g: (0,) * len(x.shape))

    spec = pl.BlockSpec
    q_spec = spec((seqs, tokens, WIDE), lambda g: (0, 0, g))
    gv_spec = spec((seqs, tokens, HEAD_DIM), lambda g: (0, 0, g))
    past_block = (seqs, past_len, HEAD_DIM)
    in_specs = [
        spec(memory_space=pltpu.SMEM),
        spec(memory_space=pltpu.HBM),
        spec(memory_space=pltpu.HBM),
        spec((GROUP, RANK, HEAD_DIM), lambda g: (g, 0, 0)),
        spec((1, RANK, HEAD_DIM), lambda g: (HEADS + g, 0, 0)),
        spec(past_block, lambda g: (0, 0, g)),
        spec(past_block, lambda g: (0, 0, KV_HEADS + g)),
        whole(cos),
        whole(sin),
    ]
    in_specs += [whole(x) for x in lows]
    in_specs += [gv_spec] * shards
    in_specs += [spec((seqs, tokens, HEAD_DIM), lambda g: (0, 0, KV_HEADS + g))] * shards
    shape = jax.ShapeDtypeStruct
    low_q_shape = shape((seqs, tokens, RANK), f32)
    low_v_shape = shape((seqs, shards * tokens, RANK), f32)
    part_rows = RANK // parts
    scores = GROUP * tokens * (shards * tokens + past_len)
    pairs = seqs * KV_HEADS * scores
    return pl.pallas_call(
        functools.partial(attention_kernel, shards),
        grid=(KV_HEADS,),
        in_specs=in_specs,
        out_specs=[
            q_spec,
            q_spec,
            spec((GROUP, parts, part_rows, HEAD_DIM), lambda g: (g, 0, 0, 0)),
            spec((1, parts, part_rows, HEAD_DIM), lambda g: (g, 0, 0, 0)),
            whole(low_q_shape),
            whole(low_v_shape),
        ]
        + [gv_spec] * shards,
        out_shape=[
            shape(query_base.shape, bf16),
            shape(query_base.shape, bf16),
            shape((HEADS, parts, part_rows, HEAD_DIM), bf16),
            shape((KV_HEADS, parts, part_rows, HEAD_DIM), bf16),
            low_q_shape,
            low_v_shape,
        ]
        + [shape((seqs, tokens, KV), bf16)] * shards,
        scratch_shapes=[
            pltpu.VMEM((2, seqs, tokens, WIDE), bf16),
            pltpu.VMEM((2, seqs, tokens, WIDE), bf16),
            pltpu.SemaphoreType.DMA((2, 2)),
        ],
        compiler_params=pltpu.CompilerParams(
            vmem_limit_bytes=min(8 * 2**20 + 96 * scores, 48 * 2**20)
        ),
        cost_estimate=pl.CostEstimate(
            flops=pairs * HEAD_DIM * 120, bytes_accessed=2**16, transcendentals=pairs
        ),
        name="attention",
    )(place, query_base, grad_out, up_blocks, up_blocks, past, past, cos, sin, *lows, *kvs, *kvs)


def low_rank_kernel(
    sp, fs, rp, index_ref, own_ref, other_ref, hidden_ref, *refs
):
    down_out, up_ref, low_ref, down_ref, sem = refs[-5:]
    z, x, r = index_ref[0], index_ref[1], index_ref[2]
    shards = sp * fs
    down_rows, up_rows = D // (shards * rp), RANK // rp
    blocks = (HEADS + KV_HEADS) // shards
    for piece in range(own_ref.shape[0]):
        shard = (z ^ (piece % sp)) * fs + (x ^ (piece // sp % fs))
        for swap, ref in enumerate((own_ref, other_ref)):
            part = r ^ (piece // shards * 2 + swap)
            at = pl.multiple_of((shard * rp + part) * down_rows, down_rows)
            down_ref[pl.ds(at, down_rows), :] = ref[piece, :down_rows]
            at = pl.multiple_of(part * up_rows, up_rows)
            for j in range(blocks):
                lo = down_rows + j * up_rows
                up_ref[shard * blocks + j, pl.ds(at, up_rows), :] = ref[piece, lo : lo + up_rows]
    copy = pltpu.make_async_copy(down_ref, down_out, sem)
    copy.start()
    rows = jnp.concatenate([hidden_ref[s] for s in range(hidden_ref.shape[0])], axis=0)
    low = mm(rows, down_ref[...], 1, 0).astype(bf16)
    for s in range(low_ref.shape[0]):
        low_ref[s] = low[s * low_ref.shape[1] : (s + 1) * low_ref.shape[1]]
    copy.wait()


def pack_kernel(rp, part_ref, down_ref, up_ref, past_ref, out_ref):
    r = part_ref[0]
    down_rows, up_rows = down_ref.shape[0] // rp, RANK // rp
    out_ref[0, :down_rows] = down_ref[pl.ds(pl.multiple_of(r * down_rows, down_rows), down_rows)]
    at = pl.multiple_of(r * up_rows, up_rows)
    lo = down_rows
    for j in range(up_ref.shape[1] // HEAD_DIM):
        cols = slice(j * HEAD_DIM, (j + 1) * HEAD_DIM)
        out_ref[0, lo : lo + up_rows] = up_ref[pl.ds(at, up_rows), cols]
        lo += up_rows
    out_ref[0, lo:] = past_ref[...]


def pack_adapters(adapter_down, adapter_up, own_past):
    sp, rp, r = lax.axis_size("sp"), lax.axis_size("rep"), lax.axis_index("rep")
    down_rows, up_rows = adapter_down.shape[0] // rp, RANK // rp
    blocks = adapter_up.shape[1] // HEAD_DIM
    rows = down_rows + adapter_up.shape[1] // HEAD_DIM * up_rows
    packed_past = own_past.reshape(-1, 2 * RANK)
    vmem = pl.BlockSpec(memory_space=pltpu.VMEM)
    buf = pl.pallas_call(
        functools.partial(pack_kernel, rp),
        in_specs=[pl.BlockSpec(memory_space=pltpu.SMEM)] + [vmem] * 3,
        out_specs=vmem,
        out_shape=jax.ShapeDtypeStruct((1, rows + packed_past.shape[0], 2 * RANK), bf16),
        compiler_params=pltpu.CompilerParams(vmem_limit_bytes=8 * 1024 * 1024),
        cost_estimate=pl.CostEstimate(flops=0, bytes_accessed=2**19, transcendentals=0),
        name="pack",
    )(r.astype(jnp.int32).reshape(1), adapter_down, adapter_up, packed_past)
    step = 1
    while step < sp:
        buf = jnp.concatenate([buf, partner(buf, "sp", step)], axis=0)
        step *= 2
    seqs, each = own_past.shape[:2]
    past = buf[:, rows:].reshape(sp, seqs, each, -1).swapaxes(0, 1).reshape(seqs, sp * each, -1)
    return buf[:, :rows], past


def adapters_packed(hidden, buf, before_rep, before_swap):
    sp, fs, rp = (lax.axis_size(a) for a in ("sp", "fsdp", "rep"))
    z, x, r = (lax.axis_index(a) for a in ("sp", "fsdp", "rep"))
    step = 1
    while step < fs:
        buf = jnp.concatenate([buf, partner(buf, "fsdp", step)], axis=0)
        step *= 2
    step = 2
    buf = tie(buf, before_rep)
    while step < rp:
        buf = jnp.concatenate([buf, partner(buf, "rep", step)], axis=0)
        step *= 2
    other = partner(tie(buf, before_swap), "rep", 1)
    index = jnp.stack([z, x, r]).astype(jnp.int32)
    vmem = pl.BlockSpec(memory_space=pltpu.VMEM)
    seqs, tokens = hidden.shape[:2]
    down_full, up_blocks, low = pl.pallas_call(
        functools.partial(low_rank_kernel, sp, fs, rp),
        in_specs=[pl.BlockSpec(memory_space=pltpu.SMEM)] + [vmem] * 3,
        out_specs=[pl.BlockSpec(memory_space=pltpu.HBM), vmem, vmem],
        scratch_shapes=[pltpu.VMEM((D, 2 * RANK), bf16), pltpu.SemaphoreType.DMA],
        out_shape=[
            jax.ShapeDtypeStruct((D, 2 * RANK), bf16),
            jax.ShapeDtypeStruct((HEADS + KV_HEADS, RANK, HEAD_DIM), bf16),
            jax.ShapeDtypeStruct((seqs, tokens, 2 * RANK), bf16),
        ],
        compiler_params=pltpu.CompilerParams(vmem_limit_bytes=12 * 1024 * 1024),
        cost_estimate=pl.CostEstimate(
            flops=2 * seqs * tokens * D * 2 * RANK, bytes_accessed=2**16, transcendentals=0
        ),
        name="low_rank",
    )(index, buf, other, hidden)
    return down_full, up_blocks, low


def adapters_plain(hidden, adapter_down, adapter_up):
    seqs, tokens = hidden.shape[:2]
    down_full = lax.all_gather(adapter_down, ("sp", "fsdp"), axis=0, tiled=True)
    up_full = lax.all_gather(adapter_up, ("sp", "fsdp"), axis=1, tiled=True)
    rows = hidden.reshape(seqs * tokens, D)
    low = jnp.dot(rows, down_full, preferred_element_type=f32).astype(bf16)
    up_blocks = up_full.reshape(RANK, HEADS + KV_HEADS, HEAD_DIM).swapaxes(0, 1)
    return down_full, up_blocks, low.reshape(seqs, tokens, 2 * RANK)


def grad_hidden_kernel(low_ref, down_ref, out_ref):
    out = mm(low_ref[...], down_ref[...], 1, 1).astype(bf16)
    tokens = out_ref.shape[1]
    for s in range(out_ref.shape[0]):
        out_ref[s] = out[s * tokens : (s + 1) * tokens]


def grad_hidden_of(low_grad, down_full, seqs, tokens):
    columns = 1024
    return pl.pallas_call(
        grad_hidden_kernel,
        grid=(D // columns,),
        in_specs=[
            pl.BlockSpec(low_grad.shape, lambda i: (0, 0)),
            pl.BlockSpec((columns, 2 * RANK), lambda i: (i, 0)),
        ],
        out_specs=pl.BlockSpec((seqs, tokens, columns), lambda i: (0, 0, i)),
        out_shape=jax.ShapeDtypeStruct((seqs, tokens, D), bf16),
        compiler_params=pltpu.CompilerParams(vmem_limit_bytes=12 * 1024 * 1024),
        cost_estimate=pl.CostEstimate(
            flops=16 * seqs * tokens * D * 2 * RANK, bytes_accessed=2**16, transcendentals=0
        ),
        name="grad_hidden",
    )(low_grad, down_full)


def adapter_grads_kernel(core_ref, hidden_ref, low_ref, guq_ref, guv_ref, send_ref, keep_ref, gd_ref):
    c = core_ref[0]
    shards, pairs = send_ref.shape[:2]
    down_rows = gd_ref.shape[1]
    columns = 2 * pairs * down_rows
    blocks = (HEADS + KV_HEADS) // shards
    up_rows = guq_ref.shape[2]
    low = low_ref[...]
    for b in range(shards):
        cols = [hidden_ref[s, :, b * columns : (b + 1) * columns] for s in range(hidden_ref.shape[0])]
        part = mm(jnp.concatenate(cols, axis=0), low, 0, 0).astype(bf16)
        for q in range(2 * pairs):
            gd_ref[q] = part[q * down_rows : (q + 1) * down_rows]
        for hi in range(pairs):
            for ref, q in ((send_ref, 2 * hi + 1 - c), (keep_ref, 2 * hi + c)):
                ref[b, hi, :down_rows] = gd_ref[q]
                for j in range(blocks):
                    block = b * blocks + j
                    src = guq_ref[block, q] if block < HEADS else guv_ref[block - HEADS, q]
                    lo = down_rows + j * up_rows
                    ref[b, hi, lo : lo + up_rows] = src


def packed_grads(hidden, low_grad, guq, guv, shards):
    rp, r = lax.axis_size("rep"), lax.axis_index("rep")
    c = lax.rem(r, 2)
    down_rows, up_rows = D // (shards * rp), RANK // rp
    up_width = (D + KV) // shards
    rows = down_rows + up_rows * up_width // (2 * RANK)
    if up_width % HEAD_DIM == 0:
        vmem = pl.BlockSpec(memory_space=pltpu.VMEM)
        packed = jax.ShapeDtypeStruct((shards, rp // 2, rows, 2 * RANK), bf16)
        return pl.pallas_call(
            adapter_grads_kernel,
            in_specs=[pl.BlockSpec(memory_space=pltpu.SMEM)] + [vmem] * 4,
            out_specs=[vmem] * 2,
            out_shape=[packed] * 2,
            scratch_shapes=[pltpu.VMEM((rp, down_rows, 2 * RANK), bf16)],
            compiler_params=pltpu.CompilerParams(vmem_limit_bytes=12 * 1024 * 1024),
            cost_estimate=pl.CostEstimate(
                flops=2 * hidden.size * 2 * RANK, bytes_accessed=5 * 2**20, transcendentals=0
            ),
            name="adapter_grads",
        )(c.astype(jnp.int32).reshape(1), hidden, low_grad, guq, guv)
    own_rows = hidden.reshape(-1, D)
    down = jnp.dot(own_rows.T, low_grad, preferred_element_type=f32).astype(bf16)
    down = down.reshape(shards, rp, down_rows, 2 * RANK)
    up = jnp.concatenate([guq, guv], axis=0).transpose(1, 2, 0, 3)
    up = up.reshape(rp, up_rows, shards, up_width).transpose(2, 0, 1, 3)
    up = up.reshape(shards, rp, -1, 2 * RANK)
    both = jnp.concatenate([down, up], axis=2).reshape(shards, rp // 2, 2, rows, 2 * RANK)
    send = lax.dynamic_index_in_dim(both, 1 - c, 2, keepdims=False)
    keep = lax.dynamic_index_in_dim(both, c, 2, keepdims=False)
    return send, keep


def finish_grads(send, keep, values, low_grad, hidden_of):
    sp, fs, rp = (lax.axis_size(a) for a in ("sp", "fsdp", "rep"))
    z, r = lax.axis_index("sp"), lax.axis_index("rep")
    shards, _, rows, lanes = send.shape
    part, hops = values[-1], []
    for k in range(sp - 1, 1, -1):
        if hops:
            part = (values[k].astype(f32) + hops[-1].astype(f32)).astype(bf16)
        hops.append(along(part, "sp", -1, k))
    got = partner(tie(send, *hops[:1]), "rep", 1)
    marks = []
    fs_bits, rep_bits = fs.bit_length() - 1, rp.bit_length() - 2
    labels = [("fsdp", b) for b in reversed(range(fs_bits))]
    labels += [("rep", b + 1) for b in reversed(range(rep_bits))]
    shape = (sp,) + (2,) * len(labels) + (rows, lanes)
    terms = [a.reshape(shape) for a in (keep, got)]

    def halve(terms, order):
        left = list(labels)
        for step, label in enumerate(order):
            axis, bit = label
            dim = 1 + left.index(label)
            left.remove(label)
            mine = lax.rem(lax.div(lax.axis_index(axis), 1 << bit), 2)

            def pick(i):
                parts = [lax.dynamic_index_in_dim(a, i, dim, keepdims=False) for a in terms]
                return sum(a.astype(f32) for a in parts).astype(bf16)

            send = pick(1 - mine)
            if step == 1:
                send = tie(send, *hops[1:])
            terms = [pick(mine), partner(send, axis, 1 << bit)]
            if step == 0:
                marks.append(terms[1])
        return sum(a.astype(f32) for a in terms).astype(bf16)

    cut = rows // 32 * 16
    first_rep, first_fsdp = labels[::-1], labels
    over_sp = halve([a[..., cut:, :] for a in terms], first_rep)
    if cut:
        other = halve([a[..., :cut, :] for a in terms], first_fsdp)
        over_sp = jnp.concatenate([other, over_sp], axis=1)
    part = values[1]
    if hops:
        part = (part.astype(f32) + tie(hops[-1], *marks).astype(f32)).astype(bf16)
    last = along(part, "sp", -1, 1)
    grad_value = (values[0].astype(f32) + last.astype(f32)).astype(bf16)
    total = lax.dynamic_index_in_dim(over_sp, z, 0, keepdims=False).astype(f32)
    for k in range(1, sp):
        send = lax.dynamic_index_in_dim(over_sp, lax.rem(z + k, sp), 0, keepdims=False)
        total = total + cyclic(send, "sp", k).astype(f32)
    grad_hidden = hidden_of(tie(low_grad, over_sp))
    own = tie(total.astype(bf16), grad_hidden, last)
    parts = [own] + [partner(own, "rep", m) for m in range(1, rp)]
    ordered = []
    for q in range(rp):
        pick = parts[0]
        for m in range(1, rp):
            pick = jnp.where((r ^ m) == q, parts[m], pick)
        ordered.append(pick.astype(f32))
    down_rows, up_rows = D // (shards * rp), RANK // rp
    up_width = (D + KV) // shards
    grad_down = jnp.concatenate([p[:down_rows] for p in ordered], axis=0)
    ups = []
    for p in ordered:
        up = p[down_rows:]
        if up_width % HEAD_DIM == 0:
            up = [up[lo : lo + up_rows] for lo in range(0, up.shape[0], up_rows)]
            up = jnp.concatenate(up, axis=1)
        ups.append(up.reshape(up_rows, up_width))
    return grad_down, jnp.concatenate(ups, axis=0), grad_hidden, grad_value


def body(
    hidden,
    query_base,
    key_span,
    value_base,
    past_keys,
    past_values,
    grad_out,
    adapter_down,
    adapter_up,
):
    sp, fs = lax.axis_size("sp"), lax.axis_size("fsdp")
    z = lax.axis_index("sp")
    seqs, tokens = hidden.shape[:2]
    past_len = past_keys.shape[1] * sp
    own_past = jnp.concatenate([past_keys, past_values], axis=2)
    kvs = [jnp.concatenate([key_span, value_base], axis=2)]
    even = adapter_up.shape[1] % HEAD_DIM == 0
    if even:
        buf, past = pack_adapters(adapter_down, adapter_up, own_past)
    else:
        buf = own_past
        past = [own_past] + [cyclic(own_past, "sp", k) for k in range(1, sp)]
        past = jnp.concatenate(past, axis=1)
    kvs.append(along(tie(kvs[0], buf), "sp", 1))
    for k in range(2, sp):
        kvs.append(along(kvs[k - 1], "sp", 1, k - 1))
    if even:
        down_full, up_blocks, low_own = adapters_packed(hidden, buf, kvs[1], kvs[min(2, sp - 1)])
    else:
        down_full, up_blocks, low_own = adapters_plain(hidden, adapter_down, adapter_up)
    lows = [low_own] + [along(low_own, "sp", k) for k in range(1, sp)]
    cos, sin = rotary_tables(tokens, past_len + z * tokens)
    place = z.astype(jnp.int32).reshape(1)

    made = attention(place, query_base, grad_out, up_blocks, past, cos, sin, lows, kvs)
    attended, grad_query, guq, guv, low_grad_q, low_grad_v = made[:6]
    values = made[6:]

    low_v_total = low_grad_v[:, :tokens]
    for k in range(1, sp):
        part = low_grad_v[:, k * tokens : (k + 1) * tokens].astype(bf16)
        low_v_total = low_v_total + along(part, "sp", -k).astype(f32)
    low_grad = (
        jnp.concatenate([low_grad_q, low_v_total], axis=2)
        .astype(bf16)
        .reshape(seqs * tokens, 2 * RANK)
    )
    send, keep = packed_grads(hidden, low_grad, guq, guv, sp * fs)
    grad_down, grad_up, grad_hidden, grad_value = finish_grads(
        send, keep, values, low_grad, lambda x: grad_hidden_of(x, down_full, seqs, tokens)
    )
    return (
        attended,
        grad_query,
        grad_value,
        grad_hidden,
        grad_down,
        grad_up,
    )


def solution(mesh):
    rows = P(("fsdp", "rep"), "sp", None)
    down, up = P(("sp", "fsdp"), None), P(None, ("sp", "fsdp"))
    return jax.shard_map(
        body,
        mesh=mesh,
        in_specs=(rows,) * 7 + (down, up),
        out_specs=(rows,) * 4 + (down, up),
        check_vma=False,
    )
```
